32 devices in a mesh: dp: 8 (over z, y), mp: 4 (over x, core).
Axes of the slice: x: 2, y: 2, z: 4, core: 2. Of those that a mesh axis runs over, the one named last changes fastest.
Arguments:
- tokens: bfloat16 [16, 1024, 768], P('dp'), may hold values from -6 to 6
- cotangent: bfloat16 [16, 1024, 768], P('dp'), may hold values from -6 to 6
- doc_lengths: int32 [16, 4], P('dp'), may hold values from 1 to 512, 1024 in all within a row
- time_steps: int32 [16], P('dp'), may hold values from 0 to 999
- qkv_master: float32 [768, 3, 768], P('dp', None, 'mp'), may hold values from -0.21875 to 0.21875
- qkv_first: float32 [768, 3, 768], P('dp', None, 'mp'), may hold values from -40 to 40
- qkv_second: float32 [768, 3, 768], P('dp', None, 'mp'), may hold values from 4.096 to 16.384
- proj_master: float32 [768, 768], P('mp', 'dp'), may hold values from -0.875 to 0.875
- proj_first: float32 [768, 768], P('mp', 'dp'), may hold values from -20 to 20
- proj_second: float32 [768, 768], P('mp', 'dp'), may hold values from 0.98304 to 4.096
- up_master: float32 [768, 3072], P('dp', 'mp'), may hold values from -0.21875 to 0.21875
- up_first: float32 [768, 3072], P('dp', 'mp'), may hold values from -40 to 40
- up_second: float32 [768, 3072], P('dp', 'mp'), may hold values from 3.2768 to 13.1072
- down_master: float32 [3072, 768], P('mp', 'dp'), may hold values from -0.109375 to 0.109375
- down_first: float32 [3072, 768], P('mp', 'dp'), may hold values from -64 to 64
- down_second: float32 [3072, 768], P('mp', 'dp'), may hold values from 10.48576 to 42.5984
- ada_master: float32 [128, 4608], P('dp'), may hold values from -0.25 to 0.25
- ada_first: float32 [128, 4608], P('dp'), may hold values from -64 to 64
- ada_second: float32 [128, 4608], P('dp'), may hold values from 8.192 to 32.768
- vec_master: float32 [13, 768], replicated, may hold values from -2 to 3
- vec_first: float32 [13, 768], replicated, may hold values from -80 to 80
- vec_second: float32 [13, 768], replicated, may hold values from 16.384 to 65.536
Outputs:
- block_out: bfloat16 [16, 1024, 768], P('dp')
- grad_tokens: float32 [16, 1024, 768], P('dp')
- qkv_new: float32 [768, 3, 768], P('dp', None, 'mp')
- qkv_first_new: float32 [768, 3, 768], P('dp', None, 'mp')
- qkv_second_new: float32 [768, 3, 768], P('dp', None, 'mp')
- proj_new: float32 [768, 768], P('mp', 'dp')
- proj_first_new: float32 [768, 768], P('mp', 'dp')
- proj_second_new: float32 [768, 768], P('mp', 'dp')
- up_new: float32 [768, 3072], P('dp', 'mp')
- up_first_new: float32 [768, 3072], P('dp', 'mp')
- up_second_new: float32 [768, 3072], P('dp', 'mp')
- down_new: float32 [3072, 768], P('mp', 'dp')
- down_first_new: float32 [3072, 768], P('mp', 'dp')
- down_second_new: float32 [3072, 768], P('mp', 'dp')
- ada_new: float32 [128, 4608], P('dp')
- ada_first_new: float32 [128, 4608], P('dp')
- ada_second_new: float32 [128, 4608], P('dp')
- vec_new: float32 [13, 768], replicated
- vec_first_new: float32 [13, 768], replicated
- vec_second_new: float32 [13, 768], replicated
The draws below stay inside these ranges and needn't reach their ends.
Inputs may be any that keep to these rules, and one draw needn't show every extreme that they name: `doc_lengths`: in every sequence the 4 document lengths sum to 1024.
All inputs are finite; a program needn't handle non-finite values.
Results may differ from the reference program's by a relative error of at most 0.018.
Values may be sent and summed in bfloat16 or wider, within the bound.
A program may use at most 192 MiB of HBM per device.

```python
import math
import jax
import jax.numpy as jnp
import numpy as np
from jax import lax

D = 768
HEADS = 12
HEAD = 64
FF = 3072
COND = 128
LEN = 1024
DOCS = 4
STEP = 10
SEQS = 16
TOKENS = 16384
VROWS = 13
N_MP = 4


def draw_vec_master(key, part):
    key = jax.random.fold_in(key, 7)
    row_count = 9 + FF // D
    noise_raw = jnp.clip(jax.random.normal(key, (row_count, D), jnp.float32), -4.0, 4.0)
    centre = jnp.array([1.0, 1.0, 0.0, 0.0, 0.0, 1.0, 0.0, 0.0, 1.0] + [0.0] * (FF // D), jnp.float32)
    spread = jnp.array([0.3] * 9 + [0.5] * (FF // D), jnp.float32)
    return centre[:, None] + spread[:, None] * noise_raw


def touch_ends(values, stream_key, smallest, high):
    longest = values.shape.index(max(values.shape))
    spots = []
    for shift in (0, 1):
        where = [jax.random.randint(jax.random.fold_in(stream_key, axis), (), 0, length) for axis, length in enumerate(values.shape)]
        where[longest] = (where[longest] + shift) % values.shape[longest]
        spots.append(tuple(where))
    return values.at[spots[0]].set(smallest).at[spots[1]].set(high)


def steps_of(key, dims, pieces, smallest, largest):
    gain = 1.0
    for position, blocks in pieces:
        draws = jax.random.uniform(jax.random.fold_in(jax.random.fold_in(key, 6), position), (blocks,), jnp.float32, smallest / len(pieces), largest / len(pieces))
        gain = gain * jnp.repeat(jnp.exp(draws), dims[position] // blocks).reshape((-1,) + (1,) * (len(dims) - 1 - position))
    return gain


def length_profile(count, total, limit, lean):
    weights = [(1 << 20) // math.isqrt(standing ** lean) + 1 for standing in range(2, count + 1)]
    spare, given = total - limit - (count - 1), [1] * (count - 1)
    while spare > 0:
        free = [i for i in range(count - 1) if given[i] < limit]
        whole, remaining = sum([weights[i] for i in free]), spare
        for i in free:
            extra = min(limit - given[i], max(1, remaining * weights[i] // whole), spare)
            given[i] = given[i] + extra
            spare = spare - extra
    return np.array([limit] + given)


def ragged_sizes(rng, count, total, limit, slope):
    if count == 2:
        one = jax.random.randint(rng, (), max(1, total - limit), min(limit, total - 1) + 1)
        return jnp.stack([one, total - one])
    lengths = jnp.asarray(length_profile(count, total, limit, slope), jnp.int32)
    pairs = (count - 1) // 2
    donor, receiver = lengths[1:1 + 2 * pairs:2], lengths[2:2 + 2 * pairs:2]
    room = jnp.minimum(donor - 1, limit - receiver)
    shifted = jax.random.randint(jax.random.fold_in(rng, 1), (pairs,), 0, 1 << 20) % (room + 1)
    lengths = lengths.at[1:1 + 2 * pairs:2].set(donor - shifted).at[2:2 + 2 * pairs:2].set(receiver + shifted)
    return lengths[jax.random.permutation(jax.random.fold_in(rng, 2), count)]


def bell_draw(stream_key, dims, scale, limit, shards=(), kind=jnp.bfloat16):
    drawn = scale * jax.random.normal(stream_key, dims, jnp.float32)
    if shards:
        drawn = drawn * steps_of(stream_key, dims, shards, -0.22, 0.18)
    return jnp.clip(drawn, -limit, limit).astype(kind)


def setup_inputs(seed: int = 0) -> dict:
    keys = jax.random.split(jax.random.key(seed), 23)
    tokens = bell_draw(keys[0], (SEQS, LEN, D), 1.0, 6.0, ((0, 8),))
    cotangent = bell_draw(keys[1], (SEQS, LEN, D), 1.0, 6.0, ((0, 8),))
    doc_lengths = jax.vmap(lambda own: ragged_sizes(own, DOCS, LEN, LEN // 2, 2))(jax.random.split(keys[2], SEQS)).reshape((SEQS, DOCS)).astype(jnp.int32)
    time_steps = touch_ends(jax.random.randint(keys[3], (SEQS,), 0, 1000), jax.random.fold_in(keys[3], 1), 0, 999).astype(jnp.int32)
    qkv_master = bell_draw(keys[4], (D, 3, D), D ** -0.5, 0.21875, ((0, 8), (2, 4)), jnp.float32)
    qkv_first = bell_draw(keys[5], (D, 3, D), (0.055 * TOKENS ** 0.5), 40.0, ((0, 8), (2, 4)), jnp.float32)
    qkv_second = jnp.clip(jnp.exp(math.log(16.384) - 1.3862944 * jax.random.uniform(keys[6], (D, 3, D), jnp.float32) ** steps_of(keys[6], (D, 3, D), ((0, 8), (2, 4)), -0.2, 0.2)), 4.096, 16.384)
    proj_master = bell_draw(keys[7], (D, D), (D // 16) ** -0.5, 0.875, ((0, 4), (1, 8)), jnp.float32)
    proj_first = bell_draw(keys[8], (D, D), (0.028 * TOKENS ** 0.5), 20.0, ((0, 4), (1, 8)), jnp.float32)
    proj_second = jnp.clip(jnp.exp(math.log(4.096) - 1.4271164 * jax.random.uniform(keys[9], (D, D), jnp.float32) ** steps_of(keys[9], (D, D), ((0, 4), (1, 8)), -0.2, 0.2)), 0.98304, 4.096)
    up_master = bell_draw(keys[10], (D, FF), D ** -0.5, 0.21875, ((0, 8), (1, 4)), jnp.float32)
    up_first = bell_draw(keys[11], (D, FF), (0.05 * TOKENS ** 0.5), 40.0, ((0, 8), (1, 4)), jnp.float32)
    up_second = jnp.clip(jnp.exp(math.log(13.1072) - 1.3862944 * jax.random.uniform(keys[12], (D, FF), jnp.float32) ** steps_of(keys[12], (D, FF), ((0, 8), (1, 4)), -0.2, 0.2)), 3.2768, 13.1072)
    down_master = bell_draw(keys[13], (FF, D), FF ** -0.5, 0.109375, ((0, 4), (1, 8)), jnp.float32)
    down_first = bell_draw(keys[14], (FF, D), (0.09 * TOKENS ** 0.5), 64.0, ((0, 4), (1, 8)), jnp.float32)
    down_second = jnp.clip(jnp.exp(math.log(42.5984) - 1.4017986 * jax.random.uniform(keys[15], (FF, D), jnp.float32) ** steps_of(keys[15], (FF, D), ((0, 4), (1, 8)), -0.2, 0.2)), 10.48576, 42.5984)
    ada_master = bell_draw(keys[16], (COND, 6 * D), (4 * COND) ** -0.5, 0.25, ((0, 8),), jnp.float32)
    ada_first = bell_draw(keys[17], (COND, 6 * D), (0.08 * TOKENS ** 0.5), 64.0, ((0, 8),), jnp.float32)
    ada_second = jnp.clip(jnp.exp(math.log(32.768) - 1.3862944 * jax.random.uniform(keys[18], (COND, 6 * D), jnp.float32) ** steps_of(keys[18], (COND, 6 * D), ((0, 8),), -0.2, 0.2)), 8.192, 32.768)
    vec_master = draw_vec_master(jax.random.fold_in(keys[22], 71), 0)
    vec_first = bell_draw(keys[20], (VROWS, D), (0.11 * TOKENS ** 0.5), 80.0, (), jnp.float32)
    vec_second = jnp.clip(jnp.exp(jax.random.uniform(keys[21], (VROWS, D), jnp.float32, math.log(16.384), math.log(65.536))), 16.384, 65.536)
    return dict(tokens=tokens, cotangent=cotangent, doc_lengths=doc_lengths, time_steps=time_steps, qkv_master=qkv_master, qkv_first=qkv_first, qkv_second=qkv_second, proj_master=proj_master, proj_first=proj_first, proj_second=proj_second, up_master=up_master, up_first=up_first, up_second=up_second, down_master=down_master, down_first=down_first, down_second=down_second, ada_master=ada_master, ada_first=ada_first, ada_second=ada_second, vec_master=vec_master, vec_first=vec_first, vec_second=vec_second)


@jax.custom_vjp
def low(v):
    return lax.optimization_barrier(v.astype(jnp.bfloat16)).astype(jnp.float32)

@jax.custom_vjp
def low_back(v):
    return v

def low_keep(v):
    return (low(v), None)

def low_pass(kept, grad):
    return (grad,)

def back_keep(v):
    return (v, None)

def back_low(kept, grad):
    return (low(grad),)
low.defvjp(low_keep, low_pass)
low_back.defvjp(back_keep, back_low)
EPS_NORM = 1e-05
ROPE_BASE = 10000.0
RATE = 0.14
RATE_VEC = 0.4
BETA_ONE = 0.9
BETA_TWO = 0.999
EPS_ADAM = 1e-08
DECAY = 0.1
NEG_BIG = -1e+30
PRECISE = lax.Precision.HIGHEST

def time_features(steps, width):
    half_size = width // 2
    freqs = jnp.exp(-jnp.log(10000.0) * jnp.arange(half_size, dtype=jnp.float32) / half_size)
    angles = steps.astype(jnp.float32)[:, None] * freqs[None, :]
    return jnp.concatenate([jnp.cos(angles), jnp.sin(angles)], axis=1)

def doc_layout(doc_lens, length):
    doc_ends = jnp.cumsum(doc_lens).astype(jnp.int32)
    places = jnp.arange(length, dtype=jnp.int32)
    passed = (places[:, None] >= doc_ends[None, :]).astype(jnp.int32)
    return (lax.optimization_barrier(jnp.sum(passed, axis=1)), places - lax.optimization_barrier(jnp.sum(passed * doc_lens[None, :], axis=1)))

def rotary_tables(positions, head_size):
    half_size = head_size // 2
    inverse = jnp.exp(-jnp.log(ROPE_BASE) * jnp.arange(half_size, dtype=jnp.float32) * 2.0 / head_size)
    angles = positions.astype(jnp.float32)[..., None] * inverse
    angles = jnp.concatenate([angles, angles], axis=-1)
    return (jnp.cos(angles), jnp.sin(angles))

def rotate_half(values):
    half_size = values.shape[-1] // 2
    return jnp.concatenate([-values[..., half_size:], values[..., :half_size]], axis=-1)

def norm_rows(values):
    centred = values - lax.optimization_barrier(jnp.mean(values, axis=-1, keepdims=True))
    return centred * lax.rsqrt(lax.optimization_barrier(jnp.mean(centred * centred, axis=-1, keepdims=True)) + EPS_NORM)

def layer_one(x_seq, doc_lens, step_no, weights, vec_w):
    w_qkv, w_proj, w_up, w_down, w_ada = weights
    cond_raw = low(time_features(step_no[None], COND)[0])
    modulate = (low_back(jnp.dot(cond_raw, w_ada, precision=PRECISE)) + vec_w[3:9].reshape(6 * D)).reshape(6, D)
    doc_ids, positions = doc_layout(doc_lens, LEN)
    cosine, sine = rotary_tables(positions, HEAD)
    cosine = cosine[:, None, :]
    sine = sine[:, None, :]
    h_attn = low(norm_rows(x_seq) * vec_w[0] * (1.0 + modulate[1]) + modulate[0])
    proj_qkv = low_back(jnp.dot(h_attn, w_qkv.reshape(D, 3 * D), precision=PRECISE)).reshape(LEN, 3, HEADS, HEAD)
    queries = low(proj_qkv[:, 0] * cosine + rotate_half(proj_qkv[:, 0]) * sine)
    keys_all = low(proj_qkv[:, 1] * cosine + rotate_half(proj_qkv[:, 1]) * sine)
    values_all = low(proj_qkv[:, 2])
    same_doc = doc_ids[:, None] == doc_ids[None, :]
    scores = low_back(jnp.einsum('qhd,khd->hqk', queries, keys_all, precision=PRECISE) * (1.0 / math.sqrt(HEAD)))
    scores = jnp.where(same_doc[None], scores, NEG_BIG)
    soft_probs = low(jax.nn.softmax(scores, axis=-1))
    mixed_out = low(low_back(jnp.einsum('hqk,khd->qhd', soft_probs, values_all, precision=PRECISE)))
    head_groups = mixed_out.reshape(LEN, N_MP, D // N_MP)
    group_parts = low(jnp.einsum('lgf,gfe->lge', head_groups, w_proj.reshape(N_MP, D // N_MP, D), precision=PRECISE))
    attn_out = low_back(lax.optimization_barrier(jnp.sum(group_parts, axis=1)))
    x_mid = x_seq + modulate[2] * attn_out
    h_mlp = low(norm_rows(x_mid) * vec_w[1] * (1.0 + modulate[4]) + modulate[3])
    up_pre = low_back(jnp.dot(h_mlp, w_up, precision=PRECISE) + vec_w[9:].reshape(FF))
    act_out = low(jax.nn.gelu(up_pre, approximate=True))
    unit_groups = act_out.reshape(LEN, N_MP, FF // N_MP)
    down_parts = low(jnp.einsum('lgf,gfe->lge', unit_groups, w_down.reshape(N_MP, FF // N_MP, D), precision=PRECISE))
    mlp_out = low_back(lax.optimization_barrier(jnp.sum(down_parts, axis=1))) + vec_w[2]
    return x_mid + modulate[5] * mlp_out

def forward(x_all, qkv_w, proj_w, up_w, down_w, ada_w, vec_w, doc_lengths, time_steps):
    weights = (low(qkv_w), low(proj_w), low(up_w), low(down_w), low(ada_w))

    def one_seq(item_set):
        return layer_one(item_set[0], item_set[1], item_set[2], weights, vec_w)
    return lax.map(jax.checkpoint(one_seq), (x_all, doc_lengths, time_steps))

def adamw(master, moment_one, second, gradient, decay_rate, rate_now):
    first_new = BETA_ONE * moment_one + (1.0 - BETA_ONE) * gradient
    second_new = BETA_TWO * second + (1.0 - BETA_TWO) * gradient * gradient
    fix_one = 1.0 - BETA_ONE ** STEP
    fix_two = 1.0 - BETA_TWO ** STEP
    stepped = first_new / fix_one / (jnp.sqrt(second_new / fix_two) + EPS_ADAM)
    return (master - rate_now * (stepped + decay_rate * master), first_new, second_new)

def reference(tokens, cotangent, doc_lengths, time_steps, qkv_master, qkv_first, qkv_second, proj_master, proj_first, proj_second, up_master, up_first, up_second, down_master, down_first, down_second, ada_master, ada_first, ada_second, vec_master, vec_first, vec_second):

    def run_layer(x_all, qkv_w, proj_w, up_w, down_w, ada_w, vec_w):
        return forward(x_all, qkv_w, proj_w, up_w, down_w, ada_w, vec_w, doc_lengths, time_steps)
    result, pull = jax.vjp(run_layer, tokens.astype(jnp.float32), qkv_master, proj_master, up_master, down_master, ada_master, vec_master)
    grads = pull(cotangent.astype(jnp.float32))
    qkv_up = adamw(qkv_master, qkv_first, qkv_second, grads[1], DECAY, RATE)
    proj_up = adamw(proj_master, proj_first, proj_second, grads[2], DECAY, RATE)
    up_up = adamw(up_master, up_first, up_second, grads[3], DECAY, RATE)
    down_up = adamw(down_master, down_first, down_second, grads[4], DECAY, RATE)
    ada_up = adamw(ada_master, ada_first, ada_second, grads[5], DECAY, RATE)
    vec_up = adamw(vec_master, vec_first, vec_second, grads[6], 0.0, RATE_VEC)
    return (result.astype(jnp.bfloat16), grads[0], qkv_up[0], qkv_up[1], qkv_up[2], proj_up[0], proj_up[1], proj_up[2], up_up[0], up_up[1], up_up[2], down_up[0], down_up[1], down_up[2], ada_up[0], ada_up[1], ada_up[2], vec_up[0], vec_up[1], vec_up[2])
```

```python
from functools import partial
import math

import jax
import jax.numpy as jnp
import numpy as np
from jax import lax
from jax.experimental import pallas as pl
from jax.experimental.pallas import tpu as pltpu
from jax.sharding import PartitionSpec as P

HEAD = 64
COND = 128
STEP = 10


EPS_NORM = 1e-05
ROPE_BASE = 10000.0
RATE = 0.14
RATE_VEC = 0.4
BETA_ONE = 0.9
BETA_TWO = 0.999
EPS_ADAM = 1e-08
DECAY = 0.1
NEG_BIG = -1e30


def time_features(steps, width):
    half_size = width // 2
    freqs = jnp.exp(-jnp.log(10000.0) * jnp.arange(half_size, dtype=jnp.float32) / half_size)
    angles = steps.astype(jnp.float32)[:, None] * freqs[None, :]
    return jnp.concatenate([jnp.cos(angles), jnp.sin(angles)], axis=1)


def doc_layout(doc_lens, length):
    doc_ends = jnp.cumsum(doc_lens)
    places = jnp.arange(length, dtype=jnp.int32)
    passed = (places[:, None] >= doc_ends[None, :]).astype(jnp.int32)
    return (jnp.sum(passed, axis=1), places - jnp.sum(passed * doc_lens[None, :], axis=1))


def rotary_tables(positions, head_size):
    half_size = head_size // 2
    inverse = jnp.exp(
        -jnp.log(ROPE_BASE) * jnp.arange(half_size, dtype=jnp.float32) * 2.0 / head_size
    )
    angles = positions.astype(jnp.float32)[..., None] * inverse
    angles = jnp.concatenate([angles, angles], axis=-1)
    return (jnp.cos(angles), jnp.sin(angles))


def rotate_half(values):
    half_size = values.shape[-1] // 2
    return jnp.concatenate([-values[..., half_size:], values[..., :half_size]], axis=-1)


def rotate_apply(values, cosine, sine):
    return values * cosine + rotate_half(values) * sine


def rotate_back(gradient, cosine, sine):
    return gradient * cosine - rotate_half(gradient * sine)


def norm_rows(values):
    centred = values - jnp.mean(values, axis=-1, keepdims=True)
    inv_std = lax.rsqrt(jnp.mean(centred * centred, axis=-1, keepdims=True) + EPS_NORM)
    return (centred * inv_std, inv_std)


def norm_back(gradient, normed, inv_std):
    return inv_std * (
        gradient
        - jnp.mean(gradient, axis=-1, keepdims=True)
        - normed * jnp.mean(gradient * normed, axis=-1, keepdims=True)
    )


def adamw(master, moment_one, second, gradient, decay_rate, rate_now):
    first_new = BETA_ONE * moment_one + (1.0 - BETA_ONE) * gradient
    second_new = BETA_TWO * second + (1.0 - BETA_TWO) * gradient * gradient
    fix_one = 1.0 - BETA_ONE**STEP
    fix_two = 1.0 - BETA_TWO**STEP
    stepped = first_new / fix_one / (jnp.sqrt(second_new / fix_two) + EPS_ADAM)
    return (master - rate_now * (stepped + decay_rate * master), first_new, second_new)


def shards(
    tokens,
    cotangent,
    doc_lengths,
    time_steps,
    qkv_master,
    qkv_first,
    qkv_second,
    proj_master,
    proj_first,
    proj_second,
    up_master,
    up_first,
    up_second,
    down_master,
    down_first,
    down_second,
    ada_master,
    ada_first,
    ada_second,
    vec_master,
    vec_first,
    vec_second,
):
    w_qkv, w_proj, w_up, w_down, w_ada = (
        lax.all_gather(qkv_master.astype(jnp.bfloat16), "dp", axis=0, tiled=True),
        lax.all_gather(proj_master.astype(jnp.bfloat16), "dp", axis=1, tiled=True),
        lax.all_gather(up_master.astype(jnp.bfloat16), "dp", axis=0, tiled=True),
        lax.all_gather(down_master.astype(jnp.bfloat16), "dp", axis=1, tiled=True),
        lax.all_gather(ada_master.astype(jnp.bfloat16), "dp", axis=0, tiled=True),
    )
    seq_count, length, model_width = tokens.shape
    row_count = seq_count * length
    local_width = w_qkv.shape[2]
    local_heads = local_width // HEAD
    hidden_local = w_up.shape[1]
    mp_index = lax.axis_index("mp")
    block_rows = min(512, length)
    blocks = length // block_rows
    factor = 1.0 / math.sqrt(HEAD)
    cond_b = time_features(time_steps, COND).astype(jnp.bfloat16)
    modulate = (
        jnp.dot(cond_b, w_ada, preferred_element_type=jnp.float32) + vec_master[3:9].reshape(-1)
    ).reshape(seq_count, 6, model_width)
    shift_one = modulate[:, 0, None]
    scale_one = modulate[:, 1, None]
    gate_one = modulate[:, 2, None]
    shift_two = modulate[:, 3, None]
    scale_two = modulate[:, 4, None]
    gate_two = modulate[:, 5, None]
    gain_one = vec_master[0]
    gain_two = vec_master[1]
    down_bias = vec_master[2]
    up_bias = lax.dynamic_slice_in_dim(
        vec_master[9:].reshape(-1), mp_index * hidden_local, hidden_local
    )
    doc_ids, positions = jax.vmap(partial(doc_layout, length=length))(doc_lengths)
    cosine, sine = rotary_tables(positions, HEAD)
    cosine = cosine[:, :, None, :]
    sine = sine[:, :, None, :]
    x_in = tokens.astype(jnp.float32)
    normed_one, inv_one = norm_rows(x_in)
    h_attn = (
        (normed_one * gain_one * (1.0 + scale_one) + shift_one)
        .astype(jnp.bfloat16)
        .reshape(row_count, model_width)
    )
    w_qkv_flat = w_qkv.reshape(model_width, 3 * local_width)
    proj_qkv = jnp.dot(h_attn, w_qkv_flat, preferred_element_type=jnp.float32).reshape(
        seq_count, length, 3, local_heads, HEAD
    )
    queries = rotate_apply(proj_qkv[:, :, 0], cosine, sine).astype(jnp.bfloat16)
    keys_all = rotate_apply(proj_qkv[:, :, 1], cosine, sine).astype(jnp.bfloat16)
    values_all = proj_qkv[:, :, 2].astype(jnp.bfloat16)

    def attend(block_index):
        seq_no = block_index // blocks
        offset = block_index % blocks * block_rows
        query_blk = lax.dynamic_slice_in_dim(queries[seq_no], offset, block_rows, 0)
        doc_query = lax.dynamic_slice_in_dim(doc_ids[seq_no], offset, block_rows, 0)
        same_doc = doc_query[:, None] == doc_ids[seq_no][None, :]
        scores = (
            jnp.einsum(
                "qhd,khd->hqk", query_blk, keys_all[seq_no], preferred_element_type=jnp.float32
            )
            * factor
        )
        scores = jnp.where(same_doc[None], scores, NEG_BIG)
        row_max = jnp.max(scores, axis=-1, keepdims=True)
        expo = jnp.exp(scores - row_max)
        totals = jnp.sum(expo, axis=-1, keepdims=True)
        soft_probs = (expo / totals).astype(jnp.bfloat16)
        mixed = jnp.einsum(
            "hqk,khd->qhd", soft_probs, values_all[seq_no], preferred_element_type=jnp.float32
        )
        return (mixed.astype(jnp.bfloat16), (row_max + jnp.log(totals))[..., 0])

    mixed_blocks, log_totals = lax.map(attend, jnp.arange(seq_count * blocks))
    mixed_flat = mixed_blocks.reshape(row_count, local_width)
    attn_out = (
        lax.psum(
            jnp.dot(mixed_flat, w_proj, preferred_element_type=jnp.float32).astype(jnp.bfloat16),
            "mp",
        )
        .astype(jnp.float32)
        .reshape(seq_count, length, model_width)
    )
    x_mid = x_in + gate_one * attn_out
    normed_two, inv_two = norm_rows(x_mid)
    h_mlp = (
        (normed_two * gain_two * (1.0 + scale_two) + shift_two)
        .astype(jnp.bfloat16)
        .reshape(row_count, model_width)
    )
    up_pre = jnp.dot(h_mlp, w_up, preferred_element_type=jnp.float32) + up_bias
    act_b = jax.nn.gelu(up_pre, approximate=True).astype(jnp.bfloat16)
    mlp_out = (
        lax.psum(
            jnp.dot(act_b, w_down, preferred_element_type=jnp.float32).astype(jnp.bfloat16), "mp"
        )
        .astype(jnp.float32)
        .reshape(seq_count, length, model_width)
        + down_bias
    )
    block_out = (x_mid + gate_two * mlp_out).astype(jnp.bfloat16)
    grad_y = cotangent.astype(jnp.float32)
    grad_mlp = grad_y * gate_two
    grad_gate_two = jnp.sum(grad_y * mlp_out, axis=1)
    grad_down_bias = jnp.sum(grad_mlp, axis=(0, 1))
    grad_mlp_b = grad_mlp.reshape(row_count, model_width).astype(jnp.bfloat16)
    grad_w_down = jnp.dot(act_b.T, grad_mlp_b, preferred_element_type=jnp.float32)
    grad_act = jnp.dot(grad_mlp_b, w_down.T, preferred_element_type=jnp.float32)
    unused, gelu_pull = jax.vjp(partial(jax.nn.gelu, approximate=True), up_pre)
    grad_up_b = gelu_pull(grad_act)[0].astype(jnp.bfloat16)
    grad_up_bias = jnp.sum(grad_up_b, axis=0, dtype=jnp.float32)
    grad_w_up = jnp.dot(h_mlp.T, grad_up_b, preferred_element_type=jnp.float32)
    grad_h_mlp = (
        lax.psum(
            jnp.dot(grad_up_b, w_up.T, preferred_element_type=jnp.float32).astype(jnp.bfloat16),
            "mp",
        )
        .astype(jnp.float32)
        .reshape(seq_count, length, model_width)
    )
    grad_shift_two = jnp.sum(grad_h_mlp, axis=1)
    grad_scale_two = jnp.sum(grad_h_mlp * normed_two * gain_two, axis=1)
    grad_gain_two = jnp.sum(grad_h_mlp * normed_two * (1.0 + scale_two), axis=(0, 1))
    grad_mid = grad_y + norm_back(grad_h_mlp * gain_two * (1.0 + scale_two), normed_two, inv_two)
    grad_gate_one = jnp.sum(grad_mid * attn_out, axis=1)
    grad_attn_b = (grad_mid * gate_one).reshape(row_count, model_width).astype(jnp.bfloat16)
    grad_w_proj = jnp.dot(mixed_flat.T, grad_attn_b, preferred_element_type=jnp.float32)
    grad_mixed = (
        jnp.dot(grad_attn_b, w_proj.T, preferred_element_type=jnp.float32)
        .astype(jnp.bfloat16)
        .reshape(seq_count, length, local_heads, HEAD)
    )

    def attend_back(seq_no):
        seq_keys = keys_all[seq_no]
        seq_values = values_all[seq_no]
        seq_docs = doc_ids[seq_no]

        def block_step(carry, block_no):
            key_acc, value_acc = carry
            offset = block_no * block_rows
            query_blk = lax.dynamic_slice_in_dim(queries[seq_no], offset, block_rows, 0)
            grad_blk = lax.dynamic_slice_in_dim(grad_mixed[seq_no], offset, block_rows, 0)
            doc_query = lax.dynamic_slice_in_dim(seq_docs, offset, block_rows, 0)
            same_doc = doc_query[:, None] == seq_docs[None, :]
            scores = (
                jnp.einsum("qhd,khd->hqk", query_blk, seq_keys, preferred_element_type=jnp.float32)
                * factor
            )
            kept_total = log_totals[seq_no * blocks + block_no][..., None]
            soft_probs = jnp.where(same_doc[None], jnp.exp(scores - kept_total), 0.0)
            probs_b = soft_probs.astype(jnp.bfloat16)
            grad_prob = jnp.einsum(
                "qhd,khd->hqk", grad_blk, seq_values, preferred_element_type=jnp.float32
            )
            delta_row = jnp.sum(soft_probs * grad_prob, axis=-1, keepdims=True)
            grad_score = (soft_probs * (grad_prob - delta_row)).astype(jnp.bfloat16)
            grad_query = (
                jnp.einsum("hqk,khd->qhd", grad_score, seq_keys, preferred_element_type=jnp.float32)
                * factor
            )
            key_acc = (
                key_acc
                + jnp.einsum(
                    "hqk,qhd->khd", grad_score, query_blk, preferred_element_type=jnp.float32
                )
                * factor
            )
            value_acc = value_acc + jnp.einsum(
                "hqk,qhd->khd", probs_b, grad_blk, preferred_element_type=jnp.float32
            )
            return ((key_acc, value_acc), grad_query)

        zeros_kv = jnp.zeros(seq_keys.shape, jnp.float32)
        (grad_key, grad_value), grad_query = lax.scan(
            block_step, (zeros_kv, zeros_kv), jnp.arange(blocks)
        )
        return (grad_query.reshape(length, local_heads, HEAD), grad_key, grad_value)

    grad_query, grad_key, grad_value = lax.map(attend_back, jnp.arange(seq_count))
    grad_proj = (
        jnp.stack(
            [
                rotate_back(grad_query, cosine, sine),
                rotate_back(grad_key, cosine, sine),
                grad_value,
            ],
            axis=2,
        )
        .astype(jnp.bfloat16)
        .reshape(row_count, 3 * local_width)
    )
    grad_w_qkv = jnp.dot(h_attn.T, grad_proj, preferred_element_type=jnp.float32).reshape(
        model_width, 3, local_width
    )
    grad_h_attn = (
        lax.psum(
            jnp.dot(grad_proj, w_qkv_flat.T, preferred_element_type=jnp.float32).astype(
                jnp.bfloat16
            ),
            "mp",
        )
        .astype(jnp.float32)
        .reshape(seq_count, length, model_width)
    )
    grad_shift_one = jnp.sum(grad_h_attn, axis=1)
    grad_scale_one = jnp.sum(grad_h_attn * normed_one * gain_one, axis=1)
    grad_gain_one = jnp.sum(grad_h_attn * normed_one * (1.0 + scale_one), axis=(0, 1))
    grad_tokens = grad_mid + norm_back(
        grad_h_attn * gain_one * (1.0 + scale_one), normed_one, inv_one
    )
    grad_mod = jnp.stack(
        [
            grad_shift_one,
            grad_scale_one,
            grad_gate_one,
            grad_shift_two,
            grad_scale_two,
            grad_gate_two,
        ],
        axis=1,
    )
    grad_mod_b = grad_mod.reshape(seq_count, 6 * model_width).astype(jnp.bfloat16)
    share_cols = model_width // lax.axis_size("mp")
    owned = (jnp.arange(model_width, dtype=jnp.int32) // share_cols == mp_index)[None, :]
    head_rows = jnp.concatenate(
        [grad_gain_one[None], grad_gain_two[None], grad_down_bias[None], jnp.sum(grad_mod, axis=0)],
        axis=0,
    )
    per_device = hidden_local // model_width
    bias_rows = lax.dynamic_update_slice_in_dim(
        jnp.zeros((vec_master.shape[0] - 9, model_width), jnp.float32),
        grad_up_bias.reshape(per_device, model_width),
        mp_index * per_device,
        0,
    )
    grad_vec = lax.psum(
        jnp.concatenate([jnp.where(owned, head_rows, 0.0), bias_rows], axis=0), ("dp", "mp")
    )
    grad_w_ada = jnp.dot(cond_b.T, grad_mod_b, preferred_element_type=jnp.float32)
    sum_qkv, sum_proj, sum_up, sum_down, sum_ada = (
        lax.psum_scatter(grad_w_qkv, "dp", scatter_dimension=0, tiled=True),
        lax.psum_scatter(grad_w_proj, "dp", scatter_dimension=1, tiled=True),
        lax.psum_scatter(grad_w_up, "dp", scatter_dimension=0, tiled=True),
        lax.psum_scatter(grad_w_down, "dp", scatter_dimension=1, tiled=True),
        lax.psum_scatter(grad_w_ada, "dp", scatter_dimension=0, tiled=True),
    )
    qkv_up = adamw(qkv_master, qkv_first, qkv_second, sum_qkv, DECAY, RATE)
    proj_up = adamw(proj_master, proj_first, proj_second, sum_proj, DECAY, RATE)
    up_up = adamw(up_master, up_first, up_second, sum_up, DECAY, RATE)
    down_up = adamw(down_master, down_first, down_second, sum_down, DECAY, RATE)
    ada_up = adamw(ada_master, ada_first, ada_second, sum_ada, DECAY, RATE)
    vec_up = adamw(vec_master, vec_first, vec_second, grad_vec, 0.0, RATE_VEC)
    return (
        block_out,
        grad_tokens,
        qkv_up[0],
        qkv_up[1],
        qkv_up[2],
        proj_up[0],
        proj_up[1],
        proj_up[2],
        up_up[0],
        up_up[1],
        up_up[2],
        down_up[0],
        down_up[1],
        down_up[2],
        ada_up[0],
        ada_up[1],
        ada_up[2],
        vec_up[0],
        vec_up[1],
        vec_up[2],
    )


LEN_FAST = 1024
WIDTH = 768
COPIES = 128
VMEM_BYTES = 66 * 2**20
NT = (((1,), (1,)), ((), ()))
NN = (((1,), (0,)), ((), ()))
TN = (((0,), (0,)), ((), ()))
F32 = jnp.float32
BF16 = jnp.bfloat16
MESH = pl.DeviceIdType.MESH
SHARD = 96
HALF = 48
QUARTER = 1152
CHUNKS = ((0, 0, 384), (0, 384, 384), (1, 0, 768), (2, 0, 768))


def mm(left, right, dims):
    return lax.dot_general(left, right, dims, preferred_element_type=F32)


def norm_tile(values):
    centred = values - jnp.mean(values, axis=1, keepdims=True)
    inv = lax.rsqrt(jnp.mean(centred * centred, axis=1, keepdims=True) + EPS_NORM)
    return centred * inv, inv


def rows(index, size):
    return pl.ds(pl.multiple_of(index * size, size), size)


def step_kernel(
    time_ref, doc_ref, tokens, cotangent, qkv_m, proj_m, up_m, down_m, ada_m, vec, freq, theta,
    grads_out, stats_out, block_out, grad_out,
    wt, ada, modq, mod, wq, tok, cot, h1, q, k, v, o, lse, cosine, sine, doc_col, doc_row,
    attn_own, attn_in, dh2_own, dh2_in, mlp_own, mlp_in,
    x1, h2, act, slope, dm, do, dzv, bo, g1, g2,
    r1a, r1b, r2, r3, st, dup, grads, acc, ka, va,
    local_sem, send_sem, recv_sem,
):
    dp = lax.axis_index("dp")
    mp = lax.axis_index("mp")
    z, y, x, core = dp // 2, dp % 2, mp // 2, mp % 2

    def device(zz, yy, xx, cc):
        return (zz * 2 + yy, xx * 2 + cc)

    to_core = device(z, y, x, 1 - core)
    to_x = device(z, y, 1 - x, core)
    to_diag = device(z, y, 1 - x, 1 - core)
    to_y = device(z, 1 - y, x, core)
    z_next = [lax.rem(z + hop, 4) for hop in range(4)]
    to_z = [device(z_next[hop], y, x, core) for hop in range(4)]
    counter = [0]
    sent = []
    done = []

    def send(src, dst, target):
        number = counter[0]
        counter[0] += 1
        copy = pltpu.make_async_remote_copy(
            src_ref=src, dst_ref=dst, send_sem=send_sem.at[number], recv_sem=recv_sem.at[number],
            device_id=target, device_id_type=MESH,
        )
        copy.start()
        sent.append(copy)
        return copy

    def arrive(copies):
        for copy in copies:
            copy.wait_recv()

    load_tok = pltpu.make_async_copy(tokens.at[x], tok, local_sem.at[0])
    load_cot = pltpu.make_async_copy(cotangent.at[x], cot, local_sem.at[1])
    load_tok.start()
    load_cot.start()

    wt[0, x, z, y] = jnp.concatenate(
        [qkv_m[:, 0, :], qkv_m[:, 1, :], qkv_m[:, 2, :], jnp.transpose(proj_m[...])], axis=1
    ).astype(BF16)
    wt[1, x, z, y] = up_m[...].astype(BF16)
    wt[2, x, z, y] = jnp.transpose(down_m[...]).astype(BF16)
    ada[z, y] = ada_m[:, pl.ds(pl.multiple_of(mp * QUARTER, 128), QUARTER)].astype(BF16)

    barrier = pltpu.get_barrier_semaphore()
    partners = [to_core, to_x, to_diag, to_y] + to_z[1:]
    for partner in partners:
        pl.semaphore_signal(barrier, inc=1, device_id=partner, device_id_type=MESH)
    pl.semaphore_wait(barrier, len(partners))

    low, high = pl.ds(0, HALF), pl.ds(HALF, HALF)

    def gather_one(chunk):
        t, start, size = CHUNKS[chunk]
        cols = pl.ds(start, size)
        copies = []
        for part in (low, high):
            piece = wt.at[t, x, z, y, part, cols]
            copies += [send(piece, piece, to_z[hop]) for hop in (1, 2, 3)]
        return copies

    def gather_two(chunk):
        t, start, size = CHUNKS[chunk]
        cols = pl.ds(start, size)
        piece_a = wt.at[t, x, :, y, low, cols]
        piece_b = wt.at[t, x, :, y, high, cols]
        return [send(piece_a, piece_a, to_x), send(piece_b, piece_b, to_y)]

    def gather_three(chunk):
        t, start, size = CHUNKS[chunk]
        cols = pl.ds(start, size)
        piece_a = wt.at[t, :, :, y, low, cols]
        piece_b = wt.at[t, x, :, :, high, cols]
        return [send(piece_a, piece_a, to_y), send(piece_b, piece_b, to_x)]

    own_ada = ada.at[z, y]
    ada_one = [send(own_ada, own_ada, to_z[hop]) for hop in (1, 2, 3)]
    one = [None] * 4
    two = [None] * 4
    three = [None] * 4
    one[0] = gather_one(0)
    one[1] = gather_one(1)

    row_id = lax.broadcasted_iota(jnp.int32, (16, 128), 0)
    lane_id = lax.broadcasted_iota(jnp.int32, (16, 128), 1)
    steps = jnp.where(row_id == 0, time_ref[0], time_ref[1]).astype(F32)
    angles = steps * freq[0:1, :]
    cond = jnp.where(lane_id < 64, jnp.cos(angles), jnp.sin(angles)).astype(BF16)

    ends = []
    total = 0
    for number in range(4):
        total = total + doc_ref[x, number]
        ends.append(total)
    col_id = lax.broadcasted_iota(jnp.int32, (8, LEN_FAST), 1)
    doc_row[...] = sum((col_id >= end).astype(jnp.int32) for end in ends)

    @pl.loop(0, LEN_FAST // 128)
    def _(index):
        block = rows(index, 128)
        token_id = lax.broadcasted_iota(jnp.int32, (128, 128), 0) + index * 128
        lanes = lax.broadcasted_iota(jnp.int32, (128, 128), 1)
        doc_col[block, :] = sum((token_id >= end).astype(jnp.int32) for end in ends)
        begin = jnp.zeros((128, 128), jnp.int32)
        for end in ends[:3]:
            begin = jnp.where(token_id >= end, end, begin)
        turned = (token_id - begin).astype(F32) * theta[0:1, :]
        cosine[block, :] = jnp.cos(turned)
        turned_sine = jnp.sin(turned)
        sine[block, :] = jnp.where(lax.rem(lanes, 64) < 32, -turned_sine, turned_sine)

    arrive(ada_one)
    own_ada = ada.at[:, y]
    ada_two = [send(own_ada, own_ada, to_y)]
    arrive(one[0])
    two[0] = gather_two(0)
    arrive(ada_two)
    modq[mp] = mm(cond, ada[...].reshape(COND, QUARTER), NN)[0:8]
    own_mod = modq.at[mp]
    mod_copies = [send(own_mod, own_mod, target) for target in (to_core, to_x, to_diag)]
    arrive(one[1])
    one[2] = gather_one(2)
    arrive(two[0])
    three[0] = gather_three(0)
    two[1] = gather_two(1)
    arrive(mod_copies)
    own_row = pl.ds(x, 1)
    half_width = WIDTH // 2
    mod[0:1, :] = modq[0, own_row, 0:WIDTH] + vec[3:4, :]
    mod[1:2, :] = (
        jnp.concatenate([modq[0, own_row, WIDTH:QUARTER], modq[1, own_row, 0:half_width]], axis=1)
        + vec[4:5, :]
    )
    mod[2:3, :] = modq[1, own_row, half_width:QUARTER] + vec[5:6, :]
    mod[3:4, :] = modq[2, own_row, 0:WIDTH] + vec[6:7, :]
    mod[4:5, :] = (
        jnp.concatenate([modq[2, own_row, WIDTH:QUARTER], modq[3, own_row, 0:half_width]], axis=1)
        + vec[7:8, :]
    )
    mod[5:6, :] = modq[3, own_row, half_width:QUARTER] + vec[8:9, :]

    load_tok.wait()
    load_cot.wait()

    @pl.loop(0, LEN_FAST // 64)
    def _(index):
        block = rows(index, 64)
        normed, _ = norm_tile(tok[block, :].astype(F32))
        h1[block, :] = (normed * (vec[0:1, :] * (1.0 + mod[1:2, :])) + mod[0:1, :]).astype(BF16)
        dm[block, :] = (cot[block, :].astype(F32) * mod[5:6, :]).astype(BF16)

    arrive(two[1])
    three[1] = gather_three(1)
    arrive(one[2])
    two[2] = gather_two(2)
    one[3] = gather_one(3)

    def pull(part):
        begin = 192 * part
        halves = [
            wt[0, side, :, :, :, begin:begin + 192].reshape(WIDTH, 192) for side in (0, 1)
        ]
        wq[part] = jnp.concatenate(halves, axis=1)

    def rotate(tile, block):
        lanes = lax.broadcasted_iota(jnp.int32, tile.shape, 1)
        swapped = jnp.where(
            lax.rem(lanes, 64) < 32, pltpu.roll(tile, 96, 1), pltpu.roll(tile, 32, 1)
        )
        return tile * cosine[block, :] + swapped * sine[block, :]

    def rotate_transposed(tile, block):
        lanes = lax.broadcasted_iota(jnp.int32, tile.shape, 1)
        turned = tile * sine[block, :]
        swapped = jnp.where(
            lax.rem(lanes, 64) < 32, pltpu.roll(turned, 96, 1), pltpu.roll(turned, 32, 1)
        )
        return tile * cosine[block, :] + swapped

    arrive(three[0])
    pull(0)
    pull(1)

    @pl.loop(0, LEN_FAST // 256)
    def _(index):
        block = rows(index, 256)
        left = h1[block, :]
        for part, target, scale in ((0, q, 0.125), (1, k, 1.0)):
            full = mm(left, wq[part], NN)
            for pair in range(3):
                cols = slice(pair * 128, pair * 128 + 128)
                turned = rotate(full[:, cols], block)
                target[block, cols] = (turned.astype(BF16).astype(F32) * scale).astype(BF16)

    arrive(three[1])
    pull(2)
    pull(3)

    @pl.loop(0, LEN_FAST // 256)
    def _(index):
        block = rows(index, 256)
        v[block, :] = mm(h1[block, :], wq[2], NN).astype(BF16)

    arrive(two[2])
    three[2] = gather_three(2)
    arrive(one[3])
    two[3] = gather_two(3)

    def head_lanes(shape, head):
        lanes = lax.broadcasted_iota(jnp.int32, shape, 1)
        return (lanes < 64) if head == 0 else (lanes >= 64)

    def same_doc(block, size):
        return jnp.concatenate([doc_col[block, :]] * 8, axis=1) == doc_row[0:1, :]

    for pair in range(3):
        cols = slice(pair * 128, pair * 128 + 128)

        @pl.loop(0, LEN_FAST // 256)
        def _(index):
            block = rows(index, 256)
            query = q[block, cols]
            mixed = []
            kept = same_doc(block, 256)
            for head in range(2):
                masked = jnp.where(head_lanes(query.shape, head), query, jnp.zeros_like(query))
                scores = jnp.where(kept, mm(masked, k[:, cols], NT), NEG_BIG)
                top = jnp.max(scores, axis=1, keepdims=True)
                expo = jnp.exp(scores - top)
                total = jnp.sum(expo, axis=1, keepdims=True)
                probs = (expo * (1.0 / total)).astype(BF16)
                number = 2 * pair + head
                lse[block, number:number + 1] = top + jnp.log(total)
                mixed.append(mm(probs, v[:, cols], NN))
            o[block, cols] = jnp.where(
                head_lanes(mixed[0].shape, 0), mixed[0], mixed[1]
            ).astype(BF16)

        if pair == 0:
            arrive(two[3])
            three[3] = gather_three(3)

    def swap(own, incoming, make):
        copies = []
        for index in range(4):
            block = slice(index * 256, index * 256 + 256)
            own[block, :] = make(block).astype(BF16)
            piece = pl.ds(index * 256, 256)
            copies.append(send(own.at[piece, :], incoming.at[piece, :], to_core))
        return copies

    attn_copies = swap(attn_own, attn_in, lambda block: mm(o[block, :], wq[3], NT))

    for part in range(4):
        attn_copies[part].wait_recv()

        @pl.loop(part * 4, part * 4 + 4)
        def _(index):
            block = rows(index, 64)
            attn = attn_own[block, :].astype(F32) + attn_in[block, :].astype(F32)
            middle = tok[block, :].astype(F32) + mod[2:3, :] * attn
            x1[block, :] = middle
            normed, _ = norm_tile(middle)
            h2[block, :] = (normed * (vec[1:2, :] * (1.0 + mod[4:5, :])) + mod[3:4, :]).astype(BF16)

    arrive(three[2])
    for side in range(2):

        @pl.loop(0, LEN_FAST // 256)
        def _(index):
            block = rows(index, 256)
            bias = vec[pl.ds(9 + 2 * side + core, 1), :]
            u = mm(h2[block, :], wt[1, side].reshape(WIDTH, WIDTH), NN) + bias
            cubic = 0.044715 * u * u
            bent = jnp.tanh(0.7978845608028654 * u * (1.0 + cubic))
            act[side, block, :] = (0.5 * u * (1.0 + bent)).astype(BF16)
            rising = 0.7978845608028654 * (1.0 + 3.0 * cubic)
            slope[side, block, :] = (
                0.5 * (1.0 + bent) + 0.5 * u * (1.0 - bent * bent) * rising
            ).astype(BF16)

    def put(grad, t_ref, side, full):
        t_ref[side] = full.astype(BF16).reshape(4, 2, SHARD, full.shape[1])

    def reduce_one(t, source, cols):
        return [
            send(source.at[:, :, 1 - y, low, cols], r1a.at[t, :, :, :, cols], to_y),
            send(source.at[1 - x, :, :, high, cols], r1b.at[t, :, :, :, cols], to_x),
        ]

    def reduce_two(t, source, cols):
        width = cols.size
        r1a[t, :, :, :, cols] = (
            r1a[t, :, :, :, cols].astype(F32) + source[:, :, y, low, cols].astype(F32)
        ).astype(BF16)
        copy_a = send(r1a.at[t, 1 - x, :, :, cols], r2.at[t, 0, :, :, cols], to_x)
        r1b[t, :, :, :, cols] = (
            r1b[t, :, :, :, cols].astype(F32) + source[x, :, :, high, cols].astype(F32)
        ).astype(BF16)
        copy_b = send(r1b.at[t, :, 1 - y, :, cols], r2.at[t, 1, :, :, cols], to_y)
        return [copy_a, copy_b]

    def reduce_three(t, cols):
        r2[t, 0, :, :, cols] = (
            r2[t, 0, :, :, cols].astype(F32) + r1a[t, x, :, :, cols].astype(F32)
        ).astype(BF16)
        r2[t, 1, :, :, cols] = (
            r2[t, 1, :, :, cols].astype(F32) + r1b[t, :, y, :, cols].astype(F32)
        ).astype(BF16)
        return [
            send(r2.at[t, group, z_next[hop], :, cols], r3.at[t, group, hop - 1, :, cols], to_z[hop])
            for group in (0, 1) for hop in (1, 2, 3)
        ]

    def reduce_end(t, cols):
        for group, part in ((0, low), (1, high)):
            grads[t, part, cols] = (
                r2[t, group, z, :, cols].astype(F32) + r3[t, group, 0, :, cols].astype(F32)
                + r3[t, group, 1, :, cols].astype(F32) + r3[t, group, 2, :, cols].astype(F32)
            )

    whole = pl.ds(0, WIDTH)
    for side in range(2):
        put(None, g2, side, mm(dm[...], act[side], TN))
    down_one = reduce_one(2, g2, whole)

    arrive(three[3])
    for side in range(2):

        @pl.loop(0, LEN_FAST // 256)
        def _(index):
            block = rows(index, 256)
            back = mm(dm[block, :], wt[2, side].reshape(WIDTH, WIDTH), NN)
            slope[side, block, :] = (back * slope[side, block, :].astype(F32)).astype(BF16)

    for side in range(2):
        put(None, g1, side, mm(h2[...], slope[side], TN))
    up_one = reduce_one(1, g1, whole)

    def back_two(block):
        return mm(slope[0, block, :], wt[1, 0].reshape(WIDTH, WIDTH), NT) + mm(
            slope[1, block, :], wt[1, 1].reshape(WIDTH, WIDTH), NT
        )

    dh2_copies = swap(dh2_own, dh2_in, back_two)
    arrive(down_one)
    down_two = reduce_two(2, g2, whole)

    def forward_two(block):
        return mm(act[0, block, :], wt[2, 0].reshape(WIDTH, WIDTH), NT) + mm(
            act[1, block, :], wt[2, 1].reshape(WIDTH, WIDTH), NT
        )

    mlp_copies = swap(mlp_own, mlp_in, forward_two)

    dup[0] = jnp.zeros((8, WIDTH), F32)
    for side in range(2):
        dup[0, side:side + 1, :] = jnp.sum(slope[side].astype(F32), axis=0, keepdims=True)
    dup_copy = send(dup.at[0], dup.at[1], to_core)

    acc[...] = jnp.zeros_like(acc)

    def add_row(row, values):
        count = values.shape[0]
        acc[row] = acc[row] + jnp.sum(values.reshape(count // 8, 8, WIDTH), axis=0)

    for part in range(4):
        dh2_copies[part].wait_recv()
        mlp_copies[part].wait_recv()

        @pl.loop(part * 4, part * 4 + 4)
        def _(index):
            block = rows(index, 64)
            middle = x1[block, :]
            seen = cot[block, :].astype(F32)
            mlp = mlp_own[block, :].astype(F32) + mlp_in[block, :].astype(F32) + vec[2:3, :]
            bo[block, :] = (middle + mod[5:6, :] * mlp).astype(BF16)
            add_row(3, seen * mlp)
            add_row(4, seen)
            back = dh2_own[block, :].astype(F32) + dh2_in[block, :].astype(F32)
            normed, inv = norm_tile(middle)
            add_row(0, back)
            add_row(1, back * normed)
            scaled = back * (vec[1:2, :] * (1.0 + mod[4:5, :]))
            grad = seen + inv * (
                scaled - jnp.mean(scaled, axis=1, keepdims=True)
                - normed * jnp.mean(scaled * normed, axis=1, keepdims=True)
            )
            x1[block, :] = grad
            attn = attn_own[block, :].astype(F32) + attn_in[block, :].astype(F32)
            add_row(2, grad * attn)
            dm[block, :] = (grad * mod[2:3, :]).astype(BF16)

    own_half = rows(core, 512)

    def publish(own, out, sem):
        store = pltpu.make_async_copy(own, out.at[x], sem)
        store.start()
        return store, send(own.at[own_half, :], out.at[x, own_half, :], to_x)

    def share(out, copy):
        copy.wait_recv()
        piece = out.at[1 - x, own_half, :]
        return send(piece, piece, to_core)

    bo_store, bo_copy = publish(bo, block_out, local_sem.at[0])

    arrive(down_two)
    down_three = reduce_three(2, whole)
    arrive(up_one)
    up_two = reduce_two(1, g1, whole)

    for copy in one[2] + two[2] + three[2]:
        copy.wait_send()
        done.append(id(copy))
    g0 = wt.at[1]

    def spread(part, full):
        rounded = full.astype(BF16)
        for side in range(2):
            g0[side, :, :, :, 192 * part:192 * part + 192] = rounded[
                :, 192 * side:192 * side + 192
            ].reshape(4, 2, SHARD, 192)

    spread(3, mm(dm[...], o[...], TN))

    @pl.loop(0, LEN_FAST // 256)
    def _(index):
        block = rows(index, 256)
        do[block, :] = mm(dm[block, :], wq[3], NN).astype(BF16)

    dzqk = h2
    for pair in range(3):
        cols = slice(pair * 128, pair * 128 + 128)
        ka[...] = jnp.zeros_like(ka)
        va[...] = jnp.zeros_like(va)

        @pl.loop(0, LEN_FAST // 256)
        def _(index):
            block = rows(index, 256)
            query = q[block, cols]
            back = do[block, cols]
            kept = same_doc(block, 256)
            product = back.astype(F32) * o[block, cols].astype(F32)
            grad_q = []
            for head in range(2):
                number = 2 * pair + head
                lanes = head_lanes(query.shape, head)
                masked_q = jnp.where(lanes, query, jnp.zeros_like(query))
                masked_b = jnp.where(lanes, back, jnp.zeros_like(back))
                scores = mm(masked_q, k[:, cols], NT)
                probs = jnp.where(kept, jnp.exp(scores - lse[block, number:number + 1]), 0.0)
                moved = mm(masked_b, v[:, cols], NT)
                delta = jnp.sum(jnp.where(lanes, product, 0.0), axis=1, keepdims=True)
                grad_s = (probs * (moved - delta)).astype(BF16)
                grad_q.append(mm(grad_s, k[:, cols], NN))
                ka[...] += mm(grad_s, masked_q, TN)
                va[...] += mm(probs.astype(BF16), masked_b, TN)
            full = jnp.where(head_lanes(grad_q[0].shape, 0), grad_q[0], grad_q[1]) * 0.125
            dzqk[block, cols] = rotate_transposed(full, block).astype(BF16)

        every = pl.ds(0, LEN_FAST)
        dzqk[:, 384 + pair * 128:512 + pair * 128] = rotate_transposed(ka[...], every).astype(BF16)
        dzv[:, cols] = va[...].astype(BF16)
        if pair == 0:
            arrive(up_two)
            up_three = reduce_three(1, whole)
            arrive(down_three)
            reduce_end(2, whole)
        if pair == 1:
            arrive(up_three)
            reduce_end(1, whole)

    bo_share = share(block_out, bo_copy)

    spread(2, mm(h1[...], dzv[...], TN))
    for part in range(2):
        spread(part, mm(h1[...], dzqk[:, 384 * part:384 * part + 384], TN))
    first, last = pl.ds(0, 384), pl.ds(384, 384)
    last_one = reduce_one(0, g0, last)
    first_one = reduce_one(0, g0, first)

    def back_one(block):
        return (
            mm(dzqk[block, 0:384], wq[0], NT) + mm(dzqk[block, 384:768], wq[1], NT)
            + mm(dzv[block, :], wq[2], NT)
        )

    gt = slope.at[0]
    dh1_copies = swap(act.at[0], act.at[1], back_one)
    for part in range(4):
        dh1_copies[part].wait_recv()

        @pl.loop(part * 4, part * 4 + 4)
        def _(index):
            block = rows(index, 64)
            back = act[0, block, :].astype(F32) + act[1, block, :].astype(F32)
            normed, inv = norm_tile(tok[block, :].astype(F32))
            add_row(5, back)
            add_row(6, back * normed)
            scaled = back * (vec[0:1, :] * (1.0 + mod[1:2, :]))
            gt[block, :] = (
                x1[block, :] + inv * (
                    scaled - jnp.mean(scaled, axis=1, keepdims=True)
                    - normed * jnp.mean(scaled * normed, axis=1, keepdims=True)
                )
            ).astype(BF16)

    gt_store, gt_copy = publish(gt, grad_out, local_sem.at[1])

    sums = [jnp.sum(acc[row], axis=0, keepdims=True) for row in range(7)]
    shift2, prod2, gate1, gate2, seen, shift1, prod1 = sums
    dup_copy.wait_recv()
    first_rows = jnp.where(core == 0, dup[0], dup[1])
    second_rows = jnp.where(core == 0, dup[1], dup[0])
    cond_row = jnp.where(x == 0, cond[0:1, :].astype(F32), cond[1:2, :].astype(F32))
    st[x, z, y] = jnp.concatenate(
        [
            shift1, prod1 * vec[0:1, :], gate1, shift2, prod2 * vec[1:2, :], gate2,
            prod1 * (1.0 + mod[1:2, :]), prod2 * (1.0 + mod[4:5, :]), seen * mod[5:6, :],
            jnp.concatenate([cond_row, jnp.zeros((1, WIDTH - 128), F32)], axis=1),
            first_rows[0:1, :], second_rows[0:1, :], first_rows[1:2, :], second_rows[1:2, :],
            jnp.zeros((2, WIDTH), F32),
        ],
        axis=0,
    ).astype(BF16)
    own_stats = st.at[x, z, y]
    stats_one = [send(own_stats, own_stats, to_z[hop]) for hop in (1, 2, 3)]

    arrive(last_one)
    last_two = reduce_two(0, g0, last)
    arrive(first_one)
    first_two = reduce_two(0, g0, first)
    arrive(stats_one)
    own_stats = st.at[x, :, y]
    stats_two = [send(own_stats, own_stats, to_y)]
    arrive(last_two)
    last_three = reduce_three(0, last)
    arrive(first_two)
    first_three = reduce_three(0, first)
    arrive(stats_two)
    own_stats = st.at[x]
    stats_three = [send(own_stats, own_stats, to_x)]
    gt_share = share(grad_out, gt_copy)
    arrive(last_three)
    reduce_end(0, last)
    arrive(first_three)
    reduce_end(0, first)
    arrive(stats_three)
    grads_store = pltpu.make_async_copy(grads, grads_out, local_sem.at[2])
    stats_store = pltpu.make_async_copy(st, stats_out, local_sem.at[3])
    grads_store.start()
    stats_store.start()
    bo_share.wait_recv()
    gt_share.wait_recv()
    for copy in sent:
        if id(copy) not in done:
            copy.wait_send()
    for store in (bo_store, gt_store, grads_store, stats_store):
        store.wait()


def fast_shards(
    tokens, cotangent, doc_lengths, time_steps,
    qkv_master, qkv_first, qkv_second, proj_master, proj_first, proj_second,
    up_master, up_first, up_second, down_master, down_first, down_second,
    ada_master, ada_first, ada_second, vec_master, vec_first, vec_second,
):
    freq = np.tile(np.exp(-np.log(10000.0) * np.arange(64) / 64).astype(np.float32), (8, 2))
    theta = np.tile(np.exp(-np.log(ROPE_BASE) * np.arange(32) * 2.0 / HEAD).astype(np.float32), (8, 4))
    vmem = pl.BlockSpec(memory_space=pltpu.VMEM)
    smem = pl.BlockSpec(memory_space=pltpu.SMEM)
    anywhere = pl.BlockSpec(memory_space=pl.ANY)
    tall = (LEN_FAST, WIDTH)
    stack = (2, 4, 2, SHARD, WIDTH)
    buffers = [
        ((3,) + stack, BF16),
        ((4, 2, 16, QUARTER), BF16),
        ((4, 8, QUARTER), F32),
        ((8, WIDTH), F32),
        ((4, WIDTH, 384), BF16),
        (tall, BF16),
        (tall, BF16),
        (tall, BF16),
        ((LEN_FAST, 384), BF16),
        ((LEN_FAST, 384), BF16),
        ((LEN_FAST, 384), BF16),
        ((LEN_FAST, 384), BF16),
        ((LEN_FAST, 128), F32),
        ((LEN_FAST, 128), F32),
        ((LEN_FAST, 128), F32),
        ((LEN_FAST, 128), jnp.int32),
        ((8, LEN_FAST), jnp.int32),
        (tall, BF16), (tall, BF16),
        (tall, BF16), (tall, BF16),
        (tall, BF16), (tall, BF16),
        (tall, F32),
        (tall, BF16),
        ((2,) + tall, BF16),
        ((2,) + tall, BF16),
        (tall, BF16),
        ((LEN_FAST, 384), BF16),
        ((LEN_FAST, 384), BF16),
        (tall, BF16),
        (stack, BF16),
        (stack, BF16),
        ((3, 2, 4, HALF, WIDTH), BF16),
        ((3, 4, 2, HALF, WIDTH), BF16),
        ((3, 2, 4, HALF, WIDTH), BF16),
        ((3, 2, 3, HALF, WIDTH), BF16),
        ((2, 4, 2, 16, WIDTH), BF16),
        ((2, 8, WIDTH), F32),
        ((3, SHARD, WIDTH), F32),
        ((8, 8, WIDTH), F32),
        ((LEN_FAST, 128), F32),
        ((LEN_FAST, 128), F32),
    ]
    grads, stats, blocks, grad_tokens = pl.pallas_call(
        step_kernel,
        out_shape=[
            jax.ShapeDtypeStruct((3, SHARD, WIDTH), F32),
            jax.ShapeDtypeStruct((2, 4, 2, 16, WIDTH), BF16),
            jax.ShapeDtypeStruct((2,) + tall, BF16),
            jax.ShapeDtypeStruct((2,) + tall, BF16),
        ],
        in_specs=[smem, smem, anywhere, anywhere] + [vmem] * 8,
        out_specs=[anywhere] * 4,
        scratch_shapes=[pltpu.VMEM(shape, kind) for shape, kind in buffers]
        + [pltpu.SemaphoreType.DMA((4,)), pltpu.SemaphoreType.DMA((COPIES,)), pltpu.SemaphoreType.DMA((COPIES,))],
        compiler_params=pltpu.CompilerParams(
            collective_id=0, has_side_effects=True, vmem_limit_bytes=VMEM_BYTES
        ),
    )(time_steps, doc_lengths, tokens, cotangent, qkv_master, proj_master, up_master, down_master,
      ada_master, vec_master, freq, theta)
    dp = lax.axis_index("dp")
    sum_qkv = grads[0, :, :576].reshape(SHARD, 3, 192)
    sum_proj = grads[0, :, 576:].T
    sum_up = grads[1]
    sum_down = grads[2].T
    stats = stats.reshape(2, 8, 16, WIDTH)
    cond = lax.dynamic_slice_in_dim(stats[:, :, 9], dp * 16, 16, 2).reshape(16, 16)
    sum_ada = lax.dot_general(
        cond, stats[:, :, :6].reshape(16, 6 * WIDTH), TN, preferred_element_type=F32
    )
    total = jnp.sum(stats.astype(F32), axis=(0, 1))
    grad_vec = jnp.concatenate([total[6:9], total[0:6], total[10:14]], axis=0)
    qkv_up = adamw(qkv_master, qkv_first, qkv_second, sum_qkv, DECAY, RATE)
    proj_up = adamw(proj_master, proj_first, proj_second, sum_proj, DECAY, RATE)
    up_up = adamw(up_master, up_first, up_second, sum_up, DECAY, RATE)
    down_up = adamw(down_master, down_first, down_second, sum_down, DECAY, RATE)
    ada_up = adamw(ada_master, ada_first, ada_second, sum_ada, DECAY, RATE)
    vec_up = adamw(vec_master, vec_first, vec_second, grad_vec, 0.0, RATE_VEC)
    return (
        blocks, grad_tokens.astype(F32), *qkv_up, *proj_up, *up_up, *down_up, *ada_up, *vec_up
    )


def solution(mesh):
    placed = (
        P("dp", None, None),
        P("dp", None, None),
        P("dp", None),
        P("dp"),
        P("dp", None, "mp"),
        P("dp", None, "mp"),
        P("dp", None, "mp"),
        P("mp", "dp"),
        P("mp", "dp"),
        P("mp", "dp"),
        P("dp", "mp"),
        P("dp", "mp"),
        P("dp", "mp"),
        P("mp", "dp"),
        P("mp", "dp"),
        P("mp", "dp"),
        P("dp", None),
        P("dp", None),
        P("dp", None),
        P(),
        P(),
        P(),
    )
    fast = mesh.shape["dp"] == 8 and mesh.shape["mp"] == 4
    return jax.shard_map(
        fast_shards if fast else shards,
        mesh=mesh,
        in_specs=placed,
        out_specs=(
            P("dp", None, None),
            P("dp", None, None),
            P("dp", None, "mp"),
            P("dp", None, "mp"),
            P("dp", None, "mp"),
            P("mp", "dp"),
            P("mp", "dp"),
            P("mp", "dp"),
            P("dp", "mp"),
            P("dp", "mp"),
            P("dp", "mp"),
            P("mp", "dp"),
            P("mp", "dp"),
            P("mp", "dp"),
            P("dp", None),
            P("dp", None),
            P("dp", None),
            P(),
            P(),
            P(),
        ),
        check_vma=False,
    )
```

```python
from functools import partial
import math

import jax
import jax.numpy as jnp
import numpy as np
from jax import lax
from jax.experimental import pallas as pl
from jax.experimental.pallas import tpu as pltpu
from jax.sharding import PartitionSpec as P

HEAD = 64
COND = 128
STEP = 10


EPS_NORM = 1e-05
ROPE_BASE = 10000.0
RATE = 0.14
RATE_VEC = 0.4
BETA_ONE = 0.9
BETA_TWO = 0.999
EPS_ADAM = 1e-08
DECAY = 0.1
NEG_BIG = -1e30


def time_features(steps, width):
    half_size = width // 2
    freqs = jnp.exp(-jnp.log(10000.0) * jnp.arange(half_size, dtype=jnp.float32) / half_size)
    angles = steps.astype(jnp.float32)[:, None] * freqs[None, :]
    return jnp.concatenate([jnp.cos(angles), jnp.sin(angles)], axis=1)


def doc_layout(doc_lens, length):
    doc_ends = jnp.cumsum(doc_lens)
    places = jnp.arange(length, dtype=jnp.int32)
    passed = (places[:, None] >= doc_ends[None, :]).astype(jnp.int32)
    return (jnp.sum(passed, axis=1), places - jnp.sum(passed * doc_lens[None, :], axis=1))


def rotary_tables(positions, head_size):
    half_size = head_size // 2
    inverse = jnp.exp(
        -jnp.log(ROPE_BASE) * jnp.arange(half_size, dtype=jnp.float32) * 2.0 / head_size
    )
    angles = positions.astype(jnp.float32)[..., None] * inverse
    angles = jnp.concatenate([angles, angles], axis=-1)
    return (jnp.cos(angles), jnp.sin(angles))


def rotate_half(values):
    half_size = values.shape[-1] // 2
    return jnp.concatenate([-values[..., half_size:], values[..., :half_size]], axis=-1)


def rotate_apply(values, cosine, sine):
    return values * cosine + rotate_half(values) * sine


def rotate_back(gradient, cosine, sine):
    return gradient * cosine - rotate_half(gradient * sine)


def norm_rows(values):
    centred = values - jnp.mean(values, axis=-1, keepdims=True)
    inv_std = lax.rsqrt(jnp.mean(centred * centred, axis=-1, keepdims=True) + EPS_NORM)
    return (centred * inv_std, inv_std)


def norm_back(gradient, normed, inv_std):
    return inv_std * (
        gradient
        - jnp.mean(gradient, axis=-1, keepdims=True)
        - normed * jnp.mean(gradient * normed, axis=-1, keepdims=True)
    )


def adamw(master, moment_one, second, gradient, decay_rate, rate_now):
    first_new = BETA_ONE * moment_one + (1.0 - BETA_ONE) * gradient
    second_new = BETA_TWO * second + (1.0 - BETA_TWO) * gradient * gradient
    fix_one = 1.0 - BETA_ONE**STEP
    fix_two = 1.0 - BETA_TWO**STEP
    stepped = first_new / fix_one / (jnp.sqrt(second_new / fix_two) + EPS_ADAM)
    return (master - rate_now * (stepped + decay_rate * master), first_new, second_new)


def shards(
    tokens,
    cotangent,
    doc_lengths,
    time_steps,
    qkv_master,
    qkv_first,
    qkv_second,
    proj_master,
    proj_first,
    proj_second,
    up_master,
    up_first,
    up_second,
    down_master,
    down_first,
    down_second,
    ada_master,
    ada_first,
    ada_second,
    vec_master,
    vec_first,
    vec_second,
):
    w_qkv, w_proj, w_up, w_down, w_ada = (
        lax.all_gather(qkv_master.astype(jnp.bfloat16), "dp", axis=0, tiled=True),
        lax.all_gather(proj_master.astype(jnp.bfloat16), "dp", axis=1, tiled=True),
        lax.all_gather(up_master.astype(jnp.bfloat16), "dp", axis=0, tiled=True),
        lax.all_gather(down_master.astype(jnp.bfloat16), "dp", axis=1, tiled=True),
        lax.all_gather(ada_master.astype(jnp.bfloat16), "dp", axis=0, tiled=True),
    )
    seq_count, length, model_width = tokens.shape
    row_count = seq_count * length
    local_width = w_qkv.shape[2]
    local_heads = local_width // HEAD
    hidden_local = w_up.shape[1]
    mp_index = lax.axis_index("mp")
    block_rows = min(512, length)
    blocks = length // block_rows
    factor = 1.0 / math.sqrt(HEAD)
    cond_b = time_features(time_steps, COND).astype(jnp.bfloat16)
    modulate = (
        jnp.dot(cond_b, w_ada, preferred_element_type=jnp.float32) + vec_master[3:9].reshape(-1)
    ).reshape(seq_count, 6, model_width)
    shift_one = modulate[:, 0, None]
    scale_one = modulate[:, 1, None]
    gate_one = modulate[:, 2, None]
    shift_two = modulate[:, 3, None]
    scale_two = modulate[:, 4, None]
    gate_two = modulate[:, 5, None]
    gain_one = vec_master[0]
    gain_two = vec_master[1]
    down_bias = vec_master[2]
    up_bias = lax.dynamic_slice_in_dim(
        vec_master[9:].reshape(-1), mp_index * hidden_local, hidden_local
    )
    doc_ids, positions = jax.vmap(partial(doc_layout, length=length))(doc_lengths)
    cosine, sine = rotary_tables(positions, HEAD)
    cosine = cosine[:, :, None, :]
    sine = sine[:, :, None, :]
    x_in = tokens.astype(jnp.float32)
    normed_one, inv_one = norm_rows(x_in)
    h_attn = (
        (normed_one * gain_one * (1.0 + scale_one) + shift_one)
        .astype(jnp.bfloat16)
        .reshape(row_count, model_width)
    )
    w_qkv_flat = w_qkv.reshape(model_width, 3 * local_width)
    proj_qkv = jnp.dot(h_attn, w_qkv_flat, preferred_element_type=jnp.float32).reshape(
        seq_count, length, 3, local_heads, HEAD
    )
    queries = rotate_apply(proj_qkv[:, :, 0], cosine, sine).astype(jnp.bfloat16)
    keys_all = rotate_apply(proj_qkv[:, :, 1], cosine, sine).astype(jnp.bfloat16)
    values_all = proj_qkv[:, :, 2].astype(jnp.bfloat16)

    def attend(block_index):
        seq_no = block_index // blocks
        offset = block_index % blocks * block_rows
        query_blk = lax.dynamic_slice_in_dim(queries[seq_no], offset, block_rows, 0)
        doc_query = lax.dynamic_slice_in_dim(doc_ids[seq_no], offset, block_rows, 0)
        same_doc = doc_query[:, None] == doc_ids[seq_no][None, :]
        scores = (
            jnp.einsum(
                "qhd,khd->hqk", query_blk, keys_all[seq_no], preferred_element_type=jnp.float32
            )
            * factor
        )
        scores = jnp.where(same_doc[None], scores, NEG_BIG)
        row_max = jnp.max(scores, axis=-1, keepdims=True)
        expo = jnp.exp(scores - row_max)
        totals = jnp.sum(expo, axis=-1, keepdims=True)
        soft_probs = (expo / totals).astype(jnp.bfloat16)
        mixed = jnp.einsum(
            "hqk,khd->qhd", soft_probs, values_all[seq_no], preferred_element_type=jnp.float32
        )
        return (mixed.astype(jnp.bfloat16), (row_max + jnp.log(totals))[..., 0])

    mixed_blocks, log_totals = lax.map(attend, jnp.arange(seq_count * blocks))
    mixed_flat = mixed_blocks.reshape(row_count, local_width)
    attn_out = (
        lax.psum(
            jnp.dot(mixed_flat, w_proj, preferred_element_type=jnp.float32).astype(jnp.bfloat16),
            "mp",
        )
        .astype(jnp.float32)
        .reshape(seq_count, length, model_width)
    )
    x_mid = x_in + gate_one * attn_out
    normed_two, inv_two = norm_rows(x_mid)
    h_mlp = (
        (normed_two * gain_two * (1.0 + scale_two) + shift_two)
        .astype(jnp.bfloat16)
        .reshape(row_count, model_width)
    )
    up_pre = jnp.dot(h_mlp, w_up, preferred_element_type=jnp.float32) + up_bias
    act_b = jax.nn.gelu(up_pre, approximate=True).astype(jnp.bfloat16)
    mlp_out = (
        lax.psum(
            jnp.dot(act_b, w_down, preferred_element_type=jnp.float32).astype(jnp.bfloat16), "mp"
        )
        .astype(jnp.float32)
        .reshape(seq_count, length, model_width)
        + down_bias
    )
    block_out = (x_mid + gate_two * mlp_out).astype(jnp.bfloat16)
    grad_y = cotangent.astype(jnp.float32)
    grad_mlp = grad_y * gate_two
    grad_gate_two = jnp.sum(grad_y * mlp_out, axis=1)
    grad_down_bias = jnp.sum(grad_mlp, axis=(0, 1))
    grad_mlp_b = grad_mlp.reshape(row_count, model_width).astype(jnp.bfloat16)
    grad_w_down = jnp.dot(act_b.T, grad_mlp_b, preferred_element_type=jnp.float32)
    grad_act = jnp.dot(grad_mlp_b, w_down.T, preferred_element_type=jnp.float32)
    unused, gelu_pull = jax.vjp(partial(jax.nn.gelu, approximate=True), up_pre)
    grad_up_b = gelu_pull(grad_act)[0].astype(jnp.bfloat16)
    grad_up_bias = jnp.sum(grad_up_b, axis=0, dtype=jnp.float32)
    grad_w_up = jnp.dot(h_mlp.T, grad_up_b, preferred_element_type=jnp.float32)
    grad_h_mlp = (
        lax.psum(
            jnp.dot(grad_up_b, w_up.T, preferred_element_type=jnp.float32).astype(jnp.bfloat16),
            "mp",
        )
        .astype(jnp.float32)
        .reshape(seq_count, length, model_width)
    )
    grad_shift_two = jnp.sum(grad_h_mlp, axis=1)
    grad_scale_two = jnp.sum(grad_h_mlp * normed_two * gain_two, axis=1)
    grad_gain_two = jnp.sum(grad_h_mlp * normed_two * (1.0 + scale_two), axis=(0, 1))
    grad_mid = grad_y + norm_back(grad_h_mlp * gain_two * (1.0 + scale_two), normed_two, inv_two)
    grad_gate_one = jnp.sum(grad_mid * attn_out, axis=1)
    grad_attn_b = (grad_mid * gate_one).reshape(row_count, model_width).astype(jnp.bfloat16)
    grad_w_proj = jnp.dot(mixed_flat.T, grad_attn_b, preferred_element_type=jnp.float32)
    grad_mixed = (
        jnp.dot(grad_attn_b, w_proj.T, preferred_element_type=jnp.float32)
        .astype(jnp.bfloat16)
        .reshape(seq_count, length, local_heads, HEAD)
    )

    def attend_back(seq_no):
        seq_keys = keys_all[seq_no]
        seq_values = values_all[seq_no]
        seq_docs = doc_ids[seq_no]

        def block_step(carry, block_no):
            key_acc, value_acc = carry
            offset = block_no * block_rows
            query_blk = lax.dynamic_slice_in_dim(queries[seq_no], offset, block_rows, 0)
            grad_blk = lax.dynamic_slice_in_dim(grad_mixed[seq_no], offset, block_rows, 0)
            doc_query = lax.dynamic_slice_in_dim(seq_docs, offset, block_rows, 0)
            same_doc = doc_query[:, None] == seq_docs[None, :]
            scores = (
                jnp.einsum("qhd,khd->hqk", query_blk, seq_keys, preferred_element_type=jnp.float32)
                * factor
            )
            kept_total = log_totals[seq_no * blocks + block_no][..., None]
            soft_probs = jnp.where(same_doc[None], jnp.exp(scores - kept_total), 0.0)
            probs_b = soft_probs.astype(jnp.bfloat16)
            grad_prob = jnp.einsum(
                "qhd,khd->hqk", grad_blk, seq_values, preferred_element_type=jnp.float32
            )
            delta_row = jnp.sum(soft_probs * grad_prob, axis=-1, keepdims=True)
            grad_score = (soft_probs * (grad_prob - delta_row)).astype(jnp.bfloat16)
            grad_query = (
                jnp.einsum("hqk,khd->qhd", grad_score, seq_keys, preferred_element_type=jnp.float32)
                * factor
            )
            key_acc = (
                key_acc
                + jnp.einsum(
                    "hqk,qhd->khd", grad_score, query_blk, preferred_element_type=jnp.float32
                )
                * factor
            )
            value_acc = value_acc + jnp.einsum(
                "hqk,qhd->khd", probs_b, grad_blk, preferred_element_type=jnp.float32
            )
            return ((key_acc, value_acc), grad_query)

        zeros_kv = jnp.zeros(seq_keys.shape, jnp.float32)
        (grad_key, grad_value), grad_query = lax.scan(
            block_step, (zeros_kv, zeros_kv), jnp.arange(blocks)
        )
        return (grad_query.reshape(length, local_heads, HEAD), grad_key, grad_value)

    grad_query, grad_key, grad_value = lax.map(attend_back, jnp.arange(seq_count))
    grad_proj = (
        jnp.stack(
            [
                rotate_back(grad_query, cosine, sine),
                rotate_back(grad_key, cosine, sine),
                grad_value,
            ],
            axis=2,
        )
        .astype(jnp.bfloat16)
        .reshape(row_count, 3 * local_width)
    )
    grad_w_qkv = jnp.dot(h_attn.T, grad_proj, preferred_element_type=jnp.float32).reshape(
        model_width, 3, local_width
    )
    grad_h_attn = (
        lax.psum(
            jnp.dot(grad_proj, w_qkv_flat.T, preferred_element_type=jnp.float32).astype(
                jnp.bfloat16
            ),
            "mp",
        )
        .astype(jnp.float32)
        .reshape(seq_count, length, model_width)
    )
    grad_shift_one = jnp.sum(grad_h_attn, axis=1)
    grad_scale_one = jnp.sum(grad_h_attn * normed_one * gain_one, axis=1)
    grad_gain_one = jnp.sum(grad_h_attn * normed_one * (1.0 + scale_one), axis=(0, 1))
    grad_tokens = grad_mid + norm_back(
        grad_h_attn * gain_one * (1.0 + scale_one), normed_one, inv_one
    )
    grad_mod = jnp.stack(
        [
            grad_shift_one,
            grad_scale_one,
            grad_gate_one,
            grad_shift_two,
            grad_scale_two,
            grad_gate_two,
        ],
        axis=1,
    )
    grad_mod_b = grad_mod.reshape(seq_count, 6 * model_width).astype(jnp.bfloat16)
    share_cols = model_width // lax.axis_size("mp")
    owned = (jnp.arange(model_width, dtype=jnp.int32) // share_cols == mp_index)[None, :]
    head_rows = jnp.concatenate(
        [grad_gain_one[None], grad_gain_two[None], grad_down_bias[None], jnp.sum(grad_mod, axis=0)],
        axis=0,
    )
    per_device = hidden_local // model_width
    bias_rows = lax.dynamic_update_slice_in_dim(
        jnp.zeros((vec_master.shape[0] - 9, model_width), jnp.float32),
        grad_up_bias.reshape(per_device, model_width),
        mp_index * per_device,
        0,
    )
    grad_vec = lax.psum(
        jnp.concatenate([jnp.where(owned, head_rows, 0.0), bias_rows], axis=0), ("dp", "mp")
    )
    grad_w_ada = jnp.dot(cond_b.T, grad_mod_b, preferred_element_type=jnp.float32)
    sum_qkv, sum_proj, sum_up, sum_down, sum_ada = (
        lax.psum_scatter(grad_w_qkv, "dp", scatter_dimension=0, tiled=True),
        lax.psum_scatter(grad_w_proj, "dp", scatter_dimension=1, tiled=True),
        lax.psum_scatter(grad_w_up, "dp", scatter_dimension=0, tiled=True),
        lax.psum_scatter(grad_w_down, "dp", scatter_dimension=1, tiled=True),
        lax.psum_scatter(grad_w_ada, "dp", scatter_dimension=0, tiled=True),
    )
    qkv_up = adamw(qkv_master, qkv_first, qkv_second, sum_qkv, DECAY, RATE)
    proj_up = adamw(proj_master, proj_first, proj_second, sum_proj, DECAY, RATE)
    up_up = adamw(up_master, up_first, up_second, sum_up, DECAY, RATE)
    down_up = adamw(down_master, down_first, down_second, sum_down, DECAY, RATE)
    ada_up = adamw(ada_master, ada_first, ada_second, sum_ada, DECAY, RATE)
    vec_up = adamw(vec_master, vec_first, vec_second, grad_vec, 0.0, RATE_VEC)
    return (
        block_out,
        grad_tokens,
        qkv_up[0],
        qkv_up[1],
        qkv_up[2],
        proj_up[0],
        proj_up[1],
        proj_up[2],
        up_up[0],
        up_up[1],
        up_up[2],
        down_up[0],
        down_up[1],
        down_up[2],
        ada_up[0],
        ada_up[1],
        ada_up[2],
        vec_up[0],
        vec_up[1],
        vec_up[2],
    )


LEN_FAST = 1024
WIDTH = 768
COPIES = 288
VMEM_BYTES = 66 * 2**20
NT = (((1,), (1,)), ((), ()))
NN = (((1,), (0,)), ((), ()))
TN = (((0,), (0,)), ((), ()))
F32 = jnp.float32
BF16 = jnp.bfloat16
MESH = pl.DeviceIdType.MESH
SHARD = 96
QUARTER = 1152
STACK = (2, 4, 2, SHARD, WIDTH)
CHUNKS = (
    (0, 0, 256), (0, 256, 256), (0, 512, 256), (1, 0, 384), (1, 384, 384), (2, 0, 384), (2, 384, 384),
)
GATHER = (
    ((0, 48, "zxy"), (48, 32, "zyx"), (80, 16, "xyz")),
    ((0, 48, "zxy"), (48, 48, "zyx")),
    ((0, 32, "zxy"), (32, 32, "zyx"), (64, 32, "xyz")),
)
REDUCE = (
    ((0, 64, "yxz"), (64, 16, "zyx"), (80, 16, "zxy")),
    ((0, 64, "yxz"), (64, 32, "xyz")),
    ((0, 32, "yxz"), (32, 32, "xyz"), (64, 32, "zyx")),
)
PLAN = (
    (("I", "g", 0, 0, 0), ("I", "g", 0, 1, 0), ("I", "g", 0, 2, 0), ("I", "g", 1, 2, 0), ("I", "g", 2, 2, 0)),
    (),
    (),
    (("W", "g", 0, 2, 0), ("W", "g", 1, 2, 0), ("W", "g", 2, 2, 0), ("I", "g", 0, 2, 1), ("I", "g", 1, 2, 1), ("I", "g", 2, 2, 1), ("I", "g", 5, 2, 0), ("I", "g", 6, 2, 0), ("W", "g", 0, 2, 1), ("W", "g", 1, 2, 1), ("W", "g", 2, 2, 1), ("W", "g", 5, 2, 0), ("W", "g", 6, 2, 0), ("I", "g", 5, 2, 1), ("I", "g", 6, 2, 1), ("W", "g", 0, 1, 0), ("I", "g", 0, 1, 1), ("I", "g", 1, 0, 0), ("W", "g", 0, 0, 0), ("I", "g", 0, 0, 1), ("I", "g", 1, 1, 0), ("I", "g", 2, 0, 0)),
    (),
    (("W", "g", 5, 2, 1), ("W", "g", 6, 2, 1), ("W", "g", 0, 1, 1), ("I", "g", 0, 1, 2), ("W", "g", 0, 0, 1), ("I", "g", 0, 0, 2), ("W", "g", 1, 0, 0), ("I", "g", 1, 0, 1), ("I", "g", 2, 1, 0), ("W", "g", 1, 1, 0), ("I", "g", 1, 1, 1), ("I", "g", 0, 2, 2), ("W", "g", 2, 0, 0), ("I", "g", 2, 0, 1), ("I", "g", 3, 0, 0)),
    (),
    (("W", "g", 2, 1, 0), ("I", "g", 2, 1, 1), ("I", "g", 3, 1, 0), ("W", "g", 1, 1, 1), ("W", "g", 0, 1, 2), ("W", "g", 1, 0, 1), ("I", "g", 1, 0, 2), ("I", "g", 1, 1, 2)),
    (("W", "g", 2, 0, 1), ("W", "g", 0, 0, 2), ("I", "g", 2, 0, 2)),
    (("W", "g", 2, 1, 1), ("W", "g", 0, 2, 2), ("I", "g", 2, 1, 2), ("I", "g", 1, 2, 2)),
    (),
    (("W", "g", 3, 0, 0), ("I", "g", 3, 0, 1), ("I", "g", 4, 0, 0)),
    (("W", "g", 1, 1, 2), ("W", "g", 3, 1, 0), ("I", "g", 3, 1, 1), ("I", "g", 4, 1, 0)),
    (),
    (("W", "g", 2, 1, 2), ("W", "g", 1, 0, 2), ("W", "g", 1, 2, 2), ("I", "g", 2, 2, 2)),
    (("W", "g", 3, 0, 1), ("I", "g", 3, 0, 2)),
    (("W", "g", 2, 0, 2), ("W", "g", 4, 0, 0), ("W", "g", 3, 1, 1), ("I", "g", 3, 1, 2), ("I", "g", 4, 0, 1), ("I", "g", 5, 0, 0)),
    (("W", "g", 4, 1, 0), ("I", "g", 4, 1, 1), ("I", "g", 5, 1, 0)),
    (("W", "g", 2, 2, 2), ("I", "g", 6, 0, 0)),
    (),
    (("W", "g", 5, 0, 0), ("I", "g", 5, 0, 1), ("I", "g", 6, 1, 0)),
    (("W", "g", 3, 0, 2), ("W", "g", 4, 0, 1), ("W", "g", 5, 1, 0), ("W", "g", 6, 0, 0), ("W", "g", 4, 1, 1), ("I", "g", 4, 0, 2), ("I", "g", 4, 1, 2), ("I", "g", 5, 1, 1), ("I", "g", 5, 2, 2), ("I", "g", 6, 2, 2)),
    (),
    (("W", "g", 6, 1, 0), ("I", "g", 6, 1, 1)),
    (),
    (),
    (("W", "g", 3, 1, 2), ("I", "g", 6, 0, 1)),
    (),
    (),
    (),
    (("W", "g", 5, 0, 1),),
    (),
    (),
    (("W", "g", 5, 1, 1), ("I", "g", 5, 0, 2), ("I", "g", 5, 1, 2)),
    (("W", "g", 6, 1, 1), ("W", "g", 6, 0, 1), ("I", "g", 6, 0, 2), ("I", "g", 6, 1, 2)),
    (("I", "r", 5, 2, 0),),
    (("W", "g", 4, 1, 2), ("I", "r", 5, 1, 0), ("W", "g", 4, 0, 2), ("I", "r", 5, 0, 0)),
    (),
    (),
    (),
    (),
    (("I", "r", 6, 0, 0), ("I", "r", 6, 1, 0), ("I", "r", 6, 2, 0), ("W", "g", 5, 0, 2), ("W", "g", 5, 1, 2), ("W", "g", 5, 2, 2), ("W", "g", 6, 2, 2)),
    (("W", "g", 6, 0, 2), ("W", "g", 6, 1, 2)),
    (("W", "r", 5, 1, 0), ("I", "r", 5, 1, 1)),
    (("I", "r", 3, 0, 0), ("I", "r", 3, 1, 0)),
    (),
    (("W", "r", 5, 0, 0), ("I", "r", 5, 0, 1)),
    (("W", "r", 6, 1, 0), ("I", "r", 6, 1, 1)),
    (("I", "r", 4, 1, 0),),
    (("W", "r", 5, 2, 0), ("W", "r", 6, 0, 0), ("I", "r", 6, 0, 1)),
    (("W", "r", 5, 1, 1), ("I", "r", 5, 2, 1), ("I", "r", 5, 1, 2)),
    (),
    (),
    (),
    (("W", "r", 6, 2, 0),),
    (("W", "r", 3, 1, 0), ("I", "b", 0, 0, 0)),
    (),
    (),
    (("W", "r", 5, 0, 1), ("W", "r", 6, 1, 1), ("I", "r", 5, 0, 2), ("I", "r", 6, 2, 1), ("I", "r", 6, 1, 2)),
    (("I", "b", 1, 0, 0),),
    (),
    (),
    (("W", "r", 5, 1, 2), ("W", "r", 5, 2, 1), ("I", "r", 5, 2, 2), ("I", "r", 3, 1, 1)),
    (),
    (),
    (),
    (),
    (),
    (("W", "r", 6, 0, 1), ("W", "r", 6, 2, 1), ("I", "r", 6, 0, 2), ("I", "r", 6, 2, 2), ("I", "r", 4, 0, 0)),
    (("W", "r", 5, 2, 2), ("W", "r", 5, 0, 2), ("W", "r", 6, 1, 2), ("W", "r", 4, 1, 0), ("I", "r", 4, 1, 1), ("I", "b", 2, 0, 0), ("I", "b", 3, 0, 0)),
    (("W", "r", 3, 1, 1), ("W", "r", 6, 2, 2), ("W", "r", 3, 0, 0), ("W", "r", 6, 0, 2), ("I", "r", 3, 0, 1), ("I", "r", 3, 1, 2)),
    (),
    (("I", "r", 0, 0, 0), ("I", "r", 0, 1, 0), ("I", "r", 0, 2, 0)),
    (("W", "b", 0, 0, 0), ("W", "r", 4, 1, 1), ("W", "b", 1, 0, 0), ("I", "r", 4, 1, 2)),
    (("W", "r", 3, 1, 2),),
    (("W", "r", 4, 0, 0), ("I", "r", 4, 0, 1)),
    (("I", "r", 1, 0, 0), ("I", "r", 1, 1, 0)),
    (("W", "r", 0, 1, 0), ("W", "r", 0, 2, 0), ("W", "r", 4, 1, 2), ("W", "b", 2, 0, 0), ("W", "b", 3, 0, 0), ("W", "r", 0, 0, 0), ("I", "r", 0, 0, 1), ("I", "r", 0, 1, 1), ("I", "r", 0, 2, 1), ("I", "r", 1, 2, 0)),
    (("W", "r", 3, 0, 1), ("W", "r", 1, 1, 0), ("W", "r", 0, 1, 1), ("W", "r", 0, 2, 1), ("I", "r", 3, 0, 2), ("I", "r", 0, 1, 2), ("I", "r", 0, 2, 2), ("I", "r", 1, 1, 1)),
    (("W", "r", 1, 0, 0), ("W", "r", 1, 2, 0), ("I", "r", 1, 0, 1), ("I", "r", 1, 2, 1)),
    (("I", "r", 2, 0, 0), ("I", "r", 2, 1, 0), ("I", "r", 2, 2, 0)),
    (("W", "r", 0, 2, 2), ("W", "r", 0, 1, 2), ("W", "r", 1, 1, 1), ("W", "r", 4, 0, 1), ("W", "r", 0, 0, 1), ("I", "r", 4, 0, 2), ("I", "r", 1, 1, 2)),
    (),
    (("W", "r", 1, 2, 1), ("I", "r", 1, 2, 2)),
    (("I", "t", 0, 0, 0),),
    (),
    (("W", "r", 1, 1, 2),),
    (("I", "t", 1, 0, 0),),
    (),
    (("W", "r", 1, 0, 1), ("W", "r", 1, 2, 2)),
    (("I", "t", 2, 0, 0),),
    (),
    (),
    (("I", "t", 3, 0, 0),),
    (("W", "r", 2, 0, 0), ("I", "r", 2, 0, 1)),
    (("W", "r", 3, 0, 2), ("W", "r", 2, 1, 0), ("W", "r", 2, 2, 0), ("I", "r", 0, 0, 2), ("I", "r", 1, 0, 2), ("I", "r", 2, 1, 1), ("W", "r", 2, 1, 1)),
    (("W", "t", 0, 0, 0), ("W", "r", 4, 0, 2), ("I", "r", 2, 2, 1)),
    (("W", "r", 0, 0, 2), ("W", "r", 1, 0, 2), ("W", "r", 2, 2, 1), ("I", "r", 2, 2, 2), ("W", "r", 2, 0, 1), ("I", "r", 2, 0, 2), ("I", "r", 2, 1, 2), ("W", "t", 1, 0, 0), ("W", "r", 2, 2, 2), ("W", "t", 2, 0, 0), ("W", "r", 2, 1, 2), ("W", "t", 3, 0, 0), ("W", "r", 2, 0, 2)),
    (),
)


def inbox_shapes():
    shapes = {}
    for chunk, (tensor, _, width) in enumerate(CHUNKS):
        for piece, (_, height, order) in enumerate(REDUCE[tensor]):
            for phase, axis in enumerate(order):
                extent = [
                    {"x": 2, "z": 4, "y": 2}[other] for other in "xzy" if other in order[phase + 1:]
                ]
                for hop in range(3 if axis == "z" else 1):
                    shapes[chunk, piece, phase, hop] = tuple(extent) + (height, width)
    return shapes


INBOX = inbox_shapes()


def mm(left, right, dims):
    return lax.dot_general(left, right, dims, preferred_element_type=F32)


def norm_tile(values):
    centred = values - jnp.mean(values, axis=1, keepdims=True)
    inv = lax.rsqrt(jnp.mean(centred * centred, axis=1, keepdims=True) + EPS_NORM)
    return centred * inv, inv


def rows(index, size):
    return pl.ds(pl.multiple_of(index * size, size), size)


def lower_lanes(shape):
    return lax.broadcasted_iota(jnp.int32, shape, 1) < 64


def interleave(first, second):
    lower = lower_lanes(first.shape)
    left = jnp.where(lower, first, pltpu.roll(second, 64, 1))
    right = jnp.where(lower, pltpu.roll(first, 64, 1), second)
    return left, right


def step_kernel(
    time_ref, doc_ref, tokens, cotangent, qkv_m, proj_m, up_m, down_m, ada_m, vec, freq, theta,
    grads_out, stats_out, block_out, grad_out,
    wt, ada, modq, mod, wqk, wv, wp, tok, cot, h1, q, k, v, o, lse, cosine, sine, same, other, kt, vt,
    attn_own, attn_in, dh2_in, mlp_in,
    x1, h2, act, slope, dm, do, dzv, bo, bo_in, gt_in, g1, g2, st, dup, dup_acc, grads, acc, ka, va,
    local_sem, send_sem, recv_sem, *inbox_refs,
):
    inbox = dict(zip(INBOX, inbox_refs))
    dp = lax.axis_index("dp")
    mp = lax.axis_index("mp")
    z, y, x, core = dp // 2, dp % 2, mp // 2, mp % 2
    own = {"x": x, "y": y, "z": z}

    def device(zz, yy, xx, cc):
        return (zz * 2 + yy, xx * 2 + cc)

    to_core = device(z, y, x, 1 - core)
    to_x = device(z, y, 1 - x, core)
    to_diag = device(z, y, 1 - x, 1 - core)
    to_y = device(z, 1 - y, x, core)
    z_next = [lax.rem(z + hop, 4) for hop in (1, 2, 3)]
    to_z = [device(place, y, x, core) for place in z_next]
    peers = {"x": [(1 - x, to_x)], "y": [(1 - y, to_y)], "z": list(zip(z_next, to_z))}
    counter = [0]
    sent = []
    done = []

    def send(src, dst, target):
        number = counter[0]
        counter[0] += 1
        assert number < COPIES
        copy = pltpu.make_async_remote_copy(
            src_ref=src, dst_ref=dst, send_sem=send_sem.at[number], recv_sem=recv_sem.at[number],
            device_id=target, device_id_type=MESH,
        )
        copy.start()
        sent.append(copy)
        return copy

    def arrive(copies):
        for copy in copies:
            copy.wait_recv()

    def flush(copies):
        for copy in copies:
            copy.wait_send()
            done.append(id(copy))

    barrier = pltpu.get_barrier_semaphore()
    partners = [to_core, to_x, to_diag, to_y] + to_z
    for partner in partners:
        pl.semaphore_signal(barrier, inc=1, device_id=partner, device_id_type=MESH)

    load_tok = pltpu.make_async_copy(tokens.at[x], tok, local_sem.at[0])
    load_cot = pltpu.make_async_copy(cotangent.at[x], cot, local_sem.at[1])
    load_tok.start()
    load_cot.start()

    ada[z, y] = ada_m[:, pl.ds(pl.multiple_of(mp * QUARTER, 128), QUARTER)].astype(BF16)
    proj_t = jnp.transpose(proj_m[...])
    wt[0, x, z, y] = jnp.concatenate(
        [
            part[:, 64 * head:64 * head + 64]
            for head in range(3) for part in (qkv_m[0], qkv_m[1], qkv_m[2], proj_t)
        ],
        axis=1,
    ).astype(BF16)
    wt[1, x, z, y] = up_m[...].astype(BF16)
    wt[2, x, z, y] = down_m[...].astype(BF16)

    pl.semaphore_wait(barrier, len(partners))

    def view(ref, fixed, height, columns):
        index = [fixed.get(axis, slice(None)) for axis in "xzy"]
        return ref.at[(*index, height, columns)]

    flying = {}
    sources = [wt.at[1], g1, g2]

    def gather(chunk, piece, phase):
        tensor, start, width = CHUNKS[chunk]
        first, height, order = GATHER[tensor][piece]
        fixed = {axis: own[axis] for axis in order[phase:]}
        block = view(wt.at[tensor], fixed, pl.ds(first, height), pl.ds(start, width))
        return [send(block, block, target) for _, target in peers[order[phase]]]

    def reduce(chunk, piece, phase):
        tensor, start, width = CHUNKS[chunk]
        first, height, order = REDUCE[tensor][piece]
        fixed = {axis: own[axis] for axis in order[:phase]}
        axis = order[phase]
        copies = []
        for hop, (place, target) in enumerate(peers[axis]):
            block = view(
                sources[tensor], {**fixed, axis: place}, pl.ds(first, height), pl.ds(start, width)
            )
            copies.append(send(block, inbox[chunk, piece, phase, hop], target))
        return copies

    def add_in(chunk, piece, phase):
        tensor, start, width = CHUNKS[chunk]
        first, height, order = REDUCE[tensor][piece]
        fixed = {axis: own[axis] for axis in order[:phase + 1]}
        index = [fixed.get(axis, slice(None)) for axis in "xzy"]
        place = (*index, pl.ds(first, height), pl.ds(start, width))
        total = sources[tensor][place].astype(F32)
        for hop in range(len(peers[order[phase]])):
            total = total + inbox[chunk, piece, phase, hop][...].astype(F32)
        if phase == 2:
            grads[tensor, pl.ds(first, height), pl.ds(start, width)] = total
        else:
            sources[tensor][place] = total.astype(BF16)

    def cross(ref, landing, part):
        piece = pl.ds(pl.multiple_of(part * 256 + core * 128, 128), 128)
        return [send(ref.at[piece, :], landing.at[piece, :], to_x)]

    def share(landing, part):
        piece = landing.at[pl.ds(pl.multiple_of(part * 256 + core * 128, 128), 128), :]
        shared.append(send(piece, piece, to_core))

    shared = []
    outputs = {"b": (bo, bo_in), "t": (slope.at[0], gt_in)}
    position = [0]

    def serve():
        for action, kind, chunk, piece, phase in PLAN[position[0]]:
            key = (kind, chunk, piece, phase)
            if action == "I":
                if kind == "g":
                    flying[key] = gather(chunk, piece, phase)
                elif kind == "r":
                    flying[key] = reduce(chunk, piece, phase)
                else:
                    flying[key] = cross(*outputs[kind], chunk)
            else:
                arrive(flying[key])
                if kind == "r":
                    add_in(chunk, piece, phase)
                elif kind != "g":
                    share(outputs[kind][1], chunk)
        position[0] += 1

    own_ada = ada.at[z, y]
    ada_one = [send(own_ada, own_ada, target) for target in to_z]
    serve()

    row_id = lax.broadcasted_iota(jnp.int32, (16, 128), 0)
    lane_id = lax.broadcasted_iota(jnp.int32, (16, 128), 1)
    steps = jnp.where(row_id == 0, time_ref[0], time_ref[1]).astype(F32)
    angles = steps * freq[0:1, :]
    cond = jnp.where(lane_id < 64, jnp.cos(angles), jnp.sin(angles)).astype(BF16)

    ends = []
    total = 0
    for number in range(4):
        total = total + doc_ref[x, number]
        ends.append(total)
    serve()

    def tables(index):
        block = rows(index, 128)
        token_id = lax.broadcasted_iota(jnp.int32, (128, 128), 0) + index * 128
        lanes = lax.broadcasted_iota(jnp.int32, (128, 128), 1)
        document = sum((token_id >= end).astype(jnp.int32) for end in ends)
        place = lax.rem(lanes, 64)
        same[block, :] = jnp.where(place == document, 1.0, 0.0).astype(BF16)
        apart = jnp.where((place < 4) & (place != document), NEG_BIG, 0.0)
        other[block, :] = jnp.where((place >= 4) & (place < 7), 1.0, apart).astype(BF16)
        begin = jnp.zeros((128, 128), jnp.int32)
        for end in ends[:3]:
            begin = jnp.where(token_id >= end, end, begin)
        turned = (token_id - begin).astype(F32) * theta[0:1, :]
        cosine[block, :] = jnp.cos(turned)
        turned_sine = jnp.sin(turned)
        sine[block, :] = jnp.where(lax.rem(lanes, 64) < 32, -turned_sine, turned_sine)

    pl.loop(0, 8)(tables)
    serve()
    serve()
    arrive(ada_one)
    own_ada = ada.at[:, y]
    ada_two = [send(own_ada, own_ada, to_y)]
    serve()
    serve()
    arrive(ada_two)
    modq[mp] = mm(cond, ada[...].reshape(COND, QUARTER), NN)[0:8]
    own_mod = modq.at[mp]
    mod_copies = [send(own_mod, own_mod, target) for target in (to_core, to_x, to_diag)]
    serve()
    serve()
    arrive(mod_copies)
    own_row = pl.ds(x, 1)
    half_width = WIDTH // 2
    mod[0:1, :] = modq[0, own_row, 0:WIDTH] + vec[3:4, :]
    mod[1:2, :] = (
        jnp.concatenate([modq[0, own_row, WIDTH:QUARTER], modq[1, own_row, 0:half_width]], axis=1)
        + vec[4:5, :]
    )
    mod[2:3, :] = modq[1, own_row, half_width:QUARTER] + vec[5:6, :]
    mod[3:4, :] = modq[2, own_row, 0:WIDTH] + vec[6:7, :]
    mod[4:5, :] = (
        jnp.concatenate([modq[2, own_row, WIDTH:QUARTER], modq[3, own_row, 0:half_width]], axis=1)
        + vec[7:8, :]
    )
    mod[5:6, :] = modq[3, own_row, half_width:QUARTER] + vec[8:9, :]

    load_tok.wait()
    load_cot.wait()

    for part in range(2):

        @pl.loop(part * 2, part * 2 + 2)
        def _(index):
            block = rows(index, 256)
            normed, _ = norm_tile(tok[block, :].astype(F32))
            h1[block, :] = (normed * (vec[0:1, :] * (1.0 + mod[1:2, :])) + mod[0:1, :]).astype(BF16)
            dm[block, :] = (cot[block, :].astype(F32) * mod[5:6, :]).astype(BF16)

        serve()

    def rotate(tile, block):
        lanes = lax.broadcasted_iota(jnp.int32, tile.shape, 1)
        swapped = jnp.where(
            lax.rem(lanes, 64) < 32, pltpu.roll(tile, 96, 1), pltpu.roll(tile, 32, 1)
        )
        return tile * cosine[block, :] + swapped * sine[block, :]

    def rotate_transposed(tile, block):
        lanes = lax.broadcasted_iota(jnp.int32, tile.shape, 1)
        turned = tile * sine[block, :]
        swapped = jnp.where(
            lax.rem(lanes, 64) < 32, pltpu.roll(turned, 96, 1), pltpu.roll(turned, 32, 1)
        )
        return tile * cosine[block, :] + swapped

    def project(pair):
        start = 256 * pair
        tiles = [
            [
                wt[0, side, :, :, :, start + 128 * part:start + 128 * part + 128].reshape(WIDTH, 128)
                for part in (0, 1)
            ]
            for side in (0, 1)
        ]
        cols = slice(pair * 128, pair * 128 + 128)
        both = slice(pair * 256, pair * 256 + 256)
        left, right = interleave(tiles[0][0], tiles[1][0])
        wqk[:, both] = jnp.concatenate([left, right], axis=1)
        wv[:, cols], wp[:, cols] = interleave(tiles[0][1], tiles[1][1])

        @pl.loop(0, LEN_FAST // 256)
        def _(index):
            block = rows(index, 256)
            full = mm(h1[block, :], wqk[:, both], NN)
            turned = rotate(full[:, 0:128], block).astype(BF16)
            q[block, cols] = (turned.astype(F32) * 0.125).astype(BF16)
            k[block, cols] = rotate(full[:, 128:256], block).astype(BF16)
            v[block, cols] = mm(h1[block, :], wv[:, cols], NN).astype(BF16)

    def own_half(shape, head):
        lower = lower_lanes(shape)
        return lower if head == 0 else ~lower

    def keep_head(tile, head):
        return jnp.where(own_half(tile.shape, head), tile, jnp.zeros_like(tile))

    def head_tiles(pair):
        cols = slice(pair * 128, pair * 128 + 128)
        for head in range(2):
            mine = own_half((LEN_FAST, 128), head)
            kt[head] = jnp.where(mine, k[:, cols], other[...])
            vt[head] = jnp.where(mine, v[:, cols], jnp.ones((LEN_FAST, 128), BF16))

    def beside(tile, values):
        place = lax.rem(lax.broadcasted_iota(jnp.int32, tile.shape, 1), 64)
        for number in range(3):
            term = values.astype(BF16)
            values = values - term.astype(F32)
            tile = jnp.where(place == 4 + number, term, tile)
        return tile

    def attend(pair, part):
        cols = slice(pair * 128, pair * 128 + 128)
        block = slice(512 * part, 512 * part + 512)
        if part == 0:
            head_tiles(pair)
        mixed = []
        for head in range(2):
            mine = own_half((512, 128), head)
            scores = mm(jnp.where(mine, q[block, cols], same[block, :]), kt[head], NT)
            top = jnp.max(scores, axis=1, keepdims=True)
            total = mm(jnp.exp(scores - top).astype(BF16), vt[head], NN)
            mixed.append(total * (1.0 / pltpu.roll(total, 64, 1)))
            number = 2 * pair + head
            beyond = 64 - 64 * head
            lse[block, number:number + 1] = top + jnp.log(total[:, beyond:beyond + 1])
        o[block, cols] = jnp.where(lower_lanes((512, 128)), mixed[0], mixed[1]).astype(BF16)

    for pair in range(3):
        serve()
        project(pair)
        serve()
        attend(pair, 0)
        serve()
        attend(pair, 1)
        serve()

    def swap(own_ref, incoming, make):
        copies = []
        for index in range(4):
            block = slice(index * 256, index * 256 + 256)
            own_ref[block, :] = make(block).astype(BF16)
            piece = pl.ds(index * 256, 256)
            copies.append(send(own_ref.at[piece, :], incoming.at[piece, :], to_core))
        return copies

    attn_copies = swap(attn_own, attn_in, lambda block: mm(o[block, :], wp[...], NT))
    serve()

    for part in range(4):
        serve()
        attn_copies[part].wait_recv()

        @pl.loop(part, part + 1)
        def _(index):
            block = rows(index, 256)
            attn = attn_own[block, :].astype(F32) + attn_in[block, :].astype(F32)
            middle = tok[block, :].astype(F32) + mod[2:3, :] * attn
            x1[block, :] = middle
            normed, _ = norm_tile(middle)
            h2[block, :] = (normed * (vec[1:2, :] * (1.0 + mod[4:5, :])) + mod[3:4, :]).astype(BF16)

        serve()

    def raise_hidden(half):
        cols = slice(384 * half, 384 * half + 384)
        for side in range(2):

            @pl.loop(0, LEN_FAST // 512)
            def _(index):
                block = rows(index, 512)
                bias = vec[pl.ds(9 + 2 * side + core, 1), cols]
                u = mm(h2[block, :], wt[1, side, :, :, :, cols].reshape(WIDTH, 384), NN) + bias
                square = u * u
                bent = jnp.tanh(u * (0.7978845608028654 + 0.03567740813636141 * square))
                half_u = 0.5 * u
                act[side, block, cols] = (half_u + half_u * bent).astype(BF16)
                rising = half_u * (0.7978845608028654 + 0.10703222440908423 * square)
                slope[side, block, cols] = (
                    0.5 + 0.5 * bent + (1.0 - bent * bent) * rising
                ).astype(BF16)

            serve()

        for side in range(2):
            grad = mm(dm[...], act[side, :, cols], TN).astype(BF16)
            g2[side, :, :, :, cols] = grad.reshape(4, 2, SHARD, 384)

    for half in range(2):
        serve()
        raise_hidden(half)
        serve()
        serve()

    def lower_hidden(half):
        cols = slice(384 * half, 384 * half + 384)
        for side in range(2):

            @pl.loop(0, LEN_FAST // 512)
            def _(index):
                block = rows(index, 512)
                back = mm(dm[block, :], wt[2, side, :, :, :, cols].reshape(WIDTH, 384), NN)
                grad = (back * slope[side, block, cols].astype(F32)).astype(BF16)
                slope[side, block, cols] = grad
                dup_acc[side, :, cols] = dup_acc[side, :, cols] + jnp.sum(
                    grad.astype(F32).reshape(64, 8, 384), axis=0
                )

        serve()
        for side in range(2):
            grad = mm(h2[...], slope[side, :, cols], TN).astype(BF16)
            g1[side, :, :, :, cols] = grad.reshape(4, 2, SHARD, 384)

    dup_acc[...] = jnp.zeros_like(dup_acc)
    for half in range(2):
        serve()
        lower_hidden(half)
        serve()
        serve()

    def back_two(block):
        return mm(slope[0, block, :], wt[1, 0].reshape(WIDTH, WIDTH), NT) + mm(
            slope[1, block, :], wt[1, 1].reshape(WIDTH, WIDTH), NT
        )

    dh2_own, mlp_own = slope.at[0], act.at[0]
    dh2_copies = swap(dh2_own, dh2_in, back_two)
    serve()

    def forward_two(block):
        return mm(act[0, block, :], wt[2, 0].reshape(WIDTH, WIDTH), NT) + mm(
            act[1, block, :], wt[2, 1].reshape(WIDTH, WIDTH), NT
        )

    mlp_copies = swap(mlp_own, mlp_in, forward_two)
    serve()

    dup[0] = jnp.zeros((8, WIDTH), F32)
    for side in range(2):
        dup[0, side:side + 1, :] = jnp.sum(dup_acc[side], axis=0, keepdims=True)
    dup_copy = send(dup.at[0], dup.at[1], to_core)
    serve()

    acc[...] = jnp.zeros_like(acc)

    def add_row(row, values):
        count = values.shape[0]
        acc[row] = acc[row] + jnp.sum(values.reshape(count // 8, 8, WIDTH), axis=0)

    for part in range(4):
        serve()
        dh2_copies[part].wait_recv()
        serve()
        mlp_copies[part].wait_recv()

        @pl.loop(part * 2, part * 2 + 2)
        def _(index):
            block = rows(index, 128)
            middle = x1[block, :]
            seen = cot[block, :].astype(F32)
            mlp = mlp_own[block, :].astype(F32) + mlp_in[block, :].astype(F32) + vec[2:3, :]
            bo[block, :] = (middle + mod[5:6, :] * mlp).astype(BF16)
            add_row(3, seen * mlp)
            add_row(4, seen)
            back = dh2_own[block, :].astype(F32) + dh2_in[block, :].astype(F32)
            normed, inv = norm_tile(middle)
            add_row(0, back)
            add_row(1, back * normed)
            scaled = back * (vec[1:2, :] * (1.0 + mod[4:5, :]))
            grad = seen + inv * (
                scaled - jnp.mean(scaled, axis=1, keepdims=True)
                - normed * jnp.mean(scaled * normed, axis=1, keepdims=True)
            )
            x1[block, :] = grad
            attn = attn_own[block, :].astype(F32) + attn_in[block, :].astype(F32)
            add_row(2, grad * attn)
            dm[block, :] = (grad * mod[2:3, :]).astype(BF16)

        serve()
        serve()

    bo_store = pltpu.make_async_copy(bo, block_out.at[x], local_sem.at[0])
    bo_store.start()

    @pl.loop(0, LEN_FAST // 256)
    def _(index):
        block = rows(index, 256)
        do[block, :] = mm(dm[block, :], wp[...], NN).astype(BF16)

    for key, copies in flying.items():
        if key[:2] in (("g", 3), ("g", 4)):
            flush(copies)
    g0 = sources[0]
    dzqk = h2

    def attend_back(pair, part):
        cols = slice(pair * 128, pair * 128 + 128)
        both = 256 * pair
        if part == 0:
            head_tiles(pair)
        width = LEN_FAST if part else LEN_FAST - 256

        @pl.loop(0, 2)
        def _(index):
            block = rows(1 + index if part else 3 * index, 256)
            keys = pl.ds(0, width) if part else pl.ds(pl.multiple_of(index * 256, 256), width)
            query = q[block, cols]
            back = do[block, cols]
            product = back.astype(F32) * o[block, cols].astype(F32)
            grad_q = []
            for head in range(2):
                number = 2 * pair + head
                mine = own_half(query.shape, head)
                queries = jnp.where(mine, query, beside(same[block, :], -lse[block, number:number + 1]))
                probs = jnp.exp(mm(queries, kt[head, keys, :], NT))
                delta = jnp.sum(keep_head(product, head), axis=1, keepdims=True)
                backs = jnp.where(mine, back, beside(jnp.zeros_like(back), -delta))
                grad_s = (probs * mm(backs, vt[head, keys, :], NT)).astype(BF16)
                grad_q.append(mm(grad_s, k[keys, cols], NN))
                ka[keys, :] += mm(grad_s, keep_head(query, head), TN)
                va[keys, :] += mm(probs.astype(BF16), keep_head(back, head), TN)
            full = jnp.where(lower_lanes(grad_q[0].shape), grad_q[0], grad_q[1]) * 0.125
            dzqk[block, both:both + 128] = rotate_transposed(full, block).astype(BF16)

    grad_p = mm(dm[...], o[...], TN).astype(BF16)
    for pair in range(3):
        g0[0, :, :, :, 256 * pair + 128:256 * pair + 256] = grad_p[
            :, 128 * pair:128 * pair + 128
        ].reshape(4, 2, SHARD, 128)

    def head_grads(pair):
        cols = slice(pair * 128, pair * 128 + 128)
        start = 256 * pair
        dzqk[:, start + 128:start + 256] = rotate_transposed(ka[...], pl.ds(0, LEN_FAST)).astype(BF16)
        dzv[:, cols] = va[...].astype(BF16)
        grad_qk = mm(h1[...], dzqk[:, start:start + 256], TN).astype(BF16)
        grad_v = mm(h1[...], dzv[:, cols], TN).astype(BF16)
        held = g0[0, :, :, :, start + 128:start + 256].reshape(WIDTH, 128)
        for number, (first, second) in enumerate(
            ((grad_qk[:, 0:128], grad_qk[:, 128:256]), (grad_v, held))
        ):
            sides = interleave(first, second)
            place = start + 128 * number
            for side in range(2):
                g0[side, :, :, :, place:place + 128] = sides[side].reshape(4, 2, SHARD, 128)

    def clear():
        ka[...] = jnp.zeros_like(ka)
        va[...] = jnp.zeros_like(va)

    serve()
    for pair in range(3):
        clear()
        attend_back(pair, 0)
        serve()
        attend_back(pair, 1)
        serve()
        head_grads(pair)
        serve()
        serve()

    def back_one(block):
        return mm(dzqk[block, :], wqk[...], NT) + mm(dzv[block, :], wv[...], NT)

    flush(dh2_copies)
    flush(mlp_copies)
    gt = slope.at[0]
    dh1_copies = swap(act.at[0], act.at[1], back_one)
    serve()
    for part in range(4):
        serve()
        dh1_copies[part].wait_recv()

        @pl.loop(part * 2, part * 2 + 2)
        def _(index):
            block = rows(index, 128)
            back = act[0, block, :].astype(F32) + act[1, block, :].astype(F32)
            normed, inv = norm_tile(tok[block, :].astype(F32))
            add_row(5, back)
            add_row(6, back * normed)
            scaled = back * (vec[0:1, :] * (1.0 + mod[1:2, :]))
            gt[block, :] = (
                x1[block, :] + inv * (
                    scaled - jnp.mean(scaled, axis=1, keepdims=True)
                    - normed * jnp.mean(scaled * normed, axis=1, keepdims=True)
                )
            ).astype(BF16)

        serve()
        serve()

    gt_store = pltpu.make_async_copy(gt, grad_out.at[x], local_sem.at[1])
    gt_store.start()

    sums = [jnp.sum(acc[row], axis=0, keepdims=True) for row in range(7)]
    shift2, prod2, gate1, gate2, seen, shift1, prod1 = sums
    dup_copy.wait_recv()
    first_rows = jnp.where(core == 0, dup[0], dup[1])
    second_rows = jnp.where(core == 0, dup[1], dup[0])
    cond_row = jnp.where(x == 0, cond[0:1, :].astype(F32), cond[1:2, :].astype(F32))
    st[x, z, y] = jnp.concatenate(
        [
            shift1, prod1 * vec[0:1, :], gate1, shift2, prod2 * vec[1:2, :], gate2,
            prod1 * (1.0 + mod[1:2, :]), prod2 * (1.0 + mod[4:5, :]), seen * mod[5:6, :],
            jnp.concatenate([cond_row, jnp.zeros((1, WIDTH - 128), F32)], axis=1),
            first_rows[0:1, :], second_rows[0:1, :], first_rows[1:2, :], second_rows[1:2, :],
            jnp.zeros((2, WIDTH), F32),
        ],
        axis=0,
    ).astype(BF16)
    own_stats = st.at[x, z, y]
    stats_one = [send(own_stats, own_stats, target) for target in to_z]
    serve()
    serve()
    arrive(stats_one)
    own_stats = st.at[x, :, y]
    stats_two = [send(own_stats, own_stats, to_y)]
    serve()
    arrive(stats_two)
    own_stats = st.at[x]
    stats_three = [send(own_stats, own_stats, to_x)]
    serve()
    grads_store = pltpu.make_async_copy(grads, grads_out, local_sem.at[2])
    grads_store.start()
    arrive(shared)
    bo_rest = pltpu.make_async_copy(bo_in, block_out.at[1 - x], local_sem.at[4])
    gt_rest = pltpu.make_async_copy(gt_in, grad_out.at[1 - x], local_sem.at[5])
    bo_rest.start()
    gt_rest.start()
    serve()
    arrive(stats_three)
    stats_store = pltpu.make_async_copy(st, stats_out, local_sem.at[3])
    stats_store.start()
    assert position[0] == len(PLAN)
    for copy in sent:
        if id(copy) not in done:
            copy.wait_send()
    for store in (bo_store, gt_store, grads_store, stats_store, bo_rest, gt_rest):
        store.wait()


def update_kernel(
    grads, stats, cond_in, blocks_in, gt,
    qkv_m, qkv_f, qkv_s, proj_m, proj_f, proj_s, up_m, up_f, up_s, down_m, down_f, down_s,
    ada_m, ada_f, ada_s, vec_m, vec_f, vec_s,
    blocks_out, gt_out,
    qkv_mo, qkv_fo, qkv_so, proj_mo, proj_fo, proj_so, up_mo, up_fo, up_so, down_mo, down_fo, down_so,
    ada_mo, ada_fo, ada_so, vec_mo, vec_fo, vec_so,
):
    step = pl.program_id(0)
    blocks_out[...] = blocks_in[...]
    gt_out[...] = gt[...].astype(F32)

    def put(refs, outs, gradient, decay, rate, index=...):
        new = adamw(refs[0][index], refs[1][index], refs[2][index], gradient, decay, rate)
        for out, value in zip(outs, new):
            out[index] = value

    @pl.when(step == 0)
    def _():
        packed = grads[0]
        for part in range(3):
            picked = [packed[:, 256 * head + 64 * part:256 * head + 64 * part + 64] for head in range(3)]
            put(
                (qkv_m, qkv_f, qkv_s), (qkv_mo, qkv_fo, qkv_so),
                jnp.concatenate(picked, axis=1), DECAY, RATE, part,
            )
        picked = [packed[:, 256 * head + 192:256 * head + 256] for head in range(3)]
        put(
            (proj_m, proj_f, proj_s), (proj_mo, proj_fo, proj_so),
            jnp.transpose(jnp.concatenate(picked, axis=1)), DECAY, RATE,
        )

    @pl.when(step == 1)
    def _():
        put((up_m, up_f, up_s), (up_mo, up_fo, up_so), grads[1], DECAY, RATE)

    @pl.when(step == 2)
    def _():
        put((down_m, down_f, down_s), (down_mo, down_fo, down_so), grads[2], DECAY, RATE)

    @pl.when(step == 3)
    def _():
        for part in range(6):
            cols = slice(WIDTH * part, WIDTH * part + WIDTH)
            gradient = mm(cond_in[...], stats[:, part, :], TN)
            put(
                (ada_m, ada_f, ada_s), (ada_mo, ada_fo, ada_so), gradient, DECAY, RATE,
                (slice(None), cols),
            )
        total = jnp.sum(stats[...].astype(F32), axis=0)
        gradient = jnp.concatenate([total[6:9], total[0:6], total[10:14]], axis=0)
        put((vec_m, vec_f, vec_s), (vec_mo, vec_fo, vec_so), gradient, 0.0, RATE_VEC)


def fast_shards(
    tokens, cotangent, doc_lengths, time_steps,
    qkv_master, qkv_first, qkv_second, proj_master, proj_first, proj_second,
    up_master, up_first, up_second, down_master, down_first, down_second,
    ada_master, ada_first, ada_second, vec_master, vec_first, vec_second,
):
    freq = np.tile(np.exp(-np.log(10000.0) * np.arange(64) / 64).astype(np.float32), (8, 2))
    theta = np.tile(np.exp(-np.log(ROPE_BASE) * np.arange(32) * 2.0 / HEAD).astype(np.float32), (8, 4))
    vmem = pl.BlockSpec(memory_space=pltpu.VMEM)
    smem = pl.BlockSpec(memory_space=pltpu.SMEM)
    anywhere = pl.BlockSpec(memory_space=pl.ANY)
    tall = (LEN_FAST, WIDTH)
    third = (LEN_FAST, 384)
    buffers = [
        ((3,) + STACK, BF16),
        ((4, 2, 16, QUARTER), BF16),
        ((4, 8, QUARTER), F32),
        ((8, WIDTH), F32),
        ((WIDTH, WIDTH), BF16), ((WIDTH, 384), BF16), ((WIDTH, 384), BF16),
        (tall, BF16), (tall, BF16), (tall, BF16),
        (third, BF16), (third, BF16), (third, BF16), (third, BF16),
        ((LEN_FAST, 128), F32),
        ((LEN_FAST, 128), F32), ((LEN_FAST, 128), F32),
        ((LEN_FAST, 128), BF16), ((LEN_FAST, 128), BF16),
        ((2, LEN_FAST, 128), BF16), ((2, LEN_FAST, 128), BF16),
        (tall, BF16), (tall, BF16),
        (tall, BF16), (tall, BF16),
        (tall, F32),
        (tall, BF16),
        ((2,) + tall, BF16), ((2,) + tall, BF16),
        (tall, BF16),
        (third, BF16), (third, BF16),
        (tall, BF16), (tall, BF16), (tall, BF16),
        (STACK, BF16), (STACK, BF16),
        ((2, 4, 2, 16, WIDTH), BF16),
        ((2, 8, WIDTH), F32), ((2, 8, WIDTH), F32),
        ((3, SHARD, WIDTH), F32),
        ((8, 8, WIDTH), F32),
        ((LEN_FAST, 128), F32), ((LEN_FAST, 128), F32),
    ]
    turned_qkv = [jnp.transpose(a, (1, 0, 2)) for a in (qkv_master, qkv_first, qkv_second)]
    turned_down = [a.T for a in (down_master, down_first, down_second)]
    grads, stats, blocks, grad_tokens = pl.pallas_call(
        step_kernel,
        out_shape=[
            jax.ShapeDtypeStruct((3, SHARD, WIDTH), F32),
            jax.ShapeDtypeStruct((2, 4, 2, 16, WIDTH), BF16),
            jax.ShapeDtypeStruct((2,) + tall, BF16),
            jax.ShapeDtypeStruct((2,) + tall, BF16),
        ],
        in_specs=[smem, smem, anywhere, anywhere] + [vmem] * 8,
        out_specs=[anywhere] * 4,
        scratch_shapes=[pltpu.VMEM(shape, kind) for shape, kind in buffers]
        + [pltpu.SemaphoreType.DMA((6,))] + [pltpu.SemaphoreType.DMA((COPIES,))] * 2
        + [pltpu.VMEM(shape, BF16) for shape in INBOX.values()],
        compiler_params=pltpu.CompilerParams(
            collective_id=0, has_side_effects=True, vmem_limit_bytes=VMEM_BYTES
        ),
    )(time_steps, doc_lengths, tokens, cotangent, turned_qkv[0], proj_master, up_master,
      turned_down[0], ada_master, vec_master, freq, theta)
    stats = stats.reshape(16, 16, WIDTH)
    cond = lax.dynamic_slice_in_dim(stats[:, 9], lax.axis_index("dp") * 16, 16, 1)
    states = [
        *turned_qkv, proj_master, proj_first, proj_second, up_master, up_first, up_second,
        *turned_down, ada_master, ada_first, ada_second, vec_master, vec_first, vec_second,
    ]

    def whole(a):
        return pl.BlockSpec(a.shape, lambda i: (0,) * a.ndim)

    strip = pl.BlockSpec((2, LEN_FAST // 4, WIDTH), lambda i: (0, i, 0))
    new = pl.pallas_call(
        update_kernel,
        grid=(4,),
        out_shape=[jax.ShapeDtypeStruct((2,) + tall, BF16), jax.ShapeDtypeStruct((2,) + tall, F32)]
        + [jax.ShapeDtypeStruct(a.shape, F32) for a in states],
        in_specs=[whole(grads), whole(stats), whole(cond), strip, strip] + [whole(a) for a in states],
        out_specs=[strip, strip] + [whole(a) for a in states],
        compiler_params=pltpu.CompilerParams(vmem_limit_bytes=VMEM_BYTES),
    )(grads, stats, cond, blocks, grad_tokens, *states)
    blocks, grad_tokens, *new = new
    new[0:3] = [jnp.transpose(a, (1, 0, 2)) for a in new[0:3]]
    new[9:12] = [a.T for a in new[9:12]]
    return (blocks, grad_tokens, *new)


def solution(mesh):
    placed = (
        P("dp", None, None),
        P("dp", None, None),
        P("dp", None),
        P("dp"),
        P("dp", None, "mp"),
        P("dp", None, "mp"),
        P("dp", None, "mp"),
        P("mp", "dp"),
        P("mp", "dp"),
        P("mp", "dp"),
        P("dp", "mp"),
        P("dp", "mp"),
        P("dp", "mp"),
        P("mp", "dp"),
        P("mp", "dp"),
        P("mp", "dp"),
        P("dp", None),
        P("dp", None),
        P("dp", None),
        P(),
        P(),
        P(),
    )
    fast = mesh.shape["dp"] == 8 and mesh.shape["mp"] == 4
    return jax.shard_map(
        fast_shards if fast else shards,
        mesh=mesh,
        in_specs=placed,
        out_specs=(
            P("dp", None, None),
            P("dp", None, None),
            P("dp", None, "mp"),
            P("dp", None, "mp"),
            P("dp", None, "mp"),
            P("mp", "dp"),
            P("mp", "dp"),
            P("mp", "dp"),
            P("dp", "mp"),
            P("dp", "mp"),
            P("dp", "mp"),
            P("mp", "dp"),
            P("mp", "dp"),
            P("mp", "dp"),
            P("dp", None),
            P("dp", None),
            P("dp", None),
            P(),
            P(),
            P(),
        ),
        check_vma=False,
    )
```

```python
from functools import partial
import math

import jax
import jax.numpy as jnp
import numpy as np
from jax import lax
from jax.experimental import pallas as pl
from jax.experimental.pallas import tpu as pltpu
from jax.sharding import PartitionSpec as P

HEAD = 64
COND = 128
STEP = 10


EPS_NORM = 1e-05
ROPE_BASE = 10000.0
RATE = 0.14
RATE_VEC = 0.4
BETA_ONE = 0.9
BETA_TWO = 0.999
EPS_ADAM = 1e-08
DECAY = 0.1
NEG_BIG = -1e30


def time_features(steps, width):
    half_size = width // 2
    freqs = jnp.exp(-jnp.log(10000.0) * jnp.arange(half_size, dtype=jnp.float32) / half_size)
    angles = steps.astype(jnp.float32)[:, None] * freqs[None, :]
    return jnp.concatenate([jnp.cos(angles), jnp.sin(angles)], axis=1)


def doc_layout(doc_lens, length):
    doc_ends = jnp.cumsum(doc_lens)
    places = jnp.arange(length, dtype=jnp.int32)
    passed = (places[:, None] >= doc_ends[None, :]).astype(jnp.int32)
    return (jnp.sum(passed, axis=1), places - jnp.sum(passed * doc_lens[None, :], axis=1))


def rotary_tables(positions, head_size):
    half_size = head_size // 2
    inverse = jnp.exp(
        -jnp.log(ROPE_BASE) * jnp.arange(half_size, dtype=jnp.float32) * 2.0 / head_size
    )
    angles = positions.astype(jnp.float32)[..., None] * inverse
    angles = jnp.concatenate([angles, angles], axis=-1)
    return (jnp.cos(angles), jnp.sin(angles))


def rotate_half(values):
    half_size = values.shape[-1] // 2
    return jnp.concatenate([-values[..., half_size:], values[..., :half_size]], axis=-1)


def rotate_apply(values, cosine, sine):
    return values * cosine + rotate_half(values) * sine


def rotate_back(gradient, cosine, sine):
    return gradient * cosine - rotate_half(gradient * sine)


def norm_rows(values):
    centred = values - jnp.mean(values, axis=-1, keepdims=True)
    inv_std = lax.rsqrt(jnp.mean(centred * centred, axis=-1, keepdims=True) + EPS_NORM)
    return (centred * inv_std, inv_std)


def norm_back(gradient, normed, inv_std):
    return inv_std * (
        gradient
        - jnp.mean(gradient, axis=-1, keepdims=True)
        - normed * jnp.mean(gradient * normed, axis=-1, keepdims=True)
    )


def adamw(master, moment_one, second, gradient, decay_rate, rate_now):
    first_new = BETA_ONE * moment_one + (1.0 - BETA_ONE) * gradient
    second_new = BETA_TWO * second + (1.0 - BETA_TWO) * gradient * gradient
    fix_one = 1.0 - BETA_ONE**STEP
    fix_two = 1.0 - BETA_TWO**STEP
    stepped = first_new / fix_one / (jnp.sqrt(second_new / fix_two) + EPS_ADAM)
    return (master - rate_now * (stepped + decay_rate * master), first_new, second_new)


def shards(
    tokens,
    cotangent,
    doc_lengths,
    time_steps,
    qkv_master,
    qkv_first,
    qkv_second,
    proj_master,
    proj_first,
    proj_second,
    up_master,
    up_first,
    up_second,
    down_master,
    down_first,
    down_second,
    ada_master,
    ada_first,
    ada_second,
    vec_master,
    vec_first,
    vec_second,
):
    w_qkv, w_proj, w_up, w_down, w_ada = (
        lax.all_gather(qkv_master.astype(jnp.bfloat16), "dp", axis=0, tiled=True),
        lax.all_gather(proj_master.astype(jnp.bfloat16), "dp", axis=1, tiled=True),
        lax.all_gather(up_master.astype(jnp.bfloat16), "dp", axis=0, tiled=True),
        lax.all_gather(down_master.astype(jnp.bfloat16), "dp", axis=1, tiled=True),
        lax.all_gather(ada_master.astype(jnp.bfloat16), "dp", axis=0, tiled=True),
    )
    seq_count, length, model_width = tokens.shape
    row_count = seq_count * length
    local_width = w_qkv.shape[2]
    local_heads = local_width // HEAD
    hidden_local = w_up.shape[1]
    mp_index = lax.axis_index("mp")
    block_rows = min(512, length)
    blocks = length // block_rows
    factor = 1.0 / math.sqrt(HEAD)
    cond_b = time_features(time_steps, COND).astype(jnp.bfloat16)
    modulate = (
        jnp.dot(cond_b, w_ada, preferred_element_type=jnp.float32) + vec_master[3:9].reshape(-1)
    ).reshape(seq_count, 6, model_width)
    shift_one = modulate[:, 0, None]
    scale_one = modulate[:, 1, None]
    gate_one = modulate[:, 2, None]
    shift_two = modulate[:, 3, None]
    scale_two = modulate[:, 4, None]
    gate_two = modulate[:, 5, None]
    gain_one = vec_master[0]
    gain_two = vec_master[1]
    down_bias = vec_master[2]
    up_bias = lax.dynamic_slice_in_dim(
        vec_master[9:].reshape(-1), mp_index * hidden_local, hidden_local
    )
    doc_ids, positions = jax.vmap(partial(doc_layout, length=length))(doc_lengths)
    cosine, sine = rotary_tables(positions, HEAD)
    cosine = cosine[:, :, None, :]
    sine = sine[:, :, None, :]
    x_in = tokens.astype(jnp.float32)
    normed_one, inv_one = norm_rows(x_in)
    h_attn = (
        (normed_one * gain_one * (1.0 + scale_one) + shift_one)
        .astype(jnp.bfloat16)
        .reshape(row_count, model_width)
    )
    w_qkv_flat = w_qkv.reshape(model_width, 3 * local_width)
    proj_qkv = jnp.dot(h_attn, w_qkv_flat, preferred_element_type=jnp.float32).reshape(
        seq_count, length, 3, local_heads, HEAD
    )
    queries = rotate_apply(proj_qkv[:, :, 0], cosine, sine).astype(jnp.bfloat16)
    keys_all = rotate_apply(proj_qkv[:, :, 1], cosine, sine).astype(jnp.bfloat16)
    values_all = proj_qkv[:, :, 2].astype(jnp.bfloat16)

    def attend(block_index):
        seq_no = block_index // blocks
        offset = block_index % blocks * block_rows
        query_blk = lax.dynamic_slice_in_dim(queries[seq_no], offset, block_rows, 0)
        doc_query = lax.dynamic_slice_in_dim(doc_ids[seq_no], offset, block_rows, 0)
        same_doc = doc_query[:, None] == doc_ids[seq_no][None, :]
        scores = (
            jnp.einsum(
                "qhd,khd->hqk", query_blk, keys_all[seq_no], preferred_element_type=jnp.float32
            )
            * factor
        )
        scores = jnp.where(same_doc[None], scores, NEG_BIG)
        row_max = jnp.max(scores, axis=-1, keepdims=True)
        expo = jnp.exp(scores - row_max)
        totals = jnp.sum(expo, axis=-1, keepdims=True)
        soft_probs = (expo / totals).astype(jnp.bfloat16)
        mixed = jnp.einsum(
            "hqk,khd->qhd", soft_probs, values_all[seq_no], preferred_element_type=jnp.float32
        )
        return (mixed.astype(jnp.bfloat16), (row_max + jnp.log(totals))[..., 0])

    mixed_blocks, log_totals = lax.map(attend, jnp.arange(seq_count * blocks))
    mixed_flat = mixed_blocks.reshape(row_count, local_width)
    attn_out = (
        lax.psum(
            jnp.dot(mixed_flat, w_proj, preferred_element_type=jnp.float32).astype(jnp.bfloat16),
            "mp",
        )
        .astype(jnp.float32)
        .reshape(seq_count, length, model_width)
    )
    x_mid = x_in + gate_one * attn_out
    normed_two, inv_two = norm_rows(x_mid)
    h_mlp = (
        (normed_two * gain_two * (1.0 + scale_two) + shift_two)
        .astype(jnp.bfloat16)
        .reshape(row_count, model_width)
    )
    up_pre = jnp.dot(h_mlp, w_up, preferred_element_type=jnp.float32) + up_bias
    act_b = jax.nn.gelu(up_pre, approximate=True).astype(jnp.bfloat16)
    mlp_out = (
        lax.psum(
            jnp.dot(act_b, w_down, preferred_element_type=jnp.float32).astype(jnp.bfloat16), "mp"
        )
        .astype(jnp.float32)
        .reshape(seq_count, length, model_width)
        + down_bias
    )
    block_out = (x_mid + gate_two * mlp_out).astype(jnp.bfloat16)
    grad_y = cotangent.astype(jnp.float32)
    grad_mlp = grad_y * gate_two
    grad_gate_two = jnp.sum(grad_y * mlp_out, axis=1)
    grad_down_bias = jnp.sum(grad_mlp, axis=(0, 1))
    grad_mlp_b = grad_mlp.reshape(row_count, model_width).astype(jnp.bfloat16)
    grad_w_down = jnp.dot(act_b.T, grad_mlp_b, preferred_element_type=jnp.float32)
    grad_act = jnp.dot(grad_mlp_b, w_down.T, preferred_element_type=jnp.float32)
    unused, gelu_pull = jax.vjp(partial(jax.nn.gelu, approximate=True), up_pre)
    grad_up_b = gelu_pull(grad_act)[0].astype(jnp.bfloat16)
    grad_up_bias = jnp.sum(grad_up_b, axis=0, dtype=jnp.float32)
    grad_w_up = jnp.dot(h_mlp.T, grad_up_b, preferred_element_type=jnp.float32)
    grad_h_mlp = (
        lax.psum(
            jnp.dot(grad_up_b, w_up.T, preferred_element_type=jnp.float32).astype(jnp.bfloat16),
            "mp",
        )
        .astype(jnp.float32)
        .reshape(seq_count, length, model_width)
    )
    grad_shift_two = jnp.sum(grad_h_mlp, axis=1)
    grad_scale_two = jnp.sum(grad_h_mlp * normed_two * gain_two, axis=1)
    grad_gain_two = jnp.sum(grad_h_mlp * normed_two * (1.0 + scale_two), axis=(0, 1))
    grad_mid = grad_y + norm_back(grad_h_mlp * gain_two * (1.0 + scale_two), normed_two, inv_two)
    grad_gate_one = jnp.sum(grad_mid * attn_out, axis=1)
    grad_attn_b = (grad_mid * gate_one).reshape(row_count, model_width).astype(jnp.bfloat16)
    grad_w_proj = jnp.dot(mixed_flat.T, grad_attn_b, preferred_element_type=jnp.float32)
    grad_mixed = (
        jnp.dot(grad_attn_b, w_proj.T, preferred_element_type=jnp.float32)
        .astype(jnp.bfloat16)
        .reshape(seq_count, length, local_heads, HEAD)
    )

    def attend_back(seq_no):
        seq_keys = keys_all[seq_no]
        seq_values = values_all[seq_no]
        seq_docs = doc_ids[seq_no]

        def block_step(carry, block_no):
            key_acc, value_acc = carry
            offset = block_no * block_rows
            query_blk = lax.dynamic_slice_in_dim(queries[seq_no], offset, block_rows, 0)
            grad_blk = lax.dynamic_slice_in_dim(grad_mixed[seq_no], offset, block_rows, 0)
            doc_query = lax.dynamic_slice_in_dim(seq_docs, offset, block_rows, 0)
            same_doc = doc_query[:, None] == seq_docs[None, :]
            scores = (
                jnp.einsum("qhd,khd->hqk", query_blk, seq_keys, preferred_element_type=jnp.float32)
                * factor
            )
            kept_total = log_totals[seq_no * blocks + block_no][..., None]
            soft_probs = jnp.where(same_doc[None], jnp.exp(scores - kept_total), 0.0)
            probs_b = soft_probs.astype(jnp.bfloat16)
            grad_prob = jnp.einsum(
                "qhd,khd->hqk", grad_blk, seq_values, preferred_element_type=jnp.float32
            )
            delta_row = jnp.sum(soft_probs * grad_prob, axis=-1, keepdims=True)
            grad_score = (soft_probs * (grad_prob - delta_row)).astype(jnp.bfloat16)
            grad_query = (
                jnp.einsum("hqk,khd->qhd", grad_score, seq_keys, preferred_element_type=jnp.float32)
                * factor
            )
            key_acc = (
                key_acc
                + jnp.einsum(
                    "hqk,qhd->khd", grad_score, query_blk, preferred_element_type=jnp.float32
                )
                * factor
            )
            value_acc = value_acc + jnp.einsum(
                "hqk,qhd->khd", probs_b, grad_blk, preferred_element_type=jnp.float32
            )
            return ((key_acc, value_acc), grad_query)

        zeros_kv = jnp.zeros(seq_keys.shape, jnp.float32)
        (grad_key, grad_value), grad_query = lax.scan(
            block_step, (zeros_kv, zeros_kv), jnp.arange(blocks)
        )
        return (grad_query.reshape(length, local_heads, HEAD), grad_key, grad_value)

    grad_query, grad_key, grad_value = lax.map(attend_back, jnp.arange(seq_count))
    grad_proj = (
        jnp.stack(
            [
                rotate_back(grad_query, cosine, sine),
                rotate_back(grad_key, cosine, sine),
                grad_value,
            ],
            axis=2,
        )
        .astype(jnp.bfloat16)
        .reshape(row_count, 3 * local_width)
    )
    grad_w_qkv = jnp.dot(h_attn.T, grad_proj, preferred_element_type=jnp.float32).reshape(
        model_width, 3, local_width
    )
    grad_h_attn = (
        lax.psum(
            jnp.dot(grad_proj, w_qkv_flat.T, preferred_element_type=jnp.float32).astype(
                jnp.bfloat16
            ),
            "mp",
        )
        .astype(jnp.float32)
        .reshape(seq_count, length, model_width)
    )
    grad_shift_one = jnp.sum(grad_h_attn, axis=1)
    grad_scale_one = jnp.sum(grad_h_attn * normed_one * gain_one, axis=1)
    grad_gain_one = jnp.sum(grad_h_attn * normed_one * (1.0 + scale_one), axis=(0, 1))
    grad_tokens = grad_mid + norm_back(
        grad_h_attn * gain_one * (1.0 + scale_one), normed_one, inv_one
    )
    grad_mod = jnp.stack(
        [
            grad_shift_one,
            grad_scale_one,
            grad_gate_one,
            grad_shift_two,
            grad_scale_two,
            grad_gate_two,
        ],
        axis=1,
    )
    grad_mod_b = grad_mod.reshape(seq_count, 6 * model_width).astype(jnp.bfloat16)
    share_cols = model_width // lax.axis_size("mp")
    owned = (jnp.arange(model_width, dtype=jnp.int32) // share_cols == mp_index)[None, :]
    head_rows = jnp.concatenate(
        [grad_gain_one[None], grad_gain_two[None], grad_down_bias[None], jnp.sum(grad_mod, axis=0)],
        axis=0,
    )
    per_device = hidden_local // model_width
    bias_rows = lax.dynamic_update_slice_in_dim(
        jnp.zeros((vec_master.shape[0] - 9, model_width), jnp.float32),
        grad_up_bias.reshape(per_device, model_width),
        mp_index * per_device,
        0,
    )
    grad_vec = lax.psum(
        jnp.concatenate([jnp.where(owned, head_rows, 0.0), bias_rows], axis=0), ("dp", "mp")
    )
    grad_w_ada = jnp.dot(cond_b.T, grad_mod_b, preferred_element_type=jnp.float32)
    sum_qkv, sum_proj, sum_up, sum_down, sum_ada = (
        lax.psum_scatter(grad_w_qkv, "dp", scatter_dimension=0, tiled=True),
        lax.psum_scatter(grad_w_proj, "dp", scatter_dimension=1, tiled=True),
        lax.psum_scatter(grad_w_up, "dp", scatter_dimension=0, tiled=True),
        lax.psum_scatter(grad_w_down, "dp", scatter_dimension=1, tiled=True),
        lax.psum_scatter(grad_w_ada, "dp", scatter_dimension=0, tiled=True),
    )
    qkv_up = adamw(qkv_master, qkv_first, qkv_second, sum_qkv, DECAY, RATE)
    proj_up = adamw(proj_master, proj_first, proj_second, sum_proj, DECAY, RATE)
    up_up = adamw(up_master, up_first, up_second, sum_up, DECAY, RATE)
    down_up = adamw(down_master, down_first, down_second, sum_down, DECAY, RATE)
    ada_up = adamw(ada_master, ada_first, ada_second, sum_ada, DECAY, RATE)
    vec_up = adamw(vec_master, vec_first, vec_second, grad_vec, 0.0, RATE_VEC)
    return (
        block_out,
        grad_tokens,
        qkv_up[0],
        qkv_up[1],
        qkv_up[2],
        proj_up[0],
        proj_up[1],
        proj_up[2],
        up_up[0],
        up_up[1],
        up_up[2],
        down_up[0],
        down_up[1],
        down_up[2],
        ada_up[0],
        ada_up[1],
        ada_up[2],
        vec_up[0],
        vec_up[1],
        vec_up[2],
    )


LEN_FAST = 1024
WIDTH = 768
COPIES = 400
VMEM_BYTES = 66 * 2**20
NT = (((1,), (1,)), ((), ()))
NN = (((1,), (0,)), ((), ()))
TN = (((0,), (0,)), ((), ()))
F32 = jnp.float32
BF16 = jnp.bfloat16
MESH = pl.DeviceIdType.MESH
SHARD = 96
QUARTER = 1152
STACK = (2, 4, 2, SHARD, WIDTH)
CHUNKS = (
    (0, 0, 256), (0, 256, 256), (0, 512, 256), (1, 0, 384), (1, 384, 384), (2, 0, 384), (2, 384, 384),
)
GATHER = (
    ((0, 16, "xzy"), (16, 32, "zxy"), (48, 32, "zyx"), (80, 16, "yzx")),
    ((0, 48, "zxy"), (48, 16, "zyx"), (64, 16, "yxz"), (80, 16, "xyz")),
    ((0, 16, "yxz"), (16, 32, "zxy"), (48, 16, "zxy"), (64, 32, "yzx")),
)
REDUCE = (
    ((0, 32, "xyz"), (32, 16, "yzx"), (48, 48, "zyx")),
    ((0, 16, "xzy"), (16, 32, "yzx"), (48, 16, "xzy"), (64, 32, "yxz")),
    ((0, 32, "xyz"), (32, 32, "zxy"), (64, 16, "zyx"), (80, 16, "yzx")),
)
PLAN = (
    (("I", "g", 0, 1, 0), ("I", "g", 0, 2, 0), ("I", "g", 0, 0, 0), ("I", "g", 1, 1, 0), ("I", "g", 0, 3, 0), ("I", "g", 1, 0, 0), ("I", "g", 1, 3, 0), ("I", "g", 2, 0, 0), ("I", "g", 2, 3, 0), ("I", "g", 3, 2, 0), ("I", "g", 3, 3, 0), ("I", "g", 4, 2, 0), ("I", "g", 4, 3, 0)),
    (),
    (("W", "g", 0, 0, 0), ("W", "g", 0, 3, 0), ("I", "g", 5, 0, 0)),
    (("W", "g", 1, 0, 0), ("W", "g", 1, 3, 0), ("I", "g", 5, 3, 0), ("W", "g", 2, 0, 0), ("W", "g", 2, 3, 0), ("I", "g", 6, 0, 0), ("W", "g", 3, 2, 0), ("W", "g", 3, 3, 0), ("I", "g", 3, 2, 1), ("I", "g", 3, 3, 1), ("W", "g", 4, 2, 0), ("W", "g", 4, 3, 0), ("I", "g", 4, 2, 1), ("I", "g", 4, 3, 1), ("W", "g", 5, 0, 0), ("I", "g", 5, 0, 1), ("I", "g", 6, 3, 0), ("I", "g", 0, 0, 1)),
    (),
    (("W", "g", 5, 3, 0), ("W", "g", 6, 0, 0), ("I", "g", 6, 0, 1), ("W", "g", 3, 2, 1), ("W", "g", 3, 3, 1), ("W", "g", 0, 1, 0), ("W", "g", 4, 2, 1), ("I", "g", 0, 1, 3), ("I", "g", 1, 2, 0), ("W", "g", 4, 3, 1), ("W", "g", 0, 2, 0), ("I", "g", 0, 2, 3), ("I", "g", 0, 3, 1), ("W", "g", 5, 0, 1), ("W", "g", 6, 3, 0), ("W", "g", 1, 1, 0), ("I", "g", 1, 1, 3), ("I", "g", 1, 0, 1), ("W", "g", 6, 0, 1), ("W", "g", 0, 1, 3), ("I", "g", 0, 1, 1), ("W", "g", 0, 0, 1), ("I", "g", 0, 0, 4), ("I", "g", 2, 1, 0), ("W", "g", 0, 2, 3), ("I", "g", 0, 2, 1), ("W", "g", 1, 2, 0), ("I", "g", 1, 2, 3), ("I", "g", 2, 2, 0)),
    (),
    (("W", "g", 1, 1, 3), ("I", "g", 1, 1, 1), ("W", "g", 0, 3, 1), ("I", "g", 0, 3, 4), ("I", "g", 1, 3, 1), ("W", "g", 0, 0, 4), ("I", "g", 0, 0, 2), ("W", "g", 1, 0, 1), ("I", "g", 1, 0, 4), ("I", "g", 3, 0, 0), ("W", "g", 0, 1, 1), ("I", "g", 0, 1, 2), ("W", "g", 1, 2, 3), ("I", "g", 1, 2, 1), ("W", "g", 2, 1, 0), ("I", "g", 2, 1, 3), ("I", "g", 2, 0, 1), ("W", "g", 0, 2, 1), ("I", "g", 0, 2, 2)),
    (("W", "g", 0, 3, 4), ("W", "g", 2, 2, 0), ("I", "g", 2, 2, 3), ("I", "g", 0, 3, 2), ("I", "g", 3, 1, 0)),
    (("W", "g", 1, 0, 4), ("W", "g", 1, 1, 1), ("W", "g", 1, 3, 1), ("W", "g", 0, 0, 2), ("I", "g", 1, 1, 2), ("I", "g", 1, 3, 4), ("I", "g", 2, 3, 1), ("I", "g", 1, 0, 2)),
    (("W", "g", 2, 1, 3), ("I", "g", 2, 1, 1), ("W", "g", 2, 2, 3), ("W", "g", 3, 0, 0), ("I", "g", 3, 0, 3), ("I", "g", 2, 2, 1), ("I", "g", 4, 0, 0), ("W", "g", 0, 1, 2), ("W", "g", 0, 2, 2), ("W", "g", 1, 3, 4), ("W", "g", 2, 0, 1), ("I", "g", 2, 0, 4), ("I", "g", 1, 3, 2), ("I", "g", 4, 1, 0), ("W", "g", 3, 1, 0), ("I", "g", 3, 1, 3), ("I", "g", 5, 1, 0), ("W", "g", 1, 2, 1), ("I", "g", 1, 2, 2), ("W", "g", 0, 3, 2)),
    (("W", "g", 2, 3, 1), ("W", "g", 3, 0, 3), ("W", "g", 2, 1, 1), ("W", "g", 2, 0, 4), ("I", "g", 2, 1, 2), ("I", "g", 2, 3, 4), ("I", "g", 3, 0, 1), ("I", "g", 2, 0, 2), ("I", "g", 5, 2, 0)),
    (("W", "g", 3, 1, 3), ("W", "g", 1, 1, 2), ("W", "g", 4, 0, 0), ("W", "g", 1, 3, 2), ("W", "g", 4, 1, 0), ("I", "g", 4, 0, 3), ("I", "g", 4, 1, 3), ("I", "g", 3, 1, 1), ("I", "g", 3, 2, 2), ("I", "g", 3, 3, 2)),
    (("W", "g", 1, 0, 2), ("W", "g", 2, 3, 4), ("W", "g", 5, 1, 0), ("W", "g", 2, 2, 1), ("W", "g", 1, 2, 2), ("W", "g", 5, 2, 0), ("I", "g", 2, 2, 2), ("I", "g", 5, 1, 3), ("I", "g", 5, 2, 3), ("I", "g", 2, 3, 2), ("I", "g", 6, 1, 0), ("I", "g", 6, 2, 0)),
    (),
    (("W", "g", 4, 0, 3), ("W", "g", 4, 1, 3), ("I", "g", 4, 0, 1), ("I", "g", 4, 1, 1)),
    (("W", "g", 2, 1, 2), ("W", "g", 3, 0, 1), ("W", "g", 5, 1, 3), ("W", "g", 3, 2, 2), ("W", "g", 5, 2, 3), ("W", "g", 2, 0, 2), ("I", "g", 3, 2, 5), ("I", "g", 3, 0, 2), ("I", "g", 5, 1, 1), ("I", "g", 5, 2, 1), ("I", "g", 5, 3, 1)),
    (("W", "g", 3, 1, 1), ("W", "g", 2, 2, 2), ("W", "g", 4, 1, 1), ("I", "g", 3, 1, 2)),
    (("W", "g", 3, 3, 2), ("I", "g", 3, 3, 5), ("I", "g", 4, 2, 2), ("W", "g", 2, 3, 2), ("I", "g", 4, 1, 2)),
    (("W", "g", 3, 2, 5), ("W", "g", 6, 1, 0), ("W", "g", 6, 2, 0), ("I", "g", 6, 1, 3), ("I", "g", 6, 2, 3), ("I", "g", 4, 3, 2), ("I", "g", 6, 3, 1)),
    (("W", "g", 3, 3, 5), ("W", "g", 4, 0, 1), ("I", "g", 4, 0, 2)),
    (("W", "g", 5, 3, 1), ("W", "g", 6, 1, 3), ("W", "g", 6, 2, 3), ("W", "g", 5, 1, 1), ("W", "g", 3, 0, 2), ("I", "g", 5, 3, 4), ("I", "g", 5, 1, 2), ("I", "g", 6, 1, 1), ("I", "g", 6, 2, 1), ("I", "g", 5, 0, 2)),
    (("W", "g", 5, 2, 1), ("I", "g", 5, 2, 2)),
    (("W", "g", 4, 2, 2), ("I", "g", 4, 2, 5), ("I", "g", 6, 0, 2)),
    (),
    (),
    (("W", "g", 3, 1, 2),),
    (),
    (),
    (),
    (("W", "g", 5, 3, 4), ("I", "g", 5, 3, 2)),
    (),
    (("W", "g", 4, 1, 2), ("W", "g", 4, 3, 2), ("W", "g", 4, 2, 5), ("I", "g", 4, 3, 5)),
    (("W", "g", 4, 0, 2), ("W", "g", 6, 1, 1), ("W", "g", 6, 3, 1), ("W", "g", 6, 2, 1), ("I", "g", 6, 3, 4), ("I", "g", 6, 1, 2), ("I", "g", 6, 2, 2)),
    (),
    (("I", "r", 5, 0, 0), ("I", "r", 5, 1, 0), ("I", "r", 5, 2, 0), ("I", "r", 5, 3, 0)),
    (("W", "g", 4, 3, 5),),
    (("W", "g", 5, 0, 2), ("W", "g", 5, 1, 2), ("W", "g", 6, 3, 4), ("I", "g", 5, 0, 5), ("I", "g", 6, 3, 2)),
    (("W", "g", 5, 3, 2), ("W", "g", 5, 2, 2)),
    (("W", "g", 6, 0, 2), ("I", "g", 6, 0, 5)),
    (("I", "r", 6, 0, 0), ("I", "r", 6, 1, 0), ("I", "r", 6, 2, 0), ("I", "r", 6, 3, 0)),
    (("W", "g", 5, 0, 5),),
    (("W", "r", 5, 0, 0), ("W", "g", 6, 1, 2)),
    (("W", "g", 6, 0, 5), ("W", "g", 6, 2, 2)),
    (("I", "r", 3, 0, 0), ("I", "r", 3, 2, 0)),
    (("W", "r", 5, 1, 0), ("I", "r", 5, 1, 3), ("W", "g", 6, 3, 2)),
    (("W", "r", 5, 3, 0), ("I", "r", 5, 0, 1)),
    (("W", "r", 5, 2, 0), ("W", "r", 6, 3, 0), ("I", "r", 5, 2, 3), ("I", "r", 3, 1, 0)),
    (("I", "r", 4, 0, 0),),
    (("W", "r", 6, 0, 0), ("W", "r", 5, 1, 3), ("I", "r", 5, 1, 1), ("I", "r", 5, 3, 1), ("I", "r", 6, 0, 1), ("I", "r", 6, 3, 1), ("I", "r", 3, 3, 0), ("I", "r", 4, 1, 0), ("I", "r", 4, 2, 0), ("I", "r", 4, 3, 0)),
    (("W", "r", 3, 0, 0), ("W", "r", 5, 0, 1), ("W", "r", 5, 2, 3), ("I", "r", 5, 0, 2), ("I", "r", 5, 2, 1), ("I", "r", 3, 0, 1)),
    (("W", "r", 3, 2, 0), ("W", "r", 6, 1, 0), ("I", "r", 6, 1, 3), ("I", "r", 3, 2, 1)),
    (),
    (),
    (),
    (("I", "b", 0, 0, 0),),
    (),
    (),
    (("W", "r", 4, 0, 0), ("W", "r", 3, 1, 0), ("I", "r", 3, 1, 1), ("I", "r", 4, 0, 1)),
    (("I", "b", 1, 0, 0),),
    (),
    (),
    (("W", "r", 5, 1, 1), ("W", "r", 6, 2, 0), ("I", "r", 6, 2, 3), ("I", "r", 5, 1, 2)),
    (("I", "b", 2, 0, 0),),
    (),
    (),
    (("W", "r", 6, 0, 1), ("W", "r", 5, 3, 1), ("W", "r", 4, 2, 0), ("I", "r", 5, 3, 4), ("I", "r", 6, 0, 2), ("I", "r", 4, 2, 1)),
    (("W", "r", 6, 1, 3), ("I", "r", 6, 1, 1), ("I", "b", 3, 0, 0)),
    (("W", "r", 6, 3, 1), ("W", "r", 5, 0, 2), ("I", "r", 5, 0, 5), ("I", "r", 6, 3, 4)),
    (("W", "r", 6, 2, 3), ("W", "r", 5, 3, 4), ("W", "r", 3, 3, 0), ("W", "r", 3, 0, 1), ("W", "b", 0, 0, 0), ("I", "r", 3, 0, 4), ("I", "r", 5, 3, 2), ("I", "r", 6, 2, 1), ("I", "r", 3, 3, 1)),
    (("W", "r", 3, 2, 1), ("W", "r", 5, 0, 5), ("I", "r", 3, 2, 4)),
    (("W", "r", 6, 3, 4), ("W", "r", 3, 0, 4), ("I", "r", 3, 0, 2)),
    (("W", "r", 4, 1, 0), ("W", "b", 1, 0, 0), ("W", "r", 3, 1, 1), ("W", "r", 3, 2, 4), ("I", "r", 3, 1, 4), ("I", "r", 6, 3, 2), ("I", "r", 3, 2, 2), ("I", "r", 4, 1, 1)),
    (("W", "r", 4, 0, 1), ("I", "r", 4, 0, 4)),
    (("I", "r", 0, 1, 0), ("I", "r", 0, 2, 0)),
    (("W", "r", 6, 0, 2), ("W", "r", 4, 3, 0), ("W", "r", 5, 2, 1), ("W", "b", 2, 0, 0), ("I", "r", 6, 0, 5), ("I", "r", 5, 2, 2)),
    (("W", "r", 5, 1, 2), ("W", "r", 4, 2, 1), ("W", "r", 3, 1, 4), ("W", "r", 6, 2, 1), ("W", "r", 6, 1, 1), ("W", "r", 3, 0, 2), ("W", "r", 4, 0, 4), ("W", "r", 3, 2, 2), ("I", "r", 4, 2, 4), ("I", "r", 6, 1, 2), ("I", "r", 6, 2, 2), ("I", "r", 4, 0, 2)),
    (("W", "r", 0, 1, 0), ("W", "r", 6, 0, 5), ("W", "r", 4, 1, 1), ("I", "r", 4, 1, 4), ("I", "r", 0, 1, 1)),
    (("W", "r", 6, 1, 2), ("W", "r", 4, 2, 4), ("W", "r", 4, 0, 2), ("W", "b", 3, 0, 0), ("I", "r", 3, 1, 2), ("I", "r", 4, 2, 2), ("I", "r", 4, 3, 1)),
    (("W", "r", 5, 3, 2),),
    (("I", "r", 1, 1, 0), ("I", "r", 1, 2, 0)),
    (("W", "r", 4, 1, 4), ("W", "r", 3, 3, 1), ("W", "r", 6, 3, 2), ("W", "r", 4, 2, 2), ("W", "r", 5, 2, 2), ("W", "r", 6, 2, 2), ("I", "r", 3, 3, 2), ("I", "r", 4, 1, 2), ("I", "r", 0, 0, 0), ("I", "r", 1, 0, 0)),
    (("W", "r", 3, 1, 2), ("W", "r", 0, 2, 0), ("I", "r", 0, 2, 3)),
    (("W", "r", 0, 1, 1), ("W", "r", 1, 1, 0), ("W", "r", 4, 3, 1), ("W", "r", 4, 1, 2), ("I", "r", 0, 1, 4), ("I", "r", 4, 3, 2), ("I", "r", 1, 1, 1)),
    (),
    (("W", "r", 0, 0, 0), ("I", "r", 0, 0, 1)),
    (("I", "r", 2, 0, 0), ("I", "r", 2, 1, 0), ("I", "r", 2, 2, 0)),
    (("W", "r", 0, 2, 3), ("W", "r", 0, 1, 4), ("W", "r", 1, 2, 0), ("W", "r", 1, 0, 0), ("I", "r", 1, 2, 3), ("I", "r", 0, 1, 2), ("I", "r", 0, 2, 1), ("I", "r", 1, 0, 1)),
    (),
    (("W", "r", 3, 3, 2), ("I", "r", 3, 3, 5)),
    (("I", "t", 0, 0, 0),),
    (),
    (("W", "r", 0, 0, 1), ("W", "r", 4, 3, 2), ("I", "r", 4, 3, 5), ("I", "r", 0, 0, 2)),
    (("I", "t", 1, 0, 0),),
    (),
    (("W", "r", 2, 0, 0), ("W", "r", 2, 1, 0), ("W", "r", 0, 1, 2), ("W", "r", 1, 1, 1), ("I", "r", 1, 1, 4), ("I", "r", 2, 0, 1), ("I", "r", 2, 1, 1)),
    (("W", "r", 0, 2, 1), ("I", "t", 2, 0, 0), ("I", "r", 0, 2, 2)),
    (),
    (("W", "r", 1, 0, 1), ("I", "r", 1, 0, 2)),
    (("I", "t", 3, 0, 0),),
    (("W", "r", 1, 2, 3), ("I", "r", 1, 2, 1)),
    (("W", "r", 3, 3, 5), ("W", "r", 4, 3, 5), ("W", "r", 1, 1, 4), ("I", "r", 1, 1, 2), ("W", "r", 2, 0, 1), ("I", "r", 2, 0, 2), ("W", "t", 0, 0, 0), ("W", "r", 1, 2, 1), ("W", "r", 2, 2, 0), ("I", "r", 2, 2, 3), ("I", "r", 1, 2, 2), ("W", "r", 0, 0, 2), ("I", "r", 0, 0, 5), ("W", "r", 2, 1, 1), ("I", "r", 2, 1, 4), ("W", "t", 1, 0, 0), ("W", "r", 1, 0, 2), ("I", "r", 1, 0, 5)),
    (("W", "r", 2, 0, 2), ("I", "r", 2, 0, 5), ("W", "r", 2, 2, 3), ("I", "r", 2, 2, 1), ("W", "r", 0, 0, 5), ("W", "r", 2, 1, 4), ("I", "r", 2, 1, 2), ("W", "t", 2, 0, 0), ("W", "r", 1, 0, 5)),
    (("W", "r", 0, 2, 2), ("W", "r", 2, 0, 5), ("W", "r", 2, 2, 1), ("I", "r", 2, 2, 2), ("W", "t", 3, 0, 0), ("W", "r", 1, 1, 2), ("W", "r", 1, 2, 2), ("W", "r", 2, 1, 2), ("W", "r", 2, 2, 2)),
    (),
)


def inbox_shapes():
    shapes = {}
    for chunk, (tensor, _, width) in enumerate(CHUNKS):
        for piece, (_, height, order) in enumerate(REDUCE[tensor]):
            for phase, axis in enumerate(order):
                extent = [
                    {"x": 2, "z": 4, "y": 2}[other] for other in "xzy" if other in order[phase + 1:]
                ]
                slots = (4,) if axis == "z" else (1,)
                shapes[chunk, piece, phase] = slots + tuple(extent) + (height, width)
    return shapes


INBOX = inbox_shapes()


def mm(left, right, dims):
    return lax.dot_general(left, right, dims, preferred_element_type=F32)


def norm_tile(values):
    centred = values - jnp.mean(values, axis=1, keepdims=True)
    inv = lax.rsqrt(jnp.mean(centred * centred, axis=1, keepdims=True) + EPS_NORM)
    return centred * inv, inv


def rows(index, size):
    return pl.ds(pl.multiple_of(index * size, size), size)


def lower_lanes(shape):
    return lax.broadcasted_iota(jnp.int32, shape, 1) < 64


def interleave(first, second):
    lower = lower_lanes(first.shape)
    left = jnp.where(lower, first, pltpu.roll(second, 64, 1))
    right = jnp.where(lower, pltpu.roll(first, 64, 1), second)
    return left, right


def step_kernel(
    time_ref, doc_ref, tokens, cotangent, qkv_m, proj_m, up_m, down_m, ada_m, vec, freq, theta,
    grads_out, stats_out, block_out, grad_out,
    wt, ada, modq, mod, wqk, wv, wp, tok, cot, h1, q, k, v, o, lse, cosine, sine, same, other, kt, vt,
    attn_own, attn_in, dh2_in, mlp_in,
    x1, h2, act, slope, dm, do, dzv, bo, bo_in, gt_in, g1, g2, st, dup, dup_acc, grads, acc, ka, va,
    local_sem, send_sem, recv_sem, *inbox_refs,
):
    inbox = dict(zip(INBOX, inbox_refs))
    dp = lax.axis_index("dp")
    mp = lax.axis_index("mp")
    z, y, x, core = dp // 2, dp % 2, mp // 2, mp % 2
    own = {"x": x, "y": y, "z": z}

    def device(zz, yy, xx, cc):
        return (zz * 2 + yy, xx * 2 + cc)

    to_core = device(z, y, x, 1 - core)
    to_x = device(z, y, 1 - x, core)
    to_diag = device(z, y, 1 - x, 1 - core)
    to_y = device(z, 1 - y, x, core)
    z_next = [lax.rem(z + hop, 4) for hop in (1, 2, 3)]
    outer, inner = (z == 0) | (z == 3), (z == 1) | (z == 2)
    z_beside, z_other, z_across = z + 1 - 2 * (z % 2), lax.rem(z + 2, 4), 3 - z
    to_beside, to_other, to_across = [device(at, y, x, core) for at in (z_beside, z_other, z_across)]
    to_z = [device(place, y, x, core) for place in z_next]
    peers = {"x": (1 - x, to_x), "y": (1 - y, to_y)}
    counter = {"send": 0, "receive": 0}
    sent = []
    sent_inner = []
    sent_outer = []
    done = []

    def slots(side, count=1):
        counter[side] += count
        assert counter[side] <= COPIES
        return counter[side] - count

    def copy_of(src, dst, target, landing, starts=True):
        number = slots("send") if starts else 0
        return pltpu.make_async_remote_copy(
            src_ref=src, dst_ref=dst, send_sem=send_sem.at[number], recv_sem=recv_sem.at[landing],
            device_id=target, device_id_type=MESH,
        )

    def send(src, dst, target, landing=None):
        copy = copy_of(src, dst, target, slots("receive") if landing is None else landing)
        copy.start()
        sent.append(copy)
        return copy

    def arrive(copies):
        for copy in copies:
            copy.wait_recv()

    def flush(copies):
        for copy in copies:
            copy.wait_send()
            done.append(id(copy))

    barrier = pltpu.get_barrier_semaphore()
    partners = [to_core, to_x, to_diag, to_y] + to_z
    for partner in partners:
        pl.semaphore_signal(barrier, inc=1, device_id=partner, device_id_type=MESH)

    load_tok = pltpu.make_async_copy(tokens.at[x], tok, local_sem.at[0])
    load_cot = pltpu.make_async_copy(cotangent.at[x], cot, local_sem.at[1])
    load_tok.start()
    load_cot.start()

    ada[z, y] = ada_m[:, pl.ds(pl.multiple_of(mp * QUARTER, 128), QUARTER)].astype(BF16)
    proj_t = jnp.transpose(proj_m[...])
    wt[0, x, z, y] = jnp.concatenate(
        [
            part[:, 64 * head:64 * head + 64]
            for head in range(3) for part in (qkv_m[0], qkv_m[1], qkv_m[2], proj_t)
        ],
        axis=1,
    ).astype(BF16)
    wt[1, x, z, y] = up_m[...].astype(BF16)
    wt[2, x, z, y] = down_m[...].astype(BF16)

    pl.semaphore_wait(barrier, len(partners))

    def view(ref, fixed, height, columns):
        index = [fixed.get(axis, slice(None)) for axis in "xzy"]
        return ref.at[(*index, height, columns)]

    flying = {}
    sources = [wt.at[1], g1, g2]

    def gather(chunk, piece, phase):
        tensor, start, width = CHUNKS[chunk]
        first_row, height, order = GATHER[tensor][piece]
        axis = order[phase]
        fixed = {name: own[name] for name in order[phase:]}

        def block(at):
            return view(
                wt.at[tensor], {**fixed, axis: at}, pl.ds(first_row, height), pl.ds(start, width)
            )

        mine = block(own[axis])
        if axis != "z":
            return [send(mine, mine, peers[axis][1])]
        beside, other = send(mine, mine, to_beside), send(mine, mine, to_other)
        landing = slots("receive")
        across = copy_of(mine, mine, to_across, landing)
        passed = block(z_other)
        onward = copy_of(passed, passed, to_beside, landing)
        pl.when(inner)(across.start)
        sent_inner.extend((across, onward))
        return [beside, other, across, onward]

    def reduce(chunk, piece, phase):
        tensor, start, width = CHUNKS[chunk]
        first_row, height, order = REDUCE[tensor][piece]
        axis = order[phase]
        fixed = {name: own[name] for name in order[:phase]}
        landing = inbox[chunk, piece, phase]

        def block(at):
            return view(
                sources[tensor], {**fixed, axis: at}, pl.ds(first_row, height), pl.ds(start, width)
            )

        if axis != "z":
            at, target = peers[axis]
            return [send(block(at), landing.at[0], target)]
        beside = send(block(z_beside), landing.at[0], to_beside)
        number = slots("receive", 3)
        at = jnp.where(outer, z_other, z_across)
        kind = jnp.where(outer, 0, 1)
        direct = send(block(at), landing.at[1 + kind], device(at, y, x, core), number + kind)
        given = copy_of(block(z_across), landing.at[3], to_beside, number + 2)
        pl.when(outer)(given.start)
        sent_outer.append(given)
        total = copy_of(block(z_other), landing.at[1], to_other, number)
        sent_inner.append(total)
        waits = [
            copy_of(block(z_other), landing.at[1 + slot], to_other, number + slot, False) for slot in (0, 1)
        ]
        return [beside, waits[0], waits[1], given, total]

    def take(kind, chunk, piece, phase):
        tensor, start, width = CHUNKS[chunk]
        first_row, height, order = (GATHER if kind == "g" else REDUCE)[tensor][piece]
        axis = order[phase % 3]
        copies = flying[kind, chunk, piece, phase % 3]
        if kind == "g":
            if axis != "z":
                arrive(copies)
            elif phase < 3:
                arrive(copies[:2])
                pl.when(inner)(copies[3].start)
            else:
                arrive(copies[2:3])
            return
        landing = inbox[chunk, piece, phase % 3]
        source = sources[tensor]

        def place(at):
            fixed = {**{name: own[name] for name in order[:phase % 3]}, axis: at}
            index = [fixed.get(name, slice(None)) for name in "xzy"]
            return (*index, pl.ds(first_row, height), pl.ds(start, width))

        target = place(own[axis])
        if axis != "z":
            arrive(copies)
            total = source[target].astype(F32) + landing[0].astype(F32)
        elif phase < 3:
            arrive(copies[:1])

            @pl.when(inner)
            def _():
                arrive(copies[1:4])
                target = place(z_other)
                source[target] = (source[target].astype(F32) + landing[3].astype(F32)).astype(BF16)
                copies[4].start()

            return
        else:

            @pl.when(outer)
            def _():
                arrive(copies[1:2])

            total = source[target].astype(F32) + landing[0].astype(F32) + landing[1].astype(F32)
            across = landing[jnp.where(inner, 2, 0)].astype(F32)
            total = total + across * jnp.where(inner, 1.0, 0.0)
        if phase % 3 == 2:
            grads[tensor, pl.ds(first_row, height), pl.ds(start, width)] = total
        else:
            source[target] = total.astype(BF16)

    def cross(ref, landing, part):
        piece = pl.ds(pl.multiple_of(part * 256 + core * 128, 128), 128)
        return [send(ref.at[piece, :], landing.at[piece, :], to_x)]

    def share(landing, part):
        piece = landing.at[pl.ds(pl.multiple_of(part * 256 + core * 128, 128), 128), :]
        shared.append(send(piece, piece, to_core))

    shared = []
    outputs = {"b": (bo, bo_in), "t": (slope.at[0], gt_in)}
    position = [0]

    def serve():
        for action, kind, chunk, piece, phase in PLAN[position[0]]:
            if action == "I":
                if phase < 3:
                    begin = {"g": gather, "r": reduce}.get(kind)
                    flying[kind, chunk, piece, phase] = (
                        begin(chunk, piece, phase) if begin else cross(*outputs[kind], chunk)
                    )
            elif kind in "gr":
                take(kind, chunk, piece, phase)
            else:
                arrive(flying[kind, chunk, piece, phase])
                share(outputs[kind][1], chunk)
        position[0] += 1

    own_ada = ada.at[z, y]
    ada_one = [send(own_ada, own_ada, target) for target in to_z]
    serve()

    row_id = lax.broadcasted_iota(jnp.int32, (16, 128), 0)
    lane_id = lax.broadcasted_iota(jnp.int32, (16, 128), 1)
    steps = jnp.where(row_id == 0, time_ref[0], time_ref[1]).astype(F32)
    angles = steps * freq[0:1, :]
    cond = jnp.where(lane_id < 64, jnp.cos(angles), jnp.sin(angles)).astype(BF16)

    ends = []
    total = 0
    for number in range(4):
        total = total + doc_ref[x, number]
        ends.append(total)
    serve()

    def tables(index):
        block = rows(index, 128)
        token_id = lax.broadcasted_iota(jnp.int32, (128, 128), 0) + index * 128
        lanes = lax.broadcasted_iota(jnp.int32, (128, 128), 1)
        document = sum((token_id >= end).astype(jnp.int32) for end in ends)
        place = lax.rem(lanes, 64)
        same[block, :] = jnp.where(place == document, 1.0, 0.0).astype(BF16)
        apart = jnp.where((place < 4) & (place != document), NEG_BIG, 0.0)
        other[block, :] = jnp.where((place >= 4) & (place < 7), 1.0, apart).astype(BF16)
        begin = jnp.zeros((128, 128), jnp.int32)
        for end in ends[:3]:
            begin = jnp.where(token_id >= end, end, begin)
        turned = (token_id - begin).astype(F32) * theta[0:1, :]
        cosine[block, :] = jnp.cos(turned)
        turned_sine = jnp.sin(turned)
        sine[block, :] = jnp.where(lax.rem(lanes, 64) < 32, -turned_sine, turned_sine)

    pl.loop(0, 8)(tables)
    serve()
    serve()
    arrive(ada_one)
    own_ada = ada.at[:, y]
    ada_two = [send(own_ada, own_ada, to_y)]
    serve()
    serve()
    arrive(ada_two)
    modq[mp] = mm(cond, ada[...].reshape(COND, QUARTER), NN)[0:8]
    own_mod = modq.at[mp]
    mod_copies = [send(own_mod, own_mod, target) for target in (to_core, to_x, to_diag)]
    serve()
    serve()
    arrive(mod_copies)
    own_row = pl.ds(x, 1)
    half_width = WIDTH // 2
    mod[0:1, :] = modq[0, own_row, 0:WIDTH] + vec[3:4, :]
    mod[1:2, :] = (
        jnp.concatenate([modq[0, own_row, WIDTH:QUARTER], modq[1, own_row, 0:half_width]], axis=1)
        + vec[4:5, :]
    )
    mod[2:3, :] = modq[1, own_row, half_width:QUARTER] + vec[5:6, :]
    mod[3:4, :] = modq[2, own_row, 0:WIDTH] + vec[6:7, :]
    mod[4:5, :] = (
        jnp.concatenate([modq[2, own_row, WIDTH:QUARTER], modq[3, own_row, 0:half_width]], axis=1)
        + vec[7:8, :]
    )
    mod[5:6, :] = modq[3, own_row, half_width:QUARTER] + vec[8:9, :]

    load_tok.wait()
    load_cot.wait()

    for part in range(2):

        @pl.loop(part * 2, part * 2 + 2)
        def _(index):
            block = rows(index, 256)
            normed, _ = norm_tile(tok[block, :].astype(F32))
            h1[block, :] = (normed * (vec[0:1, :] * (1.0 + mod[1:2, :])) + mod[0:1, :]).astype(BF16)
            dm[block, :] = (cot[block, :].astype(F32) * mod[5:6, :]).astype(BF16)

        serve()

    def rotate(tile, block):
        lanes = lax.broadcasted_iota(jnp.int32, tile.shape, 1)
        swapped = jnp.where(
            lax.rem(lanes, 64) < 32, pltpu.roll(tile, 96, 1), pltpu.roll(tile, 32, 1)
        )
        return tile * cosine[block, :] + swapped * sine[block, :]

    def rotate_transposed(tile, block):
        lanes = lax.broadcasted_iota(jnp.int32, tile.shape, 1)
        turned = tile * sine[block, :]
        swapped = jnp.where(
            lax.rem(lanes, 64) < 32, pltpu.roll(turned, 96, 1), pltpu.roll(turned, 32, 1)
        )
        return tile * cosine[block, :] + swapped

    def project(pair):
        start = 256 * pair
        tiles = [
            [
                wt[0, side, :, :, :, start + 128 * part:start + 128 * part + 128].reshape(WIDTH, 128)
                for part in (0, 1)
            ]
            for side in (0, 1)
        ]
        cols = slice(pair * 128, pair * 128 + 128)
        both = slice(pair * 256, pair * 256 + 256)
        left, right = interleave(tiles[0][0], tiles[1][0])
        wqk[:, both] = jnp.concatenate([left, right], axis=1)
        wv[:, cols], wp[:, cols] = interleave(tiles[0][1], tiles[1][1])

        @pl.loop(0, LEN_FAST // 256)
        def _(index):
            block = rows(index, 256)
            full = mm(h1[block, :], wqk[:, both], NN)
            turned = rotate(full[:, 0:128], block).astype(BF16)
            q[block, cols] = (turned.astype(F32) * 0.125).astype(BF16)
            k[block, cols] = rotate(full[:, 128:256], block).astype(BF16)
            v[block, cols] = mm(h1[block, :], wv[:, cols], NN).astype(BF16)

    def own_half(shape, head):
        lower = lower_lanes(shape)
        return lower if head == 0 else ~lower

    def keep_head(tile, head):
        return jnp.where(own_half(tile.shape, head), tile, jnp.zeros_like(tile))

    def head_tiles(pair):
        cols = slice(pair * 128, pair * 128 + 128)
        for head in range(2):
            mine = own_half((LEN_FAST, 128), head)
            kt[head] = jnp.where(mine, k[:, cols], other[...])
            vt[head] = jnp.where(mine, v[:, cols], jnp.ones((LEN_FAST, 128), BF16))

    def beside(tile, values):
        place = lax.rem(lax.broadcasted_iota(jnp.int32, tile.shape, 1), 64)
        for number in range(3):
            term = values.astype(BF16)
            values = values - term.astype(F32)
            tile = jnp.where(place == 4 + number, term, tile)
        return tile

    def attend(pair, part):
        cols = slice(pair * 128, pair * 128 + 128)
        block = slice(512 * part, 512 * part + 512)
        if part == 0:
            head_tiles(pair)
        mixed = []
        for head in range(2):
            mine = own_half((512, 128), head)
            scores = mm(jnp.where(mine, q[block, cols], same[block, :]), kt[head], NT)
            top = jnp.max(scores, axis=1, keepdims=True)
            total = mm(jnp.exp(scores - top).astype(BF16), vt[head], NN)
            mixed.append(total * (1.0 / pltpu.roll(total, 64, 1)))
            number = 2 * pair + head
            beyond = 64 - 64 * head
            lse[block, number:number + 1] = top + jnp.log(total[:, beyond:beyond + 1])
        o[block, cols] = jnp.where(lower_lanes((512, 128)), mixed[0], mixed[1]).astype(BF16)

    for pair in range(3):
        serve()
        project(pair)
        serve()
        attend(pair, 0)
        serve()
        attend(pair, 1)
        serve()

    def swap(own_ref, incoming, make):
        copies = []
        for index in range(4):
            block = slice(index * 256, index * 256 + 256)
            own_ref[block, :] = make(block).astype(BF16)
            piece = pl.ds(index * 256, 256)
            copies.append(send(own_ref.at[piece, :], incoming.at[piece, :], to_core))
        return copies

    attn_copies = swap(attn_own, attn_in, lambda block: mm(o[block, :], wp[...], NT))
    serve()

    for part in range(4):
        serve()
        attn_copies[part].wait_recv()

        @pl.loop(part, part + 1)
        def _(index):
            block = rows(index, 256)
            attn = attn_own[block, :].astype(F32) + attn_in[block, :].astype(F32)
            middle = tok[block, :].astype(F32) + mod[2:3, :] * attn
            x1[block, :] = middle
            normed, _ = norm_tile(middle)
            h2[block, :] = (normed * (vec[1:2, :] * (1.0 + mod[4:5, :])) + mod[3:4, :]).astype(BF16)

        serve()

    def raise_hidden(half):
        cols = slice(384 * half, 384 * half + 384)
        for side in range(2):

            @pl.loop(0, LEN_FAST // 512)
            def _(index):
                block = rows(index, 512)
                bias = vec[pl.ds(9 + 2 * side + core, 1), cols]
                u = mm(h2[block, :], wt[1, side, :, :, :, cols].reshape(WIDTH, 384), NN) + bias
                square = u * u
                bent = jnp.tanh(u * (0.7978845608028654 + 0.03567740813636141 * square))
                half_u = 0.5 * u
                act[side, block, cols] = (half_u + half_u * bent).astype(BF16)
                rising = half_u * (0.7978845608028654 + 0.10703222440908423 * square)
                slope[side, block, cols] = (
                    0.5 + 0.5 * bent + (1.0 - bent * bent) * rising
                ).astype(BF16)

            serve()

        for side in range(2):
            grad = mm(dm[...], act[side, :, cols], TN).astype(BF16)
            g2[side, :, :, :, cols] = grad.reshape(4, 2, SHARD, 384)

    for half in range(2):
        serve()
        raise_hidden(half)
        serve()
        serve()

    def lower_hidden(half):
        cols = slice(384 * half, 384 * half + 384)
        for side in range(2):

            @pl.loop(0, LEN_FAST // 512)
            def _(index):
                block = rows(index, 512)
                back = mm(dm[block, :], wt[2, side, :, :, :, cols].reshape(WIDTH, 384), NN)
                grad = (back * slope[side, block, cols].astype(F32)).astype(BF16)
                slope[side, block, cols] = grad
                dup_acc[side, :, cols] = dup_acc[side, :, cols] + jnp.sum(
                    grad.astype(F32).reshape(64, 8, 384), axis=0
                )

        serve()
        for side in range(2):
            grad = mm(h2[...], slope[side, :, cols], TN).astype(BF16)
            g1[side, :, :, :, cols] = grad.reshape(4, 2, SHARD, 384)

    dup_acc[...] = jnp.zeros_like(dup_acc)
    for half in range(2):
        serve()
        lower_hidden(half)
        serve()
        serve()

    def back_two(block):
        return mm(slope[0, block, :], wt[1, 0].reshape(WIDTH, WIDTH), NT) + mm(
            slope[1, block, :], wt[1, 1].reshape(WIDTH, WIDTH), NT
        )

    dh2_own, mlp_own = slope.at[0], act.at[0]
    dh2_copies = swap(dh2_own, dh2_in, back_two)
    serve()

    def forward_two(block):
        return mm(act[0, block, :], wt[2, 0].reshape(WIDTH, WIDTH), NT) + mm(
            act[1, block, :], wt[2, 1].reshape(WIDTH, WIDTH), NT
        )

    mlp_copies = swap(mlp_own, mlp_in, forward_two)
    serve()

    dup[0] = jnp.zeros((8, WIDTH), F32)
    for side in range(2):
        dup[0, side:side + 1, :] = jnp.sum(dup_acc[side], axis=0, keepdims=True)
    dup_copy = send(dup.at[0], dup.at[1], to_core)
    serve()

    acc[...] = jnp.zeros_like(acc)

    def add_row(row, values):
        count = values.shape[0]
        acc[row] = acc[row] + jnp.sum(values.reshape(count // 8, 8, WIDTH), axis=0)

    for part in range(4):
        serve()
        dh2_copies[part].wait_recv()
        serve()
        mlp_copies[part].wait_recv()

        @pl.loop(part * 2, part * 2 + 2)
        def _(index):
            block = rows(index, 128)
            middle = x1[block, :]
            seen = cot[block, :].astype(F32)
            mlp = mlp_own[block, :].astype(F32) + mlp_in[block, :].astype(F32) + vec[2:3, :]
            bo[block, :] = (middle + mod[5:6, :] * mlp).astype(BF16)
            add_row(3, seen * mlp)
            add_row(4, seen)
            back = dh2_own[block, :].astype(F32) + dh2_in[block, :].astype(F32)
            normed, inv = norm_tile(middle)
            add_row(0, back)
            add_row(1, back * normed)
            scaled = back * (vec[1:2, :] * (1.0 + mod[4:5, :]))
            grad = seen + inv * (
                scaled - jnp.mean(scaled, axis=1, keepdims=True)
                - normed * jnp.mean(scaled * normed, axis=1, keepdims=True)
            )
            x1[block, :] = grad
            attn = attn_own[block, :].astype(F32) + attn_in[block, :].astype(F32)
            add_row(2, grad * attn)
            dm[block, :] = (grad * mod[2:3, :]).astype(BF16)

        serve()
        serve()

    bo_store = pltpu.make_async_copy(bo, block_out.at[x], local_sem.at[0])
    bo_store.start()

    @pl.loop(0, LEN_FAST // 256)
    def _(index):
        block = rows(index, 256)
        do[block, :] = mm(dm[block, :], wp[...], NN).astype(BF16)

    for key, copies in flying.items():
        if key[:2] in (("g", 3), ("g", 4)):
            flush([copy for copy in copies if any(copy is other for other in sent)])
            inner_copies = [copy for copy in copies if any(copy is other for other in sent_inner)]
            done.extend(id(copy) for copy in inner_copies)

            @pl.when(inner)
            def _():
                for copy in inner_copies:
                    copy.wait_send()

    g0 = sources[0]
    dzqk = h2

    def attend_back(pair, index):
        cols = slice(pair * 128, pair * 128 + 128)
        both = 256 * pair
        if index == 0:
            head_tiles(pair)
        begin, end = max(0, index - 2) * 256, min(4, index + 3) * 256
        keys = slice(begin, end)
        block = slice(256 * index, 256 * index + 256)
        query = q[block, cols]
        back = do[block, cols]
        product = back.astype(F32) * o[block, cols].astype(F32)
        grad_q = []
        for head in range(2):
            number = 2 * pair + head
            mine = own_half(query.shape, head)
            queries = jnp.where(mine, query, beside(same[block, :], -lse[block, number:number + 1]))
            probs = jnp.exp(mm(queries, kt[head, keys, :], NT))
            delta = jnp.sum(keep_head(product, head), axis=1, keepdims=True)
            backs = jnp.where(mine, back, beside(jnp.zeros_like(back), -delta))
            grad_s = (probs * mm(backs, vt[head, keys, :], NT)).astype(BF16)
            grad_q.append(mm(grad_s, k[keys, cols], NN))
            ka[keys, :] += mm(grad_s, keep_head(query, head), TN)
            va[keys, :] += mm(probs.astype(BF16), keep_head(back, head), TN)
        full = jnp.where(lower_lanes(grad_q[0].shape), grad_q[0], grad_q[1]) * 0.125
        dzqk[block, both:both + 128] = rotate_transposed(full, block).astype(BF16)

    grad_p = mm(dm[...], o[...], TN).astype(BF16)
    for pair in range(3):
        g0[0, :, :, :, 256 * pair + 128:256 * pair + 256] = grad_p[
            :, 128 * pair:128 * pair + 128
        ].reshape(4, 2, SHARD, 128)

    def head_grads(pair):
        cols = slice(pair * 128, pair * 128 + 128)
        start = 256 * pair
        dzqk[:, start + 128:start + 256] = rotate_transposed(ka[...], pl.ds(0, LEN_FAST)).astype(BF16)
        dzv[:, cols] = va[...].astype(BF16)
        grad_qk = mm(h1[...], dzqk[:, start:start + 256], TN).astype(BF16)
        grad_v = mm(h1[...], dzv[:, cols], TN).astype(BF16)
        held = g0[0, :, :, :, start + 128:start + 256].reshape(WIDTH, 128)
        for number, (first, second) in enumerate(
            ((grad_qk[:, 0:128], grad_qk[:, 128:256]), (grad_v, held))
        ):
            sides = interleave(first, second)
            place = start + 128 * number
            for side in range(2):
                g0[side, :, :, :, place:place + 128] = sides[side].reshape(4, 2, SHARD, 128)

    def clear():
        ka[...] = jnp.zeros_like(ka)
        va[...] = jnp.zeros_like(va)

    serve()
    for pair in range(3):
        clear()
        for index in range(4):
            attend_back(pair, index)
            serve()
        head_grads(pair)
        serve()
        serve()

    def back_one(block):
        return mm(dzqk[block, :], wqk[...], NT) + mm(dzv[block, :], wv[...], NT)

    flush(dh2_copies)
    flush(mlp_copies)
    gt = slope.at[0]
    dh1_copies = swap(act.at[0], act.at[1], back_one)
    serve()
    for part in range(4):
        serve()
        dh1_copies[part].wait_recv()

        @pl.loop(part * 2, part * 2 + 2)
        def _(index):
            block = rows(index, 128)
            back = act[0, block, :].astype(F32) + act[1, block, :].astype(F32)
            normed, inv = norm_tile(tok[block, :].astype(F32))
            add_row(5, back)
            add_row(6, back * normed)
            scaled = back * (vec[0:1, :] * (1.0 + mod[1:2, :]))
            gt[block, :] = (
                x1[block, :] + inv * (
                    scaled - jnp.mean(scaled, axis=1, keepdims=True)
                    - normed * jnp.mean(scaled * normed, axis=1, keepdims=True)
                )
            ).astype(BF16)

        serve()
        serve()

    gt_store = pltpu.make_async_copy(gt, grad_out.at[x], local_sem.at[1])
    gt_store.start()

    sums = [jnp.sum(acc[row], axis=0, keepdims=True) for row in range(7)]
    shift2, prod2, gate1, gate2, seen, shift1, prod1 = sums
    dup_copy.wait_recv()
    first_rows = jnp.where(core == 0, dup[0], dup[1])
    second_rows = jnp.where(core == 0, dup[1], dup[0])
    cond_row = jnp.where(x == 0, cond[0:1, :].astype(F32), cond[1:2, :].astype(F32))
    st[x, z, y] = jnp.concatenate(
        [
            shift1, prod1 * vec[0:1, :], gate1, shift2, prod2 * vec[1:2, :], gate2,
            prod1 * (1.0 + mod[1:2, :]), prod2 * (1.0 + mod[4:5, :]), seen * mod[5:6, :],
            jnp.concatenate([cond_row, jnp.zeros((1, WIDTH - 128), F32)], axis=1),
            first_rows[0:1, :], second_rows[0:1, :], first_rows[1:2, :], second_rows[1:2, :],
            jnp.zeros((2, WIDTH), F32),
        ],
        axis=0,
    ).astype(BF16)
    half_cols = pl.ds(pl.multiple_of(core * 384, 128), 384)
    own_stats = st.at[x, z, y, :, half_cols]
    stats_one = [send(own_stats, own_stats, target) for target in to_z]
    serve()
    serve()
    arrive(stats_one)
    own_stats = st.at[x, :, y, :, half_cols]
    stats_two = [send(own_stats, own_stats, to_y)]
    serve()
    arrive(stats_two)
    own_stats = st.at[x, :, :, :, half_cols]
    stats_three = [send(own_stats, own_stats, to_x)]
    serve()
    grads_store = pltpu.make_async_copy(grads, grads_out, local_sem.at[2])
    grads_store.start()
    arrive(shared)
    bo_rest = pltpu.make_async_copy(bo_in, block_out.at[1 - x], local_sem.at[4])
    gt_rest = pltpu.make_async_copy(gt_in, grad_out.at[1 - x], local_sem.at[5])
    bo_rest.start()
    gt_rest.start()
    serve()
    arrive(stats_three)
    own_stats = st.at[:, :, :, :, half_cols]
    arrive([send(own_stats, own_stats, to_core)])
    stats_store = pltpu.make_async_copy(st, stats_out, local_sem.at[3])
    stats_store.start()
    assert position[0] == len(PLAN)
    for copy in sent:
        if id(copy) not in done:
            copy.wait_send()

    @pl.when(inner)
    def _():
        for copy in sent_inner:
            if id(copy) not in done:
                copy.wait_send()

    @pl.when(outer)
    def _():
        for copy in sent_outer:
            copy.wait_send()

    for store in (bo_store, gt_store, grads_store, stats_store, bo_rest, gt_rest):
        store.wait()


def update_kernel(
    grads, stats, blocks_in, gt,
    qkv_m, qkv_f, qkv_s, proj_m, proj_f, proj_s, up_m, up_f, up_s, down_m, down_f, down_s,
    ada_m, ada_f, ada_s, vec_m, vec_f, vec_s,
    blocks_out, gt_out,
    qkv_mo, qkv_fo, qkv_so, proj_mo, proj_fo, proj_so, up_mo, up_fo, up_so, down_mo, down_fo, down_so,
    ada_mo, ada_fo, ada_so, vec_mo, vec_fo, vec_so,
    proj_grad, ada_grad,
):
    step = pl.program_id(0)
    blocks_out[...] = blocks_in[...]
    gt_out[...] = gt[...].astype(F32)

    def put(refs, outs, gradient, decay, rate, index=...):
        new = adamw(refs[0][index], refs[1][index], refs[2][index], gradient, decay, rate)
        for out, value in zip(outs, new):
            out[index] = value

    def columns(part):
        return jnp.concatenate(
            [grads[0, :, 256 * head + 64 * part:256 * head + 64 * part + 64] for head in range(3)], axis=1
        )

    for part in range(3):
        put((qkv_m, qkv_f, qkv_s), (qkv_mo, qkv_fo, qkv_so), columns(part), DECAY, RATE, part)
    put((up_m, up_f, up_s), (up_mo, up_fo, up_so), grads[1], DECAY, RATE)
    put((down_m, down_f, down_s), (down_mo, down_fo, down_so), grads[2], DECAY, RATE)
    proj_grad[rows(step, 24), :] = columns(3)

    every = stats[...].reshape(16, 16, WIDTH)
    cond = every[:, 9, 0:COND]
    half = WIDTH // 2
    spans = (
        ((0, 0, WIDTH), (1, 0, half)), ((1, half, WIDTH), (2, 0, WIDTH)),
        ((3, 0, WIDTH), (4, 0, half)), ((4, half, WIDTH), (5, 0, WIDTH)),
    )
    for number, span in enumerate(spans):

        @pl.when(step == number)
        def _():
            moved = jnp.concatenate([every[:, part, start:end] for part, start, end in span], axis=1)
            ada_grad[...] = mm(cond, moved, TN)

    own_rows = pl.ds(pl.multiple_of(lax.axis_index("dp") * 16, 16), 16)
    put((ada_m, ada_f, ada_s), (ada_mo, ada_fo, ada_so), ada_grad[own_rows, :], DECAY, RATE)

    @pl.when(step == 3)
    def _():
        put(
            (proj_m, proj_f, proj_s), (proj_mo, proj_fo, proj_so), jnp.transpose(proj_grad[...]),
            DECAY, RATE,
        )
        total = jnp.sum(every.astype(F32), axis=0)
        gradient = jnp.concatenate([total[6:9], total[0:6], total[10:14]], axis=0)
        put((vec_m, vec_f, vec_s), (vec_mo, vec_fo, vec_so), gradient, 0.0, RATE_VEC)


def fast_shards(
    tokens, cotangent, doc_lengths, time_steps,
    qkv_master, qkv_first, qkv_second, proj_master, proj_first, proj_second,
    up_master, up_first, up_second, down_master, down_first, down_second,
    ada_master, ada_first, ada_second, vec_master, vec_first, vec_second,
):
    freq = np.tile(np.exp(-np.log(10000.0) * np.arange(64) / 64).astype(np.float32), (8, 2))
    theta = np.tile(np.exp(-np.log(ROPE_BASE) * np.arange(32) * 2.0 / HEAD).astype(np.float32), (8, 4))
    vmem = pl.BlockSpec(memory_space=pltpu.VMEM)
    smem = pl.BlockSpec(memory_space=pltpu.SMEM)
    anywhere = pl.BlockSpec(memory_space=pl.ANY)
    tall = (LEN_FAST, WIDTH)
    third = (LEN_FAST, 384)
    buffers = [
        ((3,) + STACK, BF16),
        ((4, 2, 16, QUARTER), BF16),
        ((4, 8, QUARTER), F32),
        ((8, WIDTH), F32),
        ((WIDTH, WIDTH), BF16), ((WIDTH, 384), BF16), ((WIDTH, 384), BF16),
        (tall, BF16), (tall, BF16), (tall, BF16),
        (third, BF16), (third, BF16), (third, BF16), (third, BF16),
        ((LEN_FAST, 128), F32),
        ((LEN_FAST, 128), F32), ((LEN_FAST, 128), F32),
        ((LEN_FAST, 128), BF16), ((LEN_FAST, 128), BF16),
        ((2, LEN_FAST, 128), BF16), ((2, LEN_FAST, 128), BF16),
        (tall, BF16), (tall, BF16),
        (tall, BF16), (tall, BF16),
        (tall, F32),
        (tall, BF16),
        ((2,) + tall, BF16), ((2,) + tall, BF16),
        (tall, BF16),
        (third, BF16), (third, BF16),
        (tall, BF16), (tall, BF16), (tall, BF16),
        (STACK, BF16), (STACK, BF16),
        ((2, 4, 2, 16, WIDTH), BF16),
        ((2, 8, WIDTH), F32), ((2, 8, WIDTH), F32),
        ((3, SHARD, WIDTH), F32),
        ((8, 8, WIDTH), F32),
        ((LEN_FAST, 128), F32), ((LEN_FAST, 128), F32),
    ]
    turned_qkv = [jnp.transpose(a, (1, 0, 2)) for a in (qkv_master, qkv_first, qkv_second)]
    turned_down = [a.T for a in (down_master, down_first, down_second)]
    grads, stats, blocks, grad_tokens = pl.pallas_call(
        step_kernel,
        out_shape=[
            jax.ShapeDtypeStruct((3, SHARD, WIDTH), F32),
            jax.ShapeDtypeStruct((2, 4, 2, 16, WIDTH), BF16),
            jax.ShapeDtypeStruct((2,) + tall, BF16),
            jax.ShapeDtypeStruct((2,) + tall, BF16),
        ],
        in_specs=[smem, smem, anywhere, anywhere] + [vmem] * 8,
        out_specs=[anywhere] * 4,
        scratch_shapes=[pltpu.VMEM(shape, kind) for shape, kind in buffers]
        + [pltpu.SemaphoreType.DMA((6,))] + [pltpu.SemaphoreType.DMA((COPIES,))] * 2
        + [pltpu.VMEM(shape, BF16) for shape in INBOX.values()],
        compiler_params=pltpu.CompilerParams(
            collective_id=0, has_side_effects=True, vmem_limit_bytes=VMEM_BYTES
        ),
    )(time_steps, doc_lengths, tokens, cotangent, turned_qkv[0], proj_master, up_master,
      turned_down[0], ada_master, vec_master, freq, theta)
    states = [
        *turned_qkv, proj_master, proj_first, proj_second, up_master, up_first, up_second,
        *turned_down, ada_master, ada_first, ada_second, vec_master, vec_first, vec_second,
    ]

    def whole(a):
        return pl.BlockSpec(a.shape, lambda i: (0,) * a.ndim)

    strip = pl.BlockSpec((2, LEN_FAST // 4, WIDTH), lambda i: (0, i, 0))
    part_rows = SHARD // 4
    shared = {
        "qkv": pl.BlockSpec((3, part_rows, 192), lambda i: (0, i, 0)),
        "row": pl.BlockSpec((part_rows, WIDTH), lambda i: (i, 0)),
        "ada": pl.BlockSpec((16, QUARTER), lambda i: (0, i)),
    }
    state_specs = [
        spec
        for spec in (shared["qkv"], whole(proj_master), shared["row"], shared["row"], shared["ada"], whole(vec_master))
        for _ in range(3)
    ]
    new = pl.pallas_call(
        update_kernel,
        grid=(4,),
        out_shape=[jax.ShapeDtypeStruct((2,) + tall, BF16), jax.ShapeDtypeStruct((2,) + tall, F32)]
        + [jax.ShapeDtypeStruct(a.shape, F32) for a in states],
        in_specs=[pl.BlockSpec((3, part_rows, WIDTH), lambda i: (0, i, 0)), whole(stats), strip, strip]
        + state_specs,
        out_specs=[strip, strip] + state_specs,
        scratch_shapes=[pltpu.VMEM((SHARD, 192), F32), pltpu.VMEM((COND, QUARTER), F32)],
        compiler_params=pltpu.CompilerParams(vmem_limit_bytes=VMEM_BYTES),
    )(grads, stats, blocks, grad_tokens, *states)
    blocks, grad_tokens, *new = new
    new[0:3] = [jnp.transpose(a, (1, 0, 2)) for a in new[0:3]]
    new[9:12] = [a.T for a in new[9:12]]
    return (blocks, grad_tokens, *new)


def solution(mesh):
    placed = (
        P("dp", None, None),
        P("dp", None, None),
        P("dp", None),
        P("dp"),
        P("dp", None, "mp"),
        P("dp", None, "mp"),
        P("dp", None, "mp"),
        P("mp", "dp"),
        P("mp", "dp"),
        P("mp", "dp"),
        P("dp", "mp"),
        P("dp", "mp"),
        P("dp", "mp"),
        P("mp", "dp"),
        P("mp", "dp"),
        P("mp", "dp"),
        P("dp", None),
        P("dp", None),
        P("dp", None),
        P(),
        P(),
        P(),
    )
    fast = mesh.shape["dp"] == 8 and mesh.shape["mp"] == 4
    return jax.shard_map(
        fast_shards if fast else shards,
        mesh=mesh,
        in_specs=placed,
        out_specs=(
            P("dp", None, None),
            P("dp", None, None),
            P("dp", None, "mp"),
            P("dp", None, "mp"),
            P("dp", None, "mp"),
            P("mp", "dp"),
            P("mp", "dp"),
            P("mp", "dp"),
            P("dp", "mp"),
            P("dp", "mp"),
            P("dp", "mp"),
            P("mp", "dp"),
            P("mp", "dp"),
            P("mp", "dp"),
            P("dp", None),
            P("dp", None),
            P("dp", None),
            P(),
            P(),
            P(),
        ),
        check_vma=False,
    )
```

```python
from functools import partial
import math

import jax
import jax.numpy as jnp
import numpy as np
from jax import lax
from jax.experimental import pallas as pl
from jax.experimental.pallas import tpu as pltpu
from jax.sharding import PartitionSpec as P

HEAD = 64
COND = 128
STEP = 10


EPS_NORM = 1e-05
ROPE_BASE = 10000.0
RATE = 0.14
RATE_VEC = 0.4
BETA_ONE = 0.9
BETA_TWO = 0.999
EPS_ADAM = 1e-08
DECAY = 0.1
NEG_BIG = -1e30


def time_features(steps, width):
    half_size = width // 2
    freqs = jnp.exp(-jnp.log(10000.0) * jnp.arange(half_size, dtype=jnp.float32) / half_size)
    angles = steps.astype(jnp.float32)[:, None] * freqs[None, :]
    return jnp.concatenate([jnp.cos(angles), jnp.sin(angles)], axis=1)


def doc_layout(doc_lens, length):
    doc_ends = jnp.cumsum(doc_lens)
    places = jnp.arange(length, dtype=jnp.int32)
    passed = (places[:, None] >= doc_ends[None, :]).astype(jnp.int32)
    return (jnp.sum(passed, axis=1), places - jnp.sum(passed * doc_lens[None, :], axis=1))


def rotary_tables(positions, head_size):
    half_size = head_size // 2
    inverse = jnp.exp(
        -jnp.log(ROPE_BASE) * jnp.arange(half_size, dtype=jnp.float32) * 2.0 / head_size
    )
    angles = positions.astype(jnp.float32)[..., None] * inverse
    angles = jnp.concatenate([angles, angles], axis=-1)
    return (jnp.cos(angles), jnp.sin(angles))


def rotate_half(values):
    half_size = values.shape[-1] // 2
    return jnp.concatenate([-values[..., half_size:], values[..., :half_size]], axis=-1)


def rotate_apply(values, cosine, sine):
    return values * cosine + rotate_half(values) * sine


def rotate_back(gradient, cosine, sine):
    return gradient * cosine - rotate_half(gradient * sine)


def norm_rows(values):
    centred = values - jnp.mean(values, axis=-1, keepdims=True)
    inv_std = lax.rsqrt(jnp.mean(centred * centred, axis=-1, keepdims=True) + EPS_NORM)
    return (centred * inv_std, inv_std)


def norm_back(gradient, normed, inv_std):
    return inv_std * (
        gradient
        - jnp.mean(gradient, axis=-1, keepdims=True)
        - normed * jnp.mean(gradient * normed, axis=-1, keepdims=True)
    )


def adamw(master, moment_one, second, gradient, decay_rate, rate_now):
    first_new = BETA_ONE * moment_one + (1.0 - BETA_ONE) * gradient
    second_new = BETA_TWO * second + (1.0 - BETA_TWO) * gradient * gradient
    fix_one = 1.0 - BETA_ONE**STEP
    fix_two = 1.0 - BETA_TWO**STEP
    stepped = first_new / fix_one / (jnp.sqrt(second_new / fix_two) + EPS_ADAM)
    return (master - rate_now * (stepped + decay_rate * master), first_new, second_new)


def shards(
    tokens,
    cotangent,
    doc_lengths,
    time_steps,
    qkv_master,
    qkv_first,
    qkv_second,
    proj_master,
    proj_first,
    proj_second,
    up_master,
    up_first,
    up_second,
    down_master,
    down_first,
    down_second,
    ada_master,
    ada_first,
    ada_second,
    vec_master,
    vec_first,
    vec_second,
):
    w_qkv, w_proj, w_up, w_down, w_ada = (
        lax.all_gather(qkv_master.astype(jnp.bfloat16), "dp", axis=0, tiled=True),
        lax.all_gather(proj_master.astype(jnp.bfloat16), "dp", axis=1, tiled=True),
        lax.all_gather(up_master.astype(jnp.bfloat16), "dp", axis=0, tiled=True),
        lax.all_gather(down_master.astype(jnp.bfloat16), "dp", axis=1, tiled=True),
        lax.all_gather(ada_master.astype(jnp.bfloat16), "dp", axis=0, tiled=True),
    )
    seq_count, length, model_width = tokens.shape
    row_count = seq_count * length
    local_width = w_qkv.shape[2]
    local_heads = local_width // HEAD
    hidden_local = w_up.shape[1]
    mp_index = lax.axis_index("mp")
    block_rows = min(512, length)
    blocks = length // block_rows
    factor = 1.0 / math.sqrt(HEAD)
    cond_b = time_features(time_steps, COND).astype(jnp.bfloat16)
    modulate = (
        jnp.dot(cond_b, w_ada, preferred_element_type=jnp.float32) + vec_master[3:9].reshape(-1)
    ).reshape(seq_count, 6, model_width)
    shift_one = modulate[:, 0, None]
    scale_one = modulate[:, 1, None]
    gate_one = modulate[:, 2, None]
    shift_two = modulate[:, 3, None]
    scale_two = modulate[:, 4, None]
    gate_two = modulate[:, 5, None]
    gain_one = vec_master[0]
    gain_two = vec_master[1]
    down_bias = vec_master[2]
    up_bias = lax.dynamic_slice_in_dim(
        vec_master[9:].reshape(-1), mp_index * hidden_local, hidden_local
    )
    doc_ids, positions = jax.vmap(partial(doc_layout, length=length))(doc_lengths)
    cosine, sine = rotary_tables(positions, HEAD)
    cosine = cosine[:, :, None, :]
    sine = sine[:, :, None, :]
    x_in = tokens.astype(jnp.float32)
    normed_one, inv_one = norm_rows(x_in)
    h_attn = (
        (normed_one * gain_one * (1.0 + scale_one) + shift_one)
        .astype(jnp.bfloat16)
        .reshape(row_count, model_width)
    )
    w_qkv_flat = w_qkv.reshape(model_width, 3 * local_width)
    proj_qkv = jnp.dot(h_attn, w_qkv_flat, preferred_element_type=jnp.float32).reshape(
        seq_count, length, 3, local_heads, HEAD
    )
    queries = rotate_apply(proj_qkv[:, :, 0], cosine, sine).astype(jnp.bfloat16)
    keys_all = rotate_apply(proj_qkv[:, :, 1], cosine, sine).astype(jnp.bfloat16)
    values_all = proj_qkv[:, :, 2].astype(jnp.bfloat16)

    def attend(block_index):
        seq_no = block_index // blocks
        offset = block_index % blocks * block_rows
        query_blk = lax.dynamic_slice_in_dim(queries[seq_no], offset, block_rows, 0)
        doc_query = lax.dynamic_slice_in_dim(doc_ids[seq_no], offset, block_rows, 0)
        same_doc = doc_query[:, None] == doc_ids[seq_no][None, :]
        scores = (
            jnp.einsum(
                "qhd,khd->hqk", query_blk, keys_all[seq_no], preferred_element_type=jnp.float32
            )
            * factor
        )
        scores = jnp.where(same_doc[None], scores, NEG_BIG)
        row_max = jnp.max(scores, axis=-1, keepdims=True)
        expo = jnp.exp(scores - row_max)
        totals = jnp.sum(expo, axis=-1, keepdims=True)
        soft_probs = (expo / totals).astype(jnp.bfloat16)
        mixed = jnp.einsum(
            "hqk,khd->qhd", soft_probs, values_all[seq_no], preferred_element_type=jnp.float32
        )
        return (mixed.astype(jnp.bfloat16), (row_max + jnp.log(totals))[..., 0])

    mixed_blocks, log_totals = lax.map(attend, jnp.arange(seq_count * blocks))
    mixed_flat = mixed_blocks.reshape(row_count, local_width)
    attn_out = (
        lax.psum(
            jnp.dot(mixed_flat, w_proj, preferred_element_type=jnp.float32).astype(jnp.bfloat16),
            "mp",
        )
        .astype(jnp.float32)
        .reshape(seq_count, length, model_width)
    )
    x_mid = x_in + gate_one * attn_out
    normed_two, inv_two = norm_rows(x_mid)
    h_mlp = (
        (normed_two * gain_two * (1.0 + scale_two) + shift_two)
        .astype(jnp.bfloat16)
        .reshape(row_count, model_width)
    )
    up_pre = jnp.dot(h_mlp, w_up, preferred_element_type=jnp.float32) + up_bias
    act_b = jax.nn.gelu(up_pre, approximate=True).astype(jnp.bfloat16)
    mlp_out = (
        lax.psum(
            jnp.dot(act_b, w_down, preferred_element_type=jnp.float32).astype(jnp.bfloat16), "mp"
        )
        .astype(jnp.float32)
        .reshape(seq_count, length, model_width)
        + down_bias
    )
    block_out = (x_mid + gate_two * mlp_out).astype(jnp.bfloat16)
    grad_y = cotangent.astype(jnp.float32)
    grad_mlp = grad_y * gate_two
    grad_gate_two = jnp.sum(grad_y * mlp_out, axis=1)
    grad_down_bias = jnp.sum(grad_mlp, axis=(0, 1))
    grad_mlp_b = grad_mlp.reshape(row_count, model_width).astype(jnp.bfloat16)
    grad_w_down = jnp.dot(act_b.T, grad_mlp_b, preferred_element_type=jnp.float32)
    grad_act = jnp.dot(grad_mlp_b, w_down.T, preferred_element_type=jnp.float32)
    unused, gelu_pull = jax.vjp(partial(jax.nn.gelu, approximate=True), up_pre)
    grad_up_b = gelu_pull(grad_act)[0].astype(jnp.bfloat16)
    grad_up_bias = jnp.sum(grad_up_b, axis=0, dtype=jnp.float32)
    grad_w_up = jnp.dot(h_mlp.T, grad_up_b, preferred_element_type=jnp.float32)
    grad_h_mlp = (
        lax.psum(
            jnp.dot(grad_up_b, w_up.T, preferred_element_type=jnp.float32).astype(jnp.bfloat16),
            "mp",
        )
        .astype(jnp.float32)
        .reshape(seq_count, length, model_width)
    )
    grad_shift_two = jnp.sum(grad_h_mlp, axis=1)
    grad_scale_two = jnp.sum(grad_h_mlp * normed_two * gain_two, axis=1)
    grad_gain_two = jnp.sum(grad_h_mlp * normed_two * (1.0 + scale_two), axis=(0, 1))
    grad_mid = grad_y + norm_back(grad_h_mlp * gain_two * (1.0 + scale_two), normed_two, inv_two)
    grad_gate_one = jnp.sum(grad_mid * attn_out, axis=1)
    grad_attn_b = (grad_mid * gate_one).reshape(row_count, model_width).astype(jnp.bfloat16)
    grad_w_proj = jnp.dot(mixed_flat.T, grad_attn_b, preferred_element_type=jnp.float32)
    grad_mixed = (
        jnp.dot(grad_attn_b, w_proj.T, preferred_element_type=jnp.float32)
        .astype(jnp.bfloat16)
        .reshape(seq_count, length, local_heads, HEAD)
    )

    def attend_back(seq_no):
        seq_keys = keys_all[seq_no]
        seq_values = values_all[seq_no]
        seq_docs = doc_ids[seq_no]

        def block_step(carry, block_no):
            key_acc, value_acc = carry
            offset = block_no * block_rows
            query_blk = lax.dynamic_slice_in_dim(queries[seq_no], offset, block_rows, 0)
            grad_blk = lax.dynamic_slice_in_dim(grad_mixed[seq_no], offset, block_rows, 0)
            doc_query = lax.dynamic_slice_in_dim(seq_docs, offset, block_rows, 0)
            same_doc = doc_query[:, None] == seq_docs[None, :]
            scores = (
                jnp.einsum("qhd,khd->hqk", query_blk, seq_keys, preferred_element_type=jnp.float32)
                * factor
            )
            kept_total = log_totals[seq_no * blocks + block_no][..., None]
            soft_probs = jnp.where(same_doc[None], jnp.exp(scores - kept_total), 0.0)
            probs_b = soft_probs.astype(jnp.bfloat16)
            grad_prob = jnp.einsum(
                "qhd,khd->hqk", grad_blk, seq_values, preferred_element_type=jnp.float32
            )
            delta_row = jnp.sum(soft_probs * grad_prob, axis=-1, keepdims=True)
            grad_score = (soft_probs * (grad_prob - delta_row)).astype(jnp.bfloat16)
            grad_query = (
                jnp.einsum("hqk,khd->qhd", grad_score, seq_keys, preferred_element_type=jnp.float32)
                * factor
            )
            key_acc = (
                key_acc
                + jnp.einsum(
                    "hqk,qhd->khd", grad_score, query_blk, preferred_element_type=jnp.float32
                )
                * factor
            )
            value_acc = value_acc + jnp.einsum(
                "hqk,qhd->khd", probs_b, grad_blk, preferred_element_type=jnp.float32
            )
            return ((key_acc, value_acc), grad_query)

        zeros_kv = jnp.zeros(seq_keys.shape, jnp.float32)
        (grad_key, grad_value), grad_query = lax.scan(
            block_step, (zeros_kv, zeros_kv), jnp.arange(blocks)
        )
        return (grad_query.reshape(length, local_heads, HEAD), grad_key, grad_value)

    grad_query, grad_key, grad_value = lax.map(attend_back, jnp.arange(seq_count))
    grad_proj = (
        jnp.stack(
            [
                rotate_back(grad_query, cosine, sine),
                rotate_back(grad_key, cosine, sine),
                grad_value,
            ],
            axis=2,
        )
        .astype(jnp.bfloat16)
        .reshape(row_count, 3 * local_width)
    )
    grad_w_qkv = jnp.dot(h_attn.T, grad_proj, preferred_element_type=jnp.float32).reshape(
        model_width, 3, local_width
    )
    grad_h_attn = (
        lax.psum(
            jnp.dot(grad_proj, w_qkv_flat.T, preferred_element_type=jnp.float32).astype(
                jnp.bfloat16
            ),
            "mp",
        )
        .astype(jnp.float32)
        .reshape(seq_count, length, model_width)
    )
    grad_shift_one = jnp.sum(grad_h_attn, axis=1)
    grad_scale_one = jnp.sum(grad_h_attn * normed_one * gain_one, axis=1)
    grad_gain_one = jnp.sum(grad_h_attn * normed_one * (1.0 + scale_one), axis=(0, 1))
    grad_tokens = grad_mid + norm_back(
        grad_h_attn * gain_one * (1.0 + scale_one), normed_one, inv_one
    )
    grad_mod = jnp.stack(
        [
            grad_shift_one,
            grad_scale_one,
            grad_gate_one,
            grad_shift_two,
            grad_scale_two,
            grad_gate_two,
        ],
        axis=1,
    )
    grad_mod_b = grad_mod.reshape(seq_count, 6 * model_width).astype(jnp.bfloat16)
    share_cols = model_width // lax.axis_size("mp")
    owned = (jnp.arange(model_width, dtype=jnp.int32) // share_cols == mp_index)[None, :]
    head_rows = jnp.concatenate(
        [grad_gain_one[None], grad_gain_two[None], grad_down_bias[None], jnp.sum(grad_mod, axis=0)],
        axis=0,
    )
    per_device = hidden_local // model_width
    bias_rows = lax.dynamic_update_slice_in_dim(
        jnp.zeros((vec_master.shape[0] - 9, model_width), jnp.float32),
        grad_up_bias.reshape(per_device, model_width),
        mp_index * per_device,
        0,
    )
    grad_vec = lax.psum(
        jnp.concatenate([jnp.where(owned, head_rows, 0.0), bias_rows], axis=0), ("dp", "mp")
    )
    grad_w_ada = jnp.dot(cond_b.T, grad_mod_b, preferred_element_type=jnp.float32)
    sum_qkv, sum_proj, sum_up, sum_down, sum_ada = (
        lax.psum_scatter(grad_w_qkv, "dp", scatter_dimension=0, tiled=True),
        lax.psum_scatter(grad_w_proj, "dp", scatter_dimension=1, tiled=True),
        lax.psum_scatter(grad_w_up, "dp", scatter_dimension=0, tiled=True),
        lax.psum_scatter(grad_w_down, "dp", scatter_dimension=1, tiled=True),
        lax.psum_scatter(grad_w_ada, "dp", scatter_dimension=0, tiled=True),
    )
    qkv_up = adamw(qkv_master, qkv_first, qkv_second, sum_qkv, DECAY, RATE)
    proj_up = adamw(proj_master, proj_first, proj_second, sum_proj, DECAY, RATE)
    up_up = adamw(up_master, up_first, up_second, sum_up, DECAY, RATE)
    down_up = adamw(down_master, down_first, down_second, sum_down, DECAY, RATE)
    ada_up = adamw(ada_master, ada_first, ada_second, sum_ada, DECAY, RATE)
    vec_up = adamw(vec_master, vec_first, vec_second, grad_vec, 0.0, RATE_VEC)
    return (
        block_out,
        grad_tokens,
        qkv_up[0],
        qkv_up[1],
        qkv_up[2],
        proj_up[0],
        proj_up[1],
        proj_up[2],
        up_up[0],
        up_up[1],
        up_up[2],
        down_up[0],
        down_up[1],
        down_up[2],
        ada_up[0],
        ada_up[1],
        ada_up[2],
        vec_up[0],
        vec_up[1],
        vec_up[2],
    )


LEN_FAST = 1024
WIDTH = 768
COPIES = 400
VMEM_BYTES = 66 * 2**20
NT = (((1,), (1,)), ((), ()))
NN = (((1,), (0,)), ((), ()))
TN = (((0,), (0,)), ((), ()))
F32 = jnp.float32
BF16 = jnp.bfloat16
MESH = pl.DeviceIdType.MESH
SHARD = 96
QUARTER = 1152
STACK = (2, 4, 2, SHARD, WIDTH)
CHUNKS = (
    (0, 0, 256), (0, 256, 256), (0, 512, 256), (1, 0, 384), (1, 384, 384), (2, 0, 384), (2, 384, 384),
)
GATHER = (
    ((0, 16, "zxy"), (16, 32, "zyx"), (48, 16, "xyz"), (64, 32, "zxy")),
    ((0, 16, "zyx"), (16, 32, "zyx"), (48, 32, "zxy"), (80, 16, "zyx")),
    ((0, 32, "zxy"), (32, 16, "yxz"), (48, 32, "zyx"), (80, 16, "xyz")),
    ((0, 32, "zyx"), (32, 16, "yxz"), (48, 32, "zxy"), (80, 16, "zyx")),
    ((0, 16, "yxz"), (16, 16, "xzy"), (32, 16, "zyx"), (48, 48, "zxy")),
    ((0, 16, "zyx"), (16, 16, "zxy"), (32, 32, "zyx"), (64, 32, "xyz")),
    ((0, 32, "zxy"), (32, 32, "xyz"), (64, 16, "zyx"), (80, 16, "zyx")),
)
REDUCE = (
    ((0, 16, "zxy"), (16, 16, "xyz"), (32, 32, "zxy"), (64, 32, "yzx")),
    ((0, 16, "yxz"), (16, 16, "zyx"), (32, 48, "xyz"), (80, 16, "zyx")),
    ((0, 16, "zyx"), (16, 32, "yzx"), (48, 16, "yzx"), (64, 32, "xyz")),
    ((0, 32, "yzx"), (32, 32, "xyz"), (64, 16, "xyz"), (80, 16, "zyx")),
    ((0, 16, "xzy"), (16, 32, "yxz"), (48, 16, "yzx"), (64, 32, "zyx")),
    ((0, 16, "yxz"), (16, 48, "yzx"), (64, 16, "zyx"), (80, 16, "yzx")),
    ((0, 32, "zxy"), (32, 16, "yzx"), (48, 16, "xyz"), (64, 32, "yxz")),
)
PLAN = (
    (("I", "g", 0, 0, 0), ("I", "g", 0, 1, 0), ("I", "g", 0, 3, 0), ("I", "g", 0, 2, 0), ("I", "g", 1, 0, 0), ("I", "g", 2, 1, 0), ("I", "g", 2, 3, 0)),
    (("I", "g", 3, 1, 0), ("I", "g", 4, 0, 0), ("I", "g", 4, 1, 0), ("I", "g", 5, 3, 0), ("I", "g", 6, 1, 0)),
    (("W", "g", 0, 2, 0), ("W", "g", 2, 1, 0), ("W", "g", 2, 3, 0), ("I", "g", 0, 2, 1), ("I", "g", 2, 1, 1), ("I", "g", 2, 3, 1)),
    (("W", "g", 3, 1, 0), ("W", "g", 4, 1, 0), ("I", "g", 3, 1, 1), ("W", "g", 4, 0, 0), ("I", "g", 4, 0, 1), ("W", "g", 5, 3, 0), ("I", "g", 5, 3, 1), ("W", "g", 6, 1, 0), ("I", "g", 6, 1, 1), ("I", "g", 1, 1, 0)),
    (),
    (("W", "g", 0, 2, 1), ("W", "g", 2, 1, 1), ("W", "g", 2, 3, 1), ("W", "g", 0, 0, 0), ("I", "g", 0, 0, 3), ("I", "g", 1, 2, 0), ("W", "g", 3, 1, 1), ("W", "g", 4, 0, 1), ("W", "g", 0, 1, 0), ("I", "g", 0, 1, 3), ("I", "g", 1, 3, 0), ("W", "g", 5, 3, 1), ("W", "g", 0, 3, 0), ("I", "g", 0, 3, 3), ("I", "g", 2, 0, 0), ("W", "g", 6, 1, 1), ("W", "g", 0, 0, 3), ("I", "g", 0, 0, 1), ("W", "g", 1, 0, 0), ("I", "g", 1, 0, 3), ("I", "g", 2, 2, 0), ("W", "g", 1, 1, 0), ("I", "g", 1, 1, 3), ("I", "g", 0, 2, 2), ("W", "g", 0, 1, 3), ("I", "g", 0, 1, 1), ("W", "g", 1, 2, 0), ("I", "g", 1, 2, 3), ("I", "g", 3, 0, 0), ("W", "g", 0, 3, 3), ("I", "g", 0, 3, 1), ("W", "g", 1, 0, 3), ("W", "g", 1, 3, 0), ("I", "g", 1, 0, 1), ("I", "g", 1, 3, 3), ("I", "g", 3, 2, 0), ("W", "g", 0, 0, 1), ("I", "g", 0, 0, 2)),
    (),
    (("W", "g", 2, 0, 0), ("I", "g", 2, 0, 3), ("I", "g", 3, 3, 0), ("W", "g", 1, 1, 3), ("I", "g", 1, 1, 1), ("W", "g", 2, 2, 0), ("I", "g", 2, 2, 3), ("I", "g", 4, 2, 0), ("W", "g", 1, 2, 3), ("W", "g", 0, 1, 1), ("I", "g", 0, 1, 2), ("I", "g", 1, 2, 1), ("W", "g", 1, 3, 3), ("I", "g", 1, 3, 1), ("W", "g", 1, 0, 1), ("I", "g", 1, 0, 2), ("W", "g", 0, 3, 1), ("I", "g", 0, 3, 2), ("W", "g", 2, 0, 3), ("I", "g", 2, 0, 1), ("W", "g", 0, 2, 2), ("I", "g", 0, 2, 5), ("I", "g", 4, 3, 0)),
    (("W", "g", 0, 0, 2), ("W", "g", 2, 2, 3), ("I", "g", 2, 2, 1)),
    (("W", "g", 3, 0, 0), ("W", "g", 1, 1, 1), ("I", "g", 1, 1, 2), ("I", "g", 3, 0, 3), ("I", "g", 4, 1, 1)),
    (("W", "g", 1, 3, 1), ("W", "g", 3, 2, 0), ("I", "g", 3, 2, 3), ("I", "g", 2, 1, 2), ("W", "g", 0, 1, 2), ("I", "g", 1, 3, 2), ("W", "g", 0, 2, 5), ("W", "g", 3, 3, 0), ("I", "g", 3, 3, 3), ("I", "g", 2, 3, 2), ("W", "g", 4, 2, 0), ("W", "g", 1, 2, 1), ("I", "g", 1, 2, 2), ("I", "g", 4, 2, 3), ("I", "g", 5, 0, 0), ("W", "g", 0, 3, 2)),
    (("W", "g", 3, 0, 3), ("W", "g", 1, 0, 2), ("W", "g", 3, 2, 3), ("W", "g", 3, 3, 3), ("W", "g", 2, 2, 1), ("W", "g", 4, 3, 0), ("I", "g", 2, 2, 2), ("I", "g", 4, 3, 3), ("I", "g", 3, 0, 1), ("I", "g", 3, 2, 1), ("I", "g", 3, 3, 1), ("I", "g", 5, 1, 0)),
    (("W", "g", 4, 2, 3), ("W", "g", 2, 0, 1), ("W", "g", 4, 1, 1), ("I", "g", 2, 0, 2), ("I", "g", 4, 1, 4), ("I", "g", 5, 2, 0)),
    (("W", "g", 1, 2, 2), ("W", "g", 1, 1, 2), ("W", "g", 2, 1, 2), ("W", "g", 4, 3, 3), ("I", "g", 2, 1, 5), ("I", "g", 4, 2, 1), ("I", "g", 4, 3, 1), ("I", "g", 3, 1, 2)),
    (("W", "g", 1, 3, 2),),
    (("W", "g", 3, 0, 1), ("W", "g", 4, 1, 4), ("W", "g", 2, 3, 2), ("W", "g", 3, 3, 1), ("W", "g", 5, 0, 0), ("I", "g", 5, 0, 3), ("I", "g", 2, 3, 5), ("I", "g", 3, 0, 2), ("I", "g", 3, 3, 2), ("I", "g", 6, 0, 0), ("I", "g", 6, 2, 0), ("I", "g", 4, 1, 2)),
    (("W", "g", 5, 1, 0), ("W", "g", 2, 1, 5), ("W", "g", 2, 2, 2), ("W", "g", 5, 2, 0), ("W", "g", 2, 0, 2), ("I", "g", 5, 1, 3), ("I", "g", 5, 2, 3), ("I", "g", 6, 3, 0), ("I", "g", 4, 0, 2)),
    (("W", "g", 5, 0, 3), ("W", "g", 3, 2, 1), ("W", "g", 4, 2, 1), ("W", "g", 2, 3, 5), ("I", "g", 3, 2, 2), ("I", "g", 4, 2, 2), ("I", "g", 5, 0, 1)),
    (),
    (("W", "g", 5, 1, 3), ("W", "g", 3, 1, 2), ("W", "g", 4, 1, 2), ("W", "g", 5, 2, 3), ("I", "g", 3, 1, 5), ("I", "g", 5, 1, 1), ("I", "g", 5, 2, 1), ("I", "g", 5, 3, 2)),
    (("W", "g", 4, 3, 1), ("W", "g", 6, 0, 0), ("W", "g", 6, 2, 0), ("W", "g", 6, 3, 0), ("I", "g", 6, 0, 3), ("I", "g", 6, 2, 3), ("I", "g", 6, 3, 3), ("I", "g", 4, 3, 2), ("I", "g", 6, 1, 2)),
    (("W", "g", 3, 1, 5),),
    (("W", "g", 3, 0, 2), ("W", "g", 3, 2, 2)),
    (("W", "g", 6, 0, 3), ("I", "g", 6, 0, 1), ("W", "g", 4, 0, 2), ("I", "g", 4, 0, 5), ("W", "g", 6, 2, 3), ("I", "g", 6, 2, 1), ("W", "g", 5, 0, 1), ("I", "g", 5, 0, 2), ("W", "g", 6, 3, 3), ("I", "g", 6, 3, 1)),
    (),
    (),
    (("W", "g", 3, 3, 2),),
    (),
    (),
    (),
    (("W", "g", 5, 2, 1), ("I", "g", 5, 2, 2)),
    (),
    (("W", "g", 4, 2, 2), ("W", "g", 4, 0, 5), ("W", "g", 5, 1, 1), ("I", "g", 5, 1, 2)),
    (("W", "g", 5, 3, 2), ("W", "g", 6, 0, 1), ("I", "g", 5, 3, 5)),
    (),
    (("I", "r", 5, 2, 0),),
    (("W", "g", 5, 0, 2), ("W", "g", 4, 3, 2), ("I", "g", 6, 0, 2)),
    (("W", "g", 6, 2, 1), ("I", "g", 6, 2, 2), ("I", "r", 5, 0, 0)),
    (("W", "g", 6, 3, 1), ("W", "g", 5, 3, 5), ("W", "g", 6, 1, 2), ("I", "g", 6, 1, 5), ("I", "g", 6, 3, 2), ("I", "r", 5, 1, 0)),
    (("W", "g", 5, 2, 2), ("W", "g", 5, 1, 2), ("I", "r", 5, 3, 0)),
    (("I", "r", 6, 0, 0), ("I", "r", 6, 2, 0)),
    (),
    (("W", "g", 6, 2, 2), ("W", "r", 5, 2, 0), ("I", "r", 5, 2, 3)),
    (("W", "g", 6, 3, 2), ("W", "g", 6, 0, 2), ("I", "r", 6, 1, 0)),
    (("I", "r", 3, 1, 0), ("I", "r", 3, 2, 0), ("I", "r", 3, 3, 0)),
    (("W", "g", 6, 1, 5),),
    (("W", "r", 6, 2, 0), ("W", "r", 5, 0, 0), ("W", "r", 5, 2, 3), ("I", "r", 5, 0, 1), ("I", "r", 5, 2, 1)),
    (),
    (("I", "r", 4, 0, 0), ("I", "r", 4, 3, 0)),
    (("W", "r", 6, 0, 0), ("I", "r", 6, 0, 3), ("I", "r", 4, 1, 0), ("I", "r", 4, 2, 0)),
    (("W", "r", 3, 1, 0), ("W", "r", 3, 3, 0), ("W", "r", 5, 1, 0), ("I", "r", 3, 3, 3), ("I", "r", 5, 1, 1), ("I", "r", 6, 3, 0)),
    (("W", "r", 3, 2, 0),),
    (),
    (),
    (("W", "r", 5, 0, 1), ("W", "r", 5, 3, 0), ("I", "r", 5, 3, 1), ("I", "r", 5, 0, 2), ("I", "r", 6, 2, 1)),
    (("I", "b", 0, 0, 0),),
    (),
    (),
    (),
    (("I", "b", 1, 0, 0),),
    (),
    (),
    (("W", "r", 6, 0, 3), ("W", "r", 4, 0, 0), ("W", "r", 6, 1, 0), ("I", "r", 6, 0, 1), ("I", "r", 3, 0, 0), ("I", "r", 3, 1, 1)),
    (("W", "r", 5, 2, 1), ("I", "r", 5, 2, 2), ("I", "b", 2, 0, 0)),
    (),
    (),
    (("W", "r", 3, 3, 3), ("W", "r", 4, 3, 0), ("I", "r", 4, 3, 3), ("I", "r", 4, 0, 1)),
    (("I", "b", 3, 0, 0),),
    (),
    (("W", "b", 0, 0, 0), ("W", "r", 4, 1, 0), ("I", "r", 4, 1, 1), ("I", "r", 3, 2, 1)),
    (("W", "r", 5, 1, 1), ("W", "r", 4, 2, 0), ("W", "r", 4, 3, 3), ("I", "r", 5, 1, 4), ("I", "r", 4, 2, 1), ("I", "r", 4, 3, 1), ("I", "r", 6, 1, 1)),
    (("W", "r", 5, 3, 1), ("W", "r", 5, 0, 2), ("W", "b", 1, 0, 0), ("I", "r", 5, 0, 5), ("I", "r", 5, 3, 4)),
    (("W", "r", 6, 0, 1), ("W", "r", 4, 0, 1), ("W", "r", 5, 2, 2), ("I", "r", 4, 0, 4)),
    (("W", "r", 6, 3, 0), ("W", "r", 4, 2, 1), ("W", "r", 6, 2, 1), ("W", "r", 5, 1, 4), ("I", "r", 4, 2, 4), ("I", "r", 5, 1, 2), ("I", "r", 6, 3, 1), ("I", "r", 6, 0, 2), ("I", "r", 6, 2, 2), ("I", "r", 3, 3, 1)),
    (("I", "r", 0, 0, 0), ("I", "r", 0, 1, 0), ("I", "r", 0, 2, 0)),
    (("W", "r", 5, 0, 5), ("W", "r", 6, 1, 1), ("W", "r", 5, 3, 4), ("W", "r", 4, 0, 4), ("W", "b", 2, 0, 0), ("I", "r", 6, 1, 4), ("I", "r", 5, 3, 2)),
    (("W", "r", 4, 2, 4), ("W", "r", 6, 2, 2), ("I", "r", 6, 2, 5), ("I", "r", 4, 2, 2)),
    (("W", "r", 3, 0, 0), ("W", "r", 6, 1, 4), ("I", "r", 0, 3, 0), ("I", "r", 6, 1, 2), ("I", "r", 3, 0, 1)),
    (("W", "r", 0, 0, 0), ("W", "b", 3, 0, 0), ("W", "r", 3, 1, 1), ("W", "r", 6, 2, 5), ("I", "r", 0, 0, 3), ("I", "r", 4, 0, 2), ("I", "r", 3, 1, 2)),
    (("W", "r", 3, 2, 1), ("W", "r", 4, 1, 1), ("W", "r", 4, 3, 1), ("I", "r", 4, 1, 2), ("I", "r", 4, 3, 2)),
    (("I", "r", 1, 0, 0), ("I", "r", 1, 2, 0)),
    (("W", "r", 6, 0, 2), ("W", "r", 5, 1, 2), ("W", "r", 3, 3, 1), ("W", "r", 0, 2, 0), ("W", "r", 0, 0, 3), ("I", "r", 0, 2, 3), ("I", "r", 1, 1, 0), ("I", "r", 0, 0, 1), ("I", "r", 3, 3, 2)),
    (("W", "r", 6, 3, 1), ("W", "r", 0, 3, 0)),
    (("W", "r", 4, 0, 2), ("W", "r", 0, 1, 0), ("W", "r", 3, 0, 1), ("W", "r", 5, 3, 2), ("W", "r", 4, 2, 2), ("W", "r", 6, 1, 2), ("W", "r", 4, 3, 2), ("W", "r", 1, 0, 0), ("I", "r", 3, 0, 4), ("I", "r", 1, 3, 0), ("I", "r", 1, 0, 1), ("I", "r", 0, 1, 1), ("I", "r", 0, 3, 1)),
    (("W", "r", 3, 1, 2), ("W", "r", 0, 2, 3), ("W", "r", 4, 1, 2), ("I", "r", 3, 1, 5), ("I", "r", 4, 1, 5), ("I", "r", 0, 2, 1), ("I", "r", 6, 3, 2)),
    (("W", "r", 0, 1, 1), ("W", "r", 1, 1, 0), ("I", "r", 1, 1, 3), ("I", "r", 0, 1, 2)),
    (("W", "r", 1, 2, 0), ("W", "r", 3, 0, 4), ("W", "r", 0, 0, 1), ("W", "r", 3, 3, 2), ("W", "r", 3, 1, 5), ("W", "r", 1, 0, 1), ("I", "r", 1, 2, 1), ("I", "r", 1, 0, 2), ("I", "r", 0, 0, 2), ("I", "r", 3, 0, 2)),
    (("I", "r", 2, 1, 0), ("I", "r", 2, 2, 0), ("I", "r", 2, 3, 0)),
    (),
    (("W", "r", 1, 3, 0), ("W", "r", 4, 1, 5), ("W", "r", 0, 2, 1), ("I", "r", 1, 3, 3), ("I", "r", 0, 2, 2)),
    (("W", "r", 1, 1, 3), ("I", "t", 0, 0, 0), ("I", "r", 1, 1, 1)),
    (),
    (("W", "r", 0, 3, 1), ("I", "r", 0, 3, 4), ("I", "r", 2, 0, 0)),
    (("I", "t", 1, 0, 0),),
    (),
    (("W", "r", 3, 0, 2), ("W", "r", 6, 3, 2), ("I", "r", 6, 3, 5), ("I", "r", 3, 2, 2)),
    (("W", "r", 0, 1, 2), ("I", "r", 0, 1, 5), ("I", "t", 2, 0, 0)),
    (),
    (("W", "r", 1, 2, 1), ("W", "r", 1, 0, 2), ("W", "r", 0, 0, 2), ("W", "r", 1, 3, 3), ("I", "r", 1, 0, 5), ("I", "r", 1, 3, 1), ("I", "r", 1, 2, 2)),
    (("I", "t", 3, 0, 0),),
    (("W", "r", 2, 3, 0), ("I", "r", 2, 3, 1)),
    (("W", "r", 0, 3, 4), ("I", "r", 0, 3, 2), ("W", "r", 2, 0, 0), ("W", "r", 6, 3, 5), ("I", "r", 2, 0, 3), ("W", "r", 0, 1, 5), ("W", "r", 2, 1, 0), ("I", "r", 2, 1, 1), ("W", "r", 3, 2, 2), ("I", "r", 3, 2, 5), ("W", "r", 1, 0, 5), ("W", "r", 2, 2, 0), ("I", "r", 2, 2, 1), ("W", "r", 0, 2, 2), ("W", "r", 1, 2, 2), ("I", "r", 1, 2, 5), ("W", "r", 1, 1, 1), ("I", "r", 1, 1, 2), ("W", "t", 0, 0, 0), ("W", "r", 1, 3, 1), ("I", "r", 1, 3, 2)),
    (("W", "r", 2, 0, 3), ("I", "r", 2, 0, 1), ("W", "r", 3, 2, 5), ("W", "r", 2, 3, 1), ("I", "r", 2, 3, 2), ("W", "r", 1, 2, 5), ("W", "r", 2, 1, 1), ("I", "r", 2, 1, 4), ("W", "r", 2, 2, 1), ("I", "r", 2, 2, 4)),
    (("W", "r", 2, 0, 1), ("I", "r", 2, 0, 2), ("W", "t", 1, 0, 0), ("W", "r", 2, 3, 2), ("I", "r", 2, 3, 5), ("W", "r", 2, 1, 4), ("I", "r", 2, 1, 2), ("W", "r", 2, 2, 4), ("I", "r", 2, 2, 2), ("W", "r", 2, 3, 5), ("W", "t", 2, 0, 0), ("W", "t", 3, 0, 0), ("W", "r", 0, 3, 2), ("W", "r", 1, 1, 2), ("W", "r", 1, 3, 2), ("W", "r", 2, 0, 2), ("W", "r", 2, 1, 2), ("W", "r", 2, 2, 2)),
    (),
)


def inbox_shapes():
    shapes = {}
    for chunk, (_, _, width) in enumerate(CHUNKS):
        for piece, (_, height, order) in enumerate(REDUCE[chunk]):
            for phase, axis in enumerate(order):
                extent = [
                    {"x": 2, "z": 4, "y": 2}[other] for other in "xzy" if other in order[phase + 1:]
                ]
                slots = (4,) if axis == "z" else (1,)
                shapes[chunk, piece, phase] = slots + tuple(extent) + (height, width)
    return shapes


INBOX = inbox_shapes()


def mm(left, right, dims):
    return lax.dot_general(left, right, dims, preferred_element_type=F32)


def norm_tile(values):
    centred = values - jnp.mean(values, axis=1, keepdims=True)
    inv = lax.rsqrt(jnp.mean(centred * centred, axis=1, keepdims=True) + EPS_NORM)
    return centred * inv, inv


def rows(index, size):
    return pl.ds(pl.multiple_of(index * size, size), size)


def lower_lanes(shape):
    return lax.broadcasted_iota(jnp.int32, shape, 1) < 64


def interleave(first, second):
    lower = lower_lanes(first.shape)
    left = jnp.where(lower, first, pltpu.roll(second, 64, 1))
    right = jnp.where(lower, pltpu.roll(first, 64, 1), second)
    return left, right


def step_kernel(
    time_ref, doc_ref, tokens, cotangent, qkv_h, proj_h, up_h, down_h, ada_h, vec_h, freq, theta,
    grads_out, stats_out, block_out, grad_out,
    wt, ada, modq, mod, wqk, wv, wp, tok, cot, h1, q, k, v, o, lse, cosine, sine, same, other, kt, vt,
    attn_own, attn_in, dh2_in, mlp_in,
    x1, h2, act, slope, dm, do, dzv, bo, bo_in, gt_in, g1, g2, st, dup, dup_acc, grads, acc, ka, va,
    qkv_m, proj_m, up_m, down_m, ada_m, vec, local_sem, send_sem, recv_sem, *inbox_refs,
):
    inbox = dict(zip(INBOX, inbox_refs))
    dp = lax.axis_index("dp")
    mp = lax.axis_index("mp")
    z, y, x, core = dp // 2, dp % 2, mp // 2, mp % 2
    own = {"x": x, "y": y, "z": z}

    def device(zz, yy, xx, cc):
        return (zz * 2 + yy, xx * 2 + cc)

    to_core = device(z, y, x, 1 - core)
    to_x = device(z, y, 1 - x, core)
    to_diag = device(z, y, 1 - x, 1 - core)
    to_y = device(z, 1 - y, x, core)
    z_next = [lax.rem(z + hop, 4) for hop in (1, 2, 3)]
    outer, inner = (z == 0) | (z == 3), (z == 1) | (z == 2)
    z_beside, z_other, z_across = z + 1 - 2 * (z % 2), lax.rem(z + 2, 4), 3 - z
    to_beside, to_other, to_across = [device(at, y, x, core) for at in (z_beside, z_other, z_across)]
    to_z = [device(place, y, x, core) for place in z_next]
    peers = {"x": (1 - x, to_x), "y": (1 - y, to_y)}
    counter = {"send": 0, "receive": 0}
    sent = []
    sent_inner = []
    sent_outer = []
    done = []

    def slots(side, count=1):
        counter[side] += count
        assert counter[side] <= COPIES
        return counter[side] - count

    def copy_of(src, dst, target, landing, starts=True):
        number = slots("send") if starts else 0
        return pltpu.make_async_remote_copy(
            src_ref=src, dst_ref=dst, send_sem=send_sem.at[number], recv_sem=recv_sem.at[landing],
            device_id=target, device_id_type=MESH,
        )

    def send(src, dst, target, landing=None):
        copy = copy_of(src, dst, target, slots("receive") if landing is None else landing)
        copy.start()
        sent.append(copy)
        return copy

    def arrive(copies):
        for copy in copies:
            copy.wait_recv()

    def flush(copies):
        for copy in copies:
            copy.wait_send()
            done.append(id(copy))

    barrier = pltpu.get_barrier_semaphore()
    partners = [to_core, to_x, to_diag, to_y] + to_z
    for partner in partners:
        pl.semaphore_signal(barrier, inc=1, device_id=partner, device_id_type=MESH)

    loads = [
        pltpu.make_async_copy(src, dst, local_sem.at[number])
        for number, (src, dst) in enumerate((
            (ada_h.at[:, pl.ds(pl.multiple_of(mp * QUARTER, 128), QUARTER)], ada_m), (qkv_h, qkv_m),
            (proj_h, proj_m), (up_h, up_m), (down_h, down_m), (vec_h, vec), (tokens.at[x], tok),
            (cotangent.at[x], cot),
        ))
    ]
    for load in loads:
        load.start()

    loads[0].wait()
    ada[z, y] = ada_m[...].astype(BF16)
    loads[1].wait()
    loads[2].wait()
    proj_t = jnp.transpose(proj_m[...])
    wt[0, x, z, y] = jnp.concatenate(
        [
            part[:, 64 * head:64 * head + 64]
            for head in range(3) for part in (qkv_m[0], qkv_m[1], qkv_m[2], proj_t)
        ],
        axis=1,
    ).astype(BF16)
    pl.semaphore_wait(barrier, len(partners))

    def view(ref, fixed, height, columns):
        index = [fixed.get(axis, slice(None)) for axis in "xzy"]
        return ref.at[(*index, height, columns)]

    flying = {}
    sources = [wt.at[1], g1, g2]

    def gather(chunk, piece, phase):
        tensor, start, width = CHUNKS[chunk]
        first_row, height, order = GATHER[chunk][piece]
        axis = order[phase]
        fixed = {name: own[name] for name in order[phase:]}

        def block(at):
            return view(
                wt.at[tensor], {**fixed, axis: at}, pl.ds(first_row, height), pl.ds(start, width)
            )

        mine = block(own[axis])
        if axis != "z":
            return [send(mine, mine, peers[axis][1])]
        beside, other = send(mine, mine, to_beside), send(mine, mine, to_other)
        landing = slots("receive")
        across = copy_of(mine, mine, to_across, landing)
        passed = block(z_other)
        onward = copy_of(passed, passed, to_beside, landing)
        pl.when(inner)(across.start)
        sent_inner.extend((across, onward))
        return [beside, other, across, onward]

    def reduce(chunk, piece, phase):
        tensor, start, width = CHUNKS[chunk]
        first_row, height, order = REDUCE[chunk][piece]
        axis = order[phase]
        fixed = {name: own[name] for name in order[:phase]}
        landing = inbox[chunk, piece, phase]

        def block(at):
            return view(
                sources[tensor], {**fixed, axis: at}, pl.ds(first_row, height), pl.ds(start, width)
            )

        if axis != "z":
            at, target = peers[axis]
            return [send(block(at), landing.at[0], target)]
        beside = send(block(z_beside), landing.at[0], to_beside)
        number = slots("receive", 3)
        at = jnp.where(outer, z_other, z_across)
        kind = jnp.where(outer, 0, 1)
        direct = send(block(at), landing.at[1 + kind], device(at, y, x, core), number + kind)
        given = copy_of(block(z_across), landing.at[3], to_beside, number + 2)
        pl.when(outer)(given.start)
        sent_outer.append(given)
        total = copy_of(block(z_other), landing.at[1], to_other, number)
        sent_inner.append(total)
        waits = [
            copy_of(block(z_other), landing.at[1 + slot], to_other, number + slot, False) for slot in (0, 1)
        ]
        return [beside, waits[0], waits[1], given, total]

    def take(kind, chunk, piece, phase):
        tensor, start, width = CHUNKS[chunk]
        first_row, height, order = (GATHER if kind == "g" else REDUCE)[chunk][piece]
        axis = order[phase % 3]
        copies = flying[kind, chunk, piece, phase % 3]
        if kind == "g":
            if axis != "z":
                arrive(copies)
            elif phase < 3:
                arrive(copies[:2])
                pl.when(inner)(copies[3].start)
            else:
                arrive(copies[2:3])
            return
        landing = inbox[chunk, piece, phase % 3]
        source = sources[tensor]

        def place(at):
            fixed = {**{name: own[name] for name in order[:phase % 3]}, axis: at}
            index = [fixed.get(name, slice(None)) for name in "xzy"]
            return (*index, pl.ds(first_row, height), pl.ds(start, width))

        target = place(own[axis])
        if axis != "z":
            arrive(copies)
            total = source[target].astype(F32) + landing[0].astype(F32)
        elif phase < 3:
            arrive(copies[:1])

            @pl.when(inner)
            def _():
                arrive(copies[1:4])
                target = place(z_other)
                source[target] = (source[target].astype(F32) + landing[3].astype(F32)).astype(BF16)
                copies[4].start()

            return
        else:

            @pl.when(outer)
            def _():
                arrive(copies[1:2])

            total = source[target].astype(F32) + landing[0].astype(F32) + landing[1].astype(F32)
            across = landing[jnp.where(inner, 2, 0)].astype(F32)
            total = total + across * jnp.where(inner, 1.0, 0.0)
        if phase % 3 == 2:
            grads[tensor, pl.ds(first_row, height), pl.ds(start, width)] = total
        else:
            source[target] = total.astype(BF16)

    def cross(ref, landing, part):
        piece = pl.ds(pl.multiple_of(part * 256 + core * 128, 128), 128)
        return [send(ref.at[piece, :], landing.at[piece, :], to_x)]

    def share(landing, part):
        piece = landing.at[pl.ds(pl.multiple_of(part * 256 + core * 128, 128), 128), :]
        shared.append(send(piece, piece, to_core))

    shared = []
    outputs = {"b": (bo, bo_in), "t": (slope.at[0], gt_in)}
    position = [0]

    def serve():
        for action, kind, chunk, piece, phase in PLAN[position[0]]:
            if action == "I":
                if phase < 3:
                    begin = {"g": gather, "r": reduce}.get(kind)
                    flying[kind, chunk, piece, phase] = (
                        begin(chunk, piece, phase) if begin else cross(*outputs[kind], chunk)
                    )
            elif kind in "gr":
                take(kind, chunk, piece, phase)
            else:
                arrive(flying[kind, chunk, piece, phase])
                share(outputs[kind][1], chunk)
        position[0] += 1

    own_ada = ada.at[z, y]
    ada_one = [send(own_ada, own_ada, target) for target in to_z]
    serve()
    loads[3].wait()
    wt[1, x, z, y] = up_m[...].astype(BF16)
    loads[4].wait()
    wt[2, x, z, y] = down_m[...].astype(BF16)
    loads[5].wait()

    row_id = lax.broadcasted_iota(jnp.int32, (16, 128), 0)
    lane_id = lax.broadcasted_iota(jnp.int32, (16, 128), 1)
    steps = jnp.where(row_id == 0, time_ref[0], time_ref[1]).astype(F32)
    angles = steps * freq[0:1, :]
    cond = jnp.where(lane_id < 64, jnp.cos(angles), jnp.sin(angles)).astype(BF16)

    ends = []
    total = 0
    for number in range(4):
        total = total + doc_ref[x, number]
        ends.append(total)
    serve()

    def tables(index):
        block = rows(index, 128)
        token_id = lax.broadcasted_iota(jnp.int32, (128, 128), 0) + index * 128
        lanes = lax.broadcasted_iota(jnp.int32, (128, 128), 1)
        document = sum((token_id >= end).astype(jnp.int32) for end in ends)
        place = lax.rem(lanes, 64)
        same[block, :] = jnp.where(place == document, 1.0, 0.0).astype(BF16)
        apart = jnp.where((place < 4) & (place != document), NEG_BIG, 0.0)
        other[block, :] = jnp.where((place >= 4) & (place < 7), 1.0, apart).astype(BF16)
        begin = jnp.zeros((128, 128), jnp.int32)
        for end in ends[:3]:
            begin = jnp.where(token_id >= end, end, begin)
        turned = (token_id - begin).astype(F32) * theta[0:1, :]
        cosine[block, :] = jnp.cos(turned)
        turned_sine = jnp.sin(turned)
        sine[block, :] = jnp.where(lax.rem(lanes, 64) < 32, -turned_sine, turned_sine)

    pl.loop(0, 8)(tables)
    serve()
    serve()
    arrive(ada_one)
    own_ada = ada.at[:, y]
    ada_two = [send(own_ada, own_ada, to_y)]
    serve()
    serve()
    arrive(ada_two)
    modq[mp] = mm(cond, ada[...].reshape(COND, QUARTER), NN)[0:8]
    own_mod = modq.at[mp]
    mod_copies = [send(own_mod, own_mod, target) for target in (to_core, to_x, to_diag)]
    serve()
    serve()
    arrive(mod_copies)
    own_row = pl.ds(x, 1)
    half_width = WIDTH // 2
    mod[0:1, :] = modq[0, own_row, 0:WIDTH] + vec[3:4, :]
    mod[1:2, :] = (
        jnp.concatenate([modq[0, own_row, WIDTH:QUARTER], modq[1, own_row, 0:half_width]], axis=1)
        + vec[4:5, :]
    )
    mod[2:3, :] = modq[1, own_row, half_width:QUARTER] + vec[5:6, :]
    mod[3:4, :] = modq[2, own_row, 0:WIDTH] + vec[6:7, :]
    mod[4:5, :] = (
        jnp.concatenate([modq[2, own_row, WIDTH:QUARTER], modq[3, own_row, 0:half_width]], axis=1)
        + vec[7:8, :]
    )
    mod[5:6, :] = modq[3, own_row, half_width:QUARTER] + vec[8:9, :]

    loads[6].wait()
    loads[7].wait()

    for part in range(2):

        @pl.loop(part * 2, part * 2 + 2)
        def _(index):
            block = rows(index, 256)
            normed, _ = norm_tile(tok[block, :].astype(F32))
            h1[block, :] = (normed * (vec[0:1, :] * (1.0 + mod[1:2, :])) + mod[0:1, :]).astype(BF16)
            dm[block, :] = (cot[block, :].astype(F32) * mod[5:6, :]).astype(BF16)

        serve()

    def rotate(tile, block):
        lanes = lax.broadcasted_iota(jnp.int32, tile.shape, 1)
        swapped = jnp.where(
            lax.rem(lanes, 64) < 32, pltpu.roll(tile, 96, 1), pltpu.roll(tile, 32, 1)
        )
        return tile * cosine[block, :] + swapped * sine[block, :]

    def rotate_transposed(tile, block):
        lanes = lax.broadcasted_iota(jnp.int32, tile.shape, 1)
        turned = tile * sine[block, :]
        swapped = jnp.where(
            lax.rem(lanes, 64) < 32, pltpu.roll(turned, 96, 1), pltpu.roll(turned, 32, 1)
        )
        return tile * cosine[block, :] + swapped

    def project(pair):
        start = 256 * pair
        tiles = [
            [
                wt[0, side, :, :, :, start + 128 * part:start + 128 * part + 128].reshape(WIDTH, 128)
                for part in (0, 1)
            ]
            for side in (0, 1)
        ]
        cols = slice(pair * 128, pair * 128 + 128)
        both = slice(pair * 256, pair * 256 + 256)
        left, right = interleave(tiles[0][0], tiles[1][0])
        wqk[:, both] = jnp.concatenate([left, right], axis=1)
        wv[:, cols], wp[:, cols] = interleave(tiles[0][1], tiles[1][1])

        @pl.loop(0, LEN_FAST // 256)
        def _(index):
            block = rows(index, 256)
            full = mm(h1[block, :], wqk[:, both], NN)
            turned = rotate(full[:, 0:128], block).astype(BF16)
            q[block, cols] = (turned.astype(F32) * 0.125).astype(BF16)
            k[block, cols] = rotate(full[:, 128:256], block).astype(BF16)
            v[block, cols] = mm(h1[block, :], wv[:, cols], NN).astype(BF16)

    def own_half(shape, head):
        lower = lower_lanes(shape)
        return lower if head == 0 else ~lower

    def keep_head(tile, head):
        return jnp.where(own_half(tile.shape, head), tile, jnp.zeros_like(tile))

    def head_tiles(pair):
        cols = slice(pair * 128, pair * 128 + 128)
        for head in range(2):
            mine = own_half((LEN_FAST, 128), head)
            kt[head] = jnp.where(mine, k[:, cols], other[...])
            vt[head] = jnp.where(mine, v[:, cols], jnp.ones((LEN_FAST, 128), BF16))

    def beside(tile, values):
        place = lax.rem(lax.broadcasted_iota(jnp.int32, tile.shape, 1), 64)
        for number in range(3):
            term = values.astype(BF16)
            values = values - term.astype(F32)
            tile = jnp.where(place == 4 + number, term, tile)
        return tile

    def attend(pair, part):
        cols = slice(pair * 128, pair * 128 + 128)
        block = slice(512 * part, 512 * part + 512)
        if part == 0:
            head_tiles(pair)
        mixed = []
        for head in range(2):
            mine = own_half((512, 128), head)
            scores = mm(jnp.where(mine, q[block, cols], same[block, :]), kt[head], NT)
            top = jnp.max(scores, axis=1, keepdims=True)
            total = mm(jnp.exp(scores - top).astype(BF16), vt[head], NN)
            mixed.append(total * (1.0 / pltpu.roll(total, 64, 1)))
            number = 2 * pair + head
            beyond = 64 - 64 * head
            lse[block, number:number + 1] = top + jnp.log(total[:, beyond:beyond + 1])
        o[block, cols] = jnp.where(lower_lanes((512, 128)), mixed[0], mixed[1]).astype(BF16)

    for pair in range(3):
        serve()
        project(pair)
        serve()
        attend(pair, 0)
        serve()
        attend(pair, 1)
        serve()

    def swap(own_ref, incoming, make):
        copies = []
        for index in range(4):
            block = slice(index * 256, index * 256 + 256)
            own_ref[block, :] = make(block).astype(BF16)
            piece = pl.ds(index * 256, 256)
            copies.append(send(own_ref.at[piece, :], incoming.at[piece, :], to_core))
        return copies

    attn_copies = swap(attn_own, attn_in, lambda block: mm(o[block, :], wp[...], NT))
    serve()

    for part in range(4):
        serve()
        attn_copies[part].wait_recv()

        @pl.loop(part, part + 1)
        def _(index):
            block = rows(index, 256)
            attn = attn_own[block, :].astype(F32) + attn_in[block, :].astype(F32)
            middle = tok[block, :].astype(F32) + mod[2:3, :] * attn
            x1[block, :] = middle
            normed, _ = norm_tile(middle)
            h2[block, :] = (normed * (vec[1:2, :] * (1.0 + mod[4:5, :])) + mod[3:4, :]).astype(BF16)

        serve()

    def raise_hidden(half):
        cols = slice(384 * half, 384 * half + 384)
        for side in range(2):

            @pl.loop(0, LEN_FAST // 512)
            def _(index):
                block = rows(index, 512)
                bias = vec[pl.ds(9 + 2 * side + core, 1), cols]
                u = mm(h2[block, :], wt[1, side, :, :, :, cols].reshape(WIDTH, 384), NN) + bias
                square = u * u
                bent = jnp.tanh(u * (0.7978845608028654 + 0.03567740813636141 * square))
                half_u = 0.5 * u
                act[side, block, cols] = (half_u + half_u * bent).astype(BF16)
                rising = half_u * (0.7978845608028654 + 0.10703222440908423 * square)
                slope[side, block, cols] = (
                    0.5 + 0.5 * bent + (1.0 - bent * bent) * rising
                ).astype(BF16)

            serve()

        for side in range(2):
            grad = mm(dm[...], act[side, :, cols], TN).astype(BF16)
            g2[side, :, :, :, cols] = grad.reshape(4, 2, SHARD, 384)

    for half in range(2):
        serve()
        raise_hidden(half)
        serve()
        serve()

    def lower_hidden(half):
        cols = slice(384 * half, 384 * half + 384)
        for side in range(2):

            @pl.loop(0, LEN_FAST // 512)
            def _(index):
                block = rows(index, 512)
                back = mm(dm[block, :], wt[2, side, :, :, :, cols].reshape(WIDTH, 384), NN)
                grad = (back * slope[side, block, cols].astype(F32)).astype(BF16)
                slope[side, block, cols] = grad
                dup_acc[side, :, cols] = dup_acc[side, :, cols] + jnp.sum(
                    grad.astype(F32).reshape(64, 8, 384), axis=0
                )

        serve()
        for side in range(2):
            grad = mm(h2[...], slope[side, :, cols], TN).astype(BF16)
            g1[side, :, :, :, cols] = grad.reshape(4, 2, SHARD, 384)

    dup_acc[...] = jnp.zeros_like(dup_acc)
    for half in range(2):
        serve()
        lower_hidden(half)
        serve()
        serve()

    def back_two(block):
        return mm(slope[0, block, :], wt[1, 0].reshape(WIDTH, WIDTH), NT) + mm(
            slope[1, block, :], wt[1, 1].reshape(WIDTH, WIDTH), NT
        )

    dh2_own, mlp_own = slope.at[0], act.at[0]
    dh2_copies = swap(dh2_own, dh2_in, back_two)
    serve()

    def forward_two(block):
        return mm(act[0, block, :], wt[2, 0].reshape(WIDTH, WIDTH), NT) + mm(
            act[1, block, :], wt[2, 1].reshape(WIDTH, WIDTH), NT
        )

    mlp_copies = swap(mlp_own, mlp_in, forward_two)
    serve()

    dup[0] = jnp.zeros((8, WIDTH), F32)
    for side in range(2):
        dup[0, side:side + 1, :] = jnp.sum(dup_acc[side], axis=0, keepdims=True)
    dup_copy = send(dup.at[0], dup.at[1], to_core)
    serve()

    acc[...] = jnp.zeros_like(acc)

    def add_row(row, values):
        count = values.shape[0]
        acc[row] = acc[row] + jnp.sum(values.reshape(count // 8, 8, WIDTH), axis=0)

    for part in range(4):
        serve()
        dh2_copies[part].wait_recv()
        serve()
        mlp_copies[part].wait_recv()

        @pl.loop(part * 2, part * 2 + 2)
        def _(index):
            block = rows(index, 128)
            middle = x1[block, :]
            seen = cot[block, :].astype(F32)
            mlp = mlp_own[block, :].astype(F32) + mlp_in[block, :].astype(F32) + vec[2:3, :]
            bo[block, :] = (middle + mod[5:6, :] * mlp).astype(BF16)
            add_row(3, seen * mlp)
            add_row(4, seen)
            back = dh2_own[block, :].astype(F32) + dh2_in[block, :].astype(F32)
            normed, inv = norm_tile(middle)
            add_row(0, back)
            add_row(1, back * normed)
            scaled = back * (vec[1:2, :] * (1.0 + mod[4:5, :]))
            grad = seen + inv * (
                scaled - jnp.mean(scaled, axis=1, keepdims=True)
                - normed * jnp.mean(scaled * normed, axis=1, keepdims=True)
            )
            x1[block, :] = grad
            attn = attn_own[block, :].astype(F32) + attn_in[block, :].astype(F32)
            add_row(2, grad * attn)
            dm[block, :] = (grad * mod[2:3, :]).astype(BF16)

        serve()
        serve()

    bo_store = pltpu.make_async_copy(bo, block_out.at[x], local_sem.at[8])
    bo_store.start()

    @pl.loop(0, LEN_FAST // 256)
    def _(index):
        block = rows(index, 256)
        do[block, :] = mm(dm[block, :], wp[...], NN).astype(BF16)

    for key, copies in flying.items():
        if key[:2] in (("g", 3), ("g", 4)):
            flush([copy for copy in copies if any(copy is other for other in sent)])
            inner_copies = [copy for copy in copies if any(copy is other for other in sent_inner)]
            done.extend(id(copy) for copy in inner_copies)

            @pl.when(inner)
            def _():
                for copy in inner_copies:
                    copy.wait_send()

    g0 = sources[0]
    dzqk = h2

    def attend_back(pair, index):
        cols = slice(pair * 128, pair * 128 + 128)
        both = 256 * pair
        if index == 0:
            head_tiles(pair)
        begin, end = max(0, index - 2) * 256, min(4, index + 3) * 256
        keys = slice(begin, end)
        block = slice(256 * index, 256 * index + 256)
        query = q[block, cols]
        back = do[block, cols]
        product = back.astype(F32) * o[block, cols].astype(F32)
        grad_q = []
        for head in range(2):
            number = 2 * pair + head
            mine = own_half(query.shape, head)
            queries = jnp.where(mine, query, beside(same[block, :], -lse[block, number:number + 1]))
            probs = jnp.exp(mm(queries, kt[head, keys, :], NT))
            delta = jnp.sum(keep_head(product, head), axis=1, keepdims=True)
            backs = jnp.where(mine, back, beside(jnp.zeros_like(back), -delta))
            grad_s = (probs * mm(backs, vt[head, keys, :], NT)).astype(BF16)
            grad_q.append(mm(grad_s, k[keys, cols], NN))
            ka[keys, :] += mm(grad_s, keep_head(query, head), TN)
            va[keys, :] += mm(probs.astype(BF16), keep_head(back, head), TN)
        full = jnp.where(lower_lanes(grad_q[0].shape), grad_q[0], grad_q[1]) * 0.125
        dzqk[block, both:both + 128] = rotate_transposed(full, block).astype(BF16)

    grad_p = mm(dm[...], o[...], TN).astype(BF16)
    for pair in range(3):
        g0[0, :, :, :, 256 * pair + 128:256 * pair + 256] = grad_p[
            :, 128 * pair:128 * pair + 128
        ].reshape(4, 2, SHARD, 128)

    def finish(pair):
        cols = slice(pair * 128, pair * 128 + 128)
        start = 256 * pair
        dzqk[:, start + 128:start + 256] = rotate_transposed(ka[...], pl.ds(0, LEN_FAST)).astype(BF16)
        dzv[:, cols] = va[...].astype(BF16)

    def head_grads(pair):
        cols = slice(pair * 128, pair * 128 + 128)
        start = 256 * pair
        grad_qk = mm(h1[...], dzqk[:, start:start + 256], TN).astype(BF16)
        grad_v = mm(h1[...], dzv[:, cols], TN).astype(BF16)
        held = g0[0, :, :, :, start + 128:start + 256].reshape(WIDTH, 128)
        for number, (first, second) in enumerate(
            ((grad_qk[:, 0:128], grad_qk[:, 128:256]), (grad_v, held))
        ):
            sides = interleave(first, second)
            place = start + 128 * number
            for side in range(2):
                g0[side, :, :, :, place:place + 128] = sides[side].reshape(4, 2, SHARD, 128)

    def clear():
        ka[...] = jnp.zeros_like(ka)
        va[...] = jnp.zeros_like(va)

    serve()
    for pair in range(3):
        clear()
        for index in range(4):
            attend_back(pair, index)
            serve()
        finish(pair)
        if pair < 2:
            head_grads(pair)
            serve()
            serve()

    def back_one(block):
        return mm(dzqk[block, :], wqk[...], NT) + mm(dzv[block, :], wv[...], NT)

    flush(dh2_copies)
    flush(mlp_copies)
    gt = slope.at[0]
    dh1_copies = swap(act.at[0], act.at[1], back_one)
    serve()
    head_grads(2)
    serve()
    serve()
    for part in range(4):
        serve()
        dh1_copies[part].wait_recv()

        @pl.loop(part * 2, part * 2 + 2)
        def _(index):
            block = rows(index, 128)
            back = act[0, block, :].astype(F32) + act[1, block, :].astype(F32)
            normed, inv = norm_tile(tok[block, :].astype(F32))
            add_row(5, back)
            add_row(6, back * normed)
            scaled = back * (vec[0:1, :] * (1.0 + mod[1:2, :]))
            gt[block, :] = (
                x1[block, :] + inv * (
                    scaled - jnp.mean(scaled, axis=1, keepdims=True)
                    - normed * jnp.mean(scaled * normed, axis=1, keepdims=True)
                )
            ).astype(BF16)

        serve()
        serve()

    gt_store = pltpu.make_async_copy(gt, grad_out.at[x], local_sem.at[9])
    gt_store.start()

    sums = [jnp.sum(acc[row], axis=0, keepdims=True) for row in range(7)]
    shift2, prod2, gate1, gate2, seen, shift1, prod1 = sums
    dup_copy.wait_recv()
    first_rows = jnp.where(core == 0, dup[0], dup[1])
    second_rows = jnp.where(core == 0, dup[1], dup[0])
    cond_row = jnp.where(x == 0, cond[0:1, :].astype(F32), cond[1:2, :].astype(F32))
    st[x, z, y] = jnp.concatenate(
        [
            shift1, prod1 * vec[0:1, :], gate1, shift2, prod2 * vec[1:2, :], gate2,
            prod1 * (1.0 + mod[1:2, :]), prod2 * (1.0 + mod[4:5, :]), seen * mod[5:6, :],
            jnp.concatenate([cond_row, jnp.zeros((1, WIDTH - 128), F32)], axis=1),
            first_rows[0:1, :], second_rows[0:1, :], first_rows[1:2, :], second_rows[1:2, :],
            jnp.zeros((2, WIDTH), F32),
        ],
        axis=0,
    ).astype(BF16)
    half_cols = pl.ds(pl.multiple_of(core * 384, 128), 384)
    own_stats = st.at[x, z, y, :, half_cols]
    stats_one = [send(own_stats, own_stats, target) for target in to_z]
    serve()
    serve()
    arrive(stats_one)
    own_stats = st.at[x, :, y, :, half_cols]
    stats_two = [send(own_stats, own_stats, to_y)]
    serve()
    arrive(stats_two)
    own_stats = st.at[x, :, :, :, half_cols]
    stats_three = [send(own_stats, own_stats, to_x)]
    serve()
    grads_store = pltpu.make_async_copy(grads, grads_out, local_sem.at[10])
    grads_store.start()
    arrive(shared)
    bo_rest = pltpu.make_async_copy(bo_in, block_out.at[1 - x], local_sem.at[12])
    gt_rest = pltpu.make_async_copy(gt_in, grad_out.at[1 - x], local_sem.at[13])
    bo_rest.start()
    gt_rest.start()
    serve()
    arrive(stats_three)
    own_stats = st.at[:, :, :, :, half_cols]
    arrive([send(own_stats, own_stats, to_core)])
    stats_store = pltpu.make_async_copy(st, stats_out, local_sem.at[11])
    stats_store.start()
    assert position[0] == len(PLAN)
    for copy in sent:
        if id(copy) not in done:
            copy.wait_send()

    @pl.when(inner)
    def _():
        for copy in sent_inner:
            if id(copy) not in done:
                copy.wait_send()

    @pl.when(outer)
    def _():
        for copy in sent_outer:
            copy.wait_send()

    for store in (bo_store, gt_store, grads_store, stats_store, bo_rest, gt_rest):
        store.wait()


def update_kernel(
    grads, stats, blocks_in, gt,
    qkv_m, qkv_f, qkv_s, proj_m, proj_f, proj_s, up_m, up_f, up_s, down_m, down_f, down_s,
    ada_m, ada_f, ada_s, vec_m, vec_f, vec_s,
    blocks_out, gt_out,
    qkv_mo, qkv_fo, qkv_so, proj_mo, proj_fo, proj_so, up_mo, up_fo, up_so, down_mo, down_fo, down_so,
    ada_mo, ada_fo, ada_so, vec_mo, vec_fo, vec_so,
    proj_grad, ada_grad,
):
    step = pl.program_id(0)
    blocks_out[...] = blocks_in[...]
    gt_out[...] = gt[...].astype(F32)

    def put(refs, outs, gradient, decay, rate, index=...):
        new = adamw(refs[0][index], refs[1][index], refs[2][index], gradient, decay, rate)
        for out, value in zip(outs, new):
            out[index] = value

    def columns(part):
        return jnp.concatenate(
            [grads[0, :, 256 * head + 64 * part:256 * head + 64 * part + 64] for head in range(3)], axis=1
        )

    for part in range(3):
        put((qkv_m, qkv_f, qkv_s), (qkv_mo, qkv_fo, qkv_so), columns(part), DECAY, RATE, part)
    put((up_m, up_f, up_s), (up_mo, up_fo, up_so), grads[1], DECAY, RATE)
    put((down_m, down_f, down_s), (down_mo, down_fo, down_so), grads[2], DECAY, RATE)
    proj_grad[rows(step, SHARD // 2), :] = columns(3)

    every = stats[...].reshape(16, 16, WIDTH)
    cond = every[:, 9, 0:COND]
    for number in range(2):

        @pl.when(step == number)
        def _():
            moved = jnp.concatenate([every[:, 3 * number + part, :] for part in range(3)], axis=1)
            ada_grad[...] = mm(cond, moved, TN)

    own_rows = pl.ds(pl.multiple_of(lax.axis_index("dp") * 16, 16), 16)
    put((ada_m, ada_f, ada_s), (ada_mo, ada_fo, ada_so), ada_grad[own_rows, :], DECAY, RATE)

    @pl.when(step == 1)
    def _():
        put(
            (proj_m, proj_f, proj_s), (proj_mo, proj_fo, proj_so), jnp.transpose(proj_grad[...]),
            DECAY, RATE,
        )
        total = jnp.sum(every.astype(F32), axis=0)
        gradient = jnp.concatenate([total[6:9], total[0:6], total[10:14]], axis=0)
        put((vec_m, vec_f, vec_s), (vec_mo, vec_fo, vec_so), gradient, 0.0, RATE_VEC)


def fast_shards(
    tokens, cotangent, doc_lengths, time_steps,
    qkv_master, qkv_first, qkv_second, proj_master, proj_first, proj_second,
    up_master, up_first, up_second, down_master, down_first, down_second,
    ada_master, ada_first, ada_second, vec_master, vec_first, vec_second,
):
    freq = np.tile(np.exp(-np.log(10000.0) * np.arange(64) / 64).astype(np.float32), (8, 2))
    theta = np.tile(np.exp(-np.log(ROPE_BASE) * np.arange(32) * 2.0 / HEAD).astype(np.float32), (8, 4))
    vmem = pl.BlockSpec(memory_space=pltpu.VMEM)
    smem = pl.BlockSpec(memory_space=pltpu.SMEM)
    anywhere = pl.BlockSpec(memory_space=pl.ANY)
    tall = (LEN_FAST, WIDTH)
    third = (LEN_FAST, 384)
    buffers = [
        ((3,) + STACK, BF16),
        ((4, 2, 16, QUARTER), BF16),
        ((4, 8, QUARTER), F32),
        ((8, WIDTH), F32),
        ((WIDTH, WIDTH), BF16), ((WIDTH, 384), BF16), ((WIDTH, 384), BF16),
        (tall, BF16), (tall, BF16), (tall, BF16),
        (third, BF16), (third, BF16), (third, BF16), (third, BF16),
        ((LEN_FAST, 128), F32),
        ((LEN_FAST, 128), F32), ((LEN_FAST, 128), F32),
        ((LEN_FAST, 128), BF16), ((LEN_FAST, 128), BF16),
        ((2, LEN_FAST, 128), BF16), ((2, LEN_FAST, 128), BF16),
        (tall, BF16), (tall, BF16),
        (tall, BF16), (tall, BF16),
        (tall, F32),
        (tall, BF16),
        ((2,) + tall, BF16), ((2,) + tall, BF16),
        (tall, BF16),
        (third, BF16), (third, BF16),
        (tall, BF16), (tall, BF16), (tall, BF16),
        (STACK, BF16), (STACK, BF16),
        ((2, 4, 2, 16, WIDTH), BF16),
        ((2, 8, WIDTH), F32), ((2, 8, WIDTH), F32),
        ((3, SHARD, WIDTH), F32),
        ((8, 8, WIDTH), F32),
        ((LEN_FAST, 128), F32), ((LEN_FAST, 128), F32),
    ]
    turned_qkv = [jnp.transpose(a, (1, 0, 2)) for a in (qkv_master, qkv_first, qkv_second)]
    turned_down = [a.T for a in (down_master, down_first, down_second)]
    grads, stats, blocks, grad_tokens = pl.pallas_call(
        step_kernel,
        out_shape=[
            jax.ShapeDtypeStruct((3, SHARD, WIDTH), F32),
            jax.ShapeDtypeStruct((2, 4, 2, 16, WIDTH), BF16),
            jax.ShapeDtypeStruct((2,) + tall, BF16),
            jax.ShapeDtypeStruct((2,) + tall, BF16),
        ],
        in_specs=[smem, smem] + [anywhere] * 8 + [vmem] * 2,
        out_specs=[anywhere] * 4,
        scratch_shapes=[pltpu.VMEM(shape, kind) for shape, kind in buffers]
        + [
            pltpu.VMEM((3, SHARD, 192), F32), pltpu.VMEM((192, SHARD), F32), pltpu.VMEM((SHARD, WIDTH), F32),
            pltpu.VMEM((SHARD, WIDTH), F32), pltpu.VMEM((16, QUARTER), F32), pltpu.VMEM(vec_master.shape, F32),
        ]
        + [pltpu.SemaphoreType.DMA((14,))] + [pltpu.SemaphoreType.DMA((COPIES,))] * 2
        + [pltpu.VMEM(shape, BF16) for shape in INBOX.values()],
        compiler_params=pltpu.CompilerParams(
            collective_id=0, has_side_effects=True, vmem_limit_bytes=VMEM_BYTES
        ),
    )(time_steps, doc_lengths, tokens, cotangent, turned_qkv[0], proj_master, up_master,
      turned_down[0], ada_master, vec_master, freq, theta)
    states = [
        *turned_qkv, proj_master, proj_first, proj_second, up_master, up_first, up_second,
        *turned_down, ada_master, ada_first, ada_second, vec_master, vec_first, vec_second,
    ]

    def whole(a):
        return pl.BlockSpec(a.shape, lambda i: (0,) * a.ndim)

    strip = pl.BlockSpec((2, LEN_FAST // 2, WIDTH), lambda i: (0, i, 0))
    part_rows = SHARD // 2
    shared = {
        "qkv": pl.BlockSpec((3, part_rows, 192), lambda i: (0, i, 0)),
        "row": pl.BlockSpec((part_rows, WIDTH), lambda i: (i, 0)),
        "ada": pl.BlockSpec((16, 2 * QUARTER), lambda i: (0, i)),
    }
    state_specs = [
        spec
        for spec in (shared["qkv"], whole(proj_master), shared["row"], shared["row"], shared["ada"], whole(vec_master))
        for _ in range(3)
    ]
    new = pl.pallas_call(
        update_kernel,
        grid=(2,),
        out_shape=[jax.ShapeDtypeStruct((2,) + tall, BF16), jax.ShapeDtypeStruct((2,) + tall, F32)]
        + [jax.ShapeDtypeStruct(a.shape, F32) for a in states],
        in_specs=[pl.BlockSpec((3, part_rows, WIDTH), lambda i: (0, i, 0)), whole(stats), strip, strip]
        + state_specs,
        out_specs=[strip, strip] + state_specs,
        scratch_shapes=[pltpu.VMEM((SHARD, 192), F32), pltpu.VMEM((COND, 2 * QUARTER), F32)],
        compiler_params=pltpu.CompilerParams(vmem_limit_bytes=VMEM_BYTES),
    )(grads, stats, blocks, grad_tokens, *states)
    blocks, grad_tokens, *new = new
    new[0:3] = [jnp.transpose(a, (1, 0, 2)) for a in new[0:3]]
    new[9:12] = [a.T for a in new[9:12]]
    return (blocks, grad_tokens, *new)


def solution(mesh):
    placed = (
        P("dp", None, None),
        P("dp", None, None),
        P("dp", None),
        P("dp"),
        P("dp", None, "mp"),
        P("dp", None, "mp"),
        P("dp", None, "mp"),
        P("mp", "dp"),
        P("mp", "dp"),
        P("mp", "dp"),
        P("dp", "mp"),
        P("dp", "mp"),
        P("dp", "mp"),
        P("mp", "dp"),
        P("mp", "dp"),
        P("mp", "dp"),
        P("dp", None),
        P("dp", None),
        P("dp", None),
        P(),
        P(),
        P(),
    )
    fast = mesh.shape["dp"] == 8 and mesh.shape["mp"] == 4
    return jax.shard_map(
        fast_shards if fast else shards,
        mesh=mesh,
        in_specs=placed,
        out_specs=(
            P("dp", None, None),
            P("dp", None, None),
            P("dp", None, "mp"),
            P("dp", None, "mp"),
            P("dp", None, "mp"),
            P("mp", "dp"),
            P("mp", "dp"),
            P("mp", "dp"),
            P("dp", "mp"),
            P("dp", "mp"),
            P("dp", "mp"),
            P("mp", "dp"),
            P("mp", "dp"),
            P("mp", "dp"),
            P("dp", None),
            P("dp", None),
            P("dp", None),
            P(),
            P(),
            P(),
        ),
        check_vma=False,
    )
```

```python
from functools import partial
import math

import jax
import jax.numpy as jnp
import numpy as np
from jax import lax
from jax.experimental import pallas as pl
from jax.experimental.pallas import tpu as pltpu
from jax.sharding import PartitionSpec as P

HEAD = 64
COND = 128
STEP = 10


EPS_NORM = 1e-05
ROPE_BASE = 10000.0
RATE = 0.14
RATE_VEC = 0.4
BETA_ONE = 0.9
BETA_TWO = 0.999
EPS_ADAM = 1e-08
DECAY = 0.1
NEG_BIG = -1e30


def time_features(steps, width):
    half_size = width // 2
    freqs = jnp.exp(-jnp.log(10000.0) * jnp.arange(half_size, dtype=jnp.float32) / half_size)
    angles = steps.astype(jnp.float32)[:, None] * freqs[None, :]
    return jnp.concatenate([jnp.cos(angles), jnp.sin(angles)], axis=1)


def doc_layout(doc_lens, length):
    doc_ends = jnp.cumsum(doc_lens)
    places = jnp.arange(length, dtype=jnp.int32)
    passed = (places[:, None] >= doc_ends[None, :]).astype(jnp.int32)
    return (jnp.sum(passed, axis=1), places - jnp.sum(passed * doc_lens[None, :], axis=1))


def rotary_tables(positions, head_size):
    half_size = head_size // 2
    inverse = jnp.exp(
        -jnp.log(ROPE_BASE) * jnp.arange(half_size, dtype=jnp.float32) * 2.0 / head_size
    )
    angles = positions.astype(jnp.float32)[..., None] * inverse
    angles = jnp.concatenate([angles, angles], axis=-1)
    return (jnp.cos(angles), jnp.sin(angles))


def rotate_half(values):
    half_size = values.shape[-1] // 2
    return jnp.concatenate([-values[..., half_size:], values[..., :half_size]], axis=-1)


def rotate_apply(values, cosine, sine):
    return values * cosine + rotate_half(values) * sine


def rotate_back(gradient, cosine, sine):
    return gradient * cosine - rotate_half(gradient * sine)


def norm_rows(values):
    centred = values - jnp.mean(values, axis=-1, keepdims=True)
    inv_std = lax.rsqrt(jnp.mean(centred * centred, axis=-1, keepdims=True) + EPS_NORM)
    return (centred * inv_std, inv_std)


def norm_back(gradient, normed, inv_std):
    return inv_std * (
        gradient
        - jnp.mean(gradient, axis=-1, keepdims=True)
        - normed * jnp.mean(gradient * normed, axis=-1, keepdims=True)
    )


def adamw(master, moment_one, second, gradient, decay_rate, rate_now):
    first_new = BETA_ONE * moment_one + (1.0 - BETA_ONE) * gradient
    second_new = BETA_TWO * second + (1.0 - BETA_TWO) * gradient * gradient
    fix_one = 1.0 - BETA_ONE**STEP
    fix_two = 1.0 - BETA_TWO**STEP
    stepped = first_new / fix_one / (jnp.sqrt(second_new / fix_two) + EPS_ADAM)
    return (master - rate_now * (stepped + decay_rate * master), first_new, second_new)


def shards(
    tokens,
    cotangent,
    doc_lengths,
    time_steps,
    qkv_master,
    qkv_first,
    qkv_second,
    proj_master,
    proj_first,
    proj_second,
    up_master,
    up_first,
    up_second,
    down_master,
    down_first,
    down_second,
    ada_master,
    ada_first,
    ada_second,
    vec_master,
    vec_first,
    vec_second,
):
    w_qkv, w_proj, w_up, w_down, w_ada = (
        lax.all_gather(qkv_master.astype(jnp.bfloat16), "dp", axis=0, tiled=True),
        lax.all_gather(proj_master.astype(jnp.bfloat16), "dp", axis=1, tiled=True),
        lax.all_gather(up_master.astype(jnp.bfloat16), "dp", axis=0, tiled=True),
        lax.all_gather(down_master.astype(jnp.bfloat16), "dp", axis=1, tiled=True),
        lax.all_gather(ada_master.astype(jnp.bfloat16), "dp", axis=0, tiled=True),
    )
    seq_count, length, model_width = tokens.shape
    row_count = seq_count * length
    local_width = w_qkv.shape[2]
    local_heads = local_width // HEAD
    hidden_local = w_up.shape[1]
    mp_index = lax.axis_index("mp")
    block_rows = min(512, length)
    blocks = length // block_rows
    factor = 1.0 / math.sqrt(HEAD)
    cond_b = time_features(time_steps, COND).astype(jnp.bfloat16)
    modulate = (
        jnp.dot(cond_b, w_ada, preferred_element_type=jnp.float32) + vec_master[3:9].reshape(-1)
    ).reshape(seq_count, 6, model_width)
    shift_one = modulate[:, 0, None]
    scale_one = modulate[:, 1, None]
    gate_one = modulate[:, 2, None]
    shift_two = modulate[:, 3, None]
    scale_two = modulate[:, 4, None]
    gate_two = modulate[:, 5, None]
    gain_one = vec_master[0]
    gain_two = vec_master[1]
    down_bias = vec_master[2]
    up_bias = lax.dynamic_slice_in_dim(
        vec_master[9:].reshape(-1), mp_index * hidden_local, hidden_local
    )
    doc_ids, positions = jax.vmap(partial(doc_layout, length=length))(doc_lengths)
    cosine, sine = rotary_tables(positions, HEAD)
    cosine = cosine[:, :, None, :]
    sine = sine[:, :, None, :]
    x_in = tokens.astype(jnp.float32)
    normed_one, inv_one = norm_rows(x_in)
    h_attn = (
        (normed_one * gain_one * (1.0 + scale_one) + shift_one)
        .astype(jnp.bfloat16)
        .reshape(row_count, model_width)
    )
    w_qkv_flat = w_qkv.reshape(model_width, 3 * local_width)
    proj_qkv = jnp.dot(h_attn, w_qkv_flat, preferred_element_type=jnp.float32).reshape(
        seq_count, length, 3, local_heads, HEAD
    )
    queries = rotate_apply(proj_qkv[:, :, 0], cosine, sine).astype(jnp.bfloat16)
    keys_all = rotate_apply(proj_qkv[:, :, 1], cosine, sine).astype(jnp.bfloat16)
    values_all = proj_qkv[:, :, 2].astype(jnp.bfloat16)

    def attend(block_index):
        seq_no = block_index // blocks
        offset = block_index % blocks * block_rows
        query_blk = lax.dynamic_slice_in_dim(queries[seq_no], offset, block_rows, 0)
        doc_query = lax.dynamic_slice_in_dim(doc_ids[seq_no], offset, block_rows, 0)
        same_doc = doc_query[:, None] == doc_ids[seq_no][None, :]
        scores = (
            jnp.einsum(
                "qhd,khd->hqk", query_blk, keys_all[seq_no], preferred_element_type=jnp.float32
            )
            * factor
        )
        scores = jnp.where(same_doc[None], scores, NEG_BIG)
        row_max = jnp.max(scores, axis=-1, keepdims=True)
        expo = jnp.exp(scores - row_max)
        totals = jnp.sum(expo, axis=-1, keepdims=True)
        soft_probs = (expo / totals).astype(jnp.bfloat16)
        mixed = jnp.einsum(
            "hqk,khd->qhd", soft_probs, values_all[seq_no], preferred_element_type=jnp.float32
        )
        return (mixed.astype(jnp.bfloat16), (row_max + jnp.log(totals))[..., 0])

    mixed_blocks, log_totals = lax.map(attend, jnp.arange(seq_count * blocks))
    mixed_flat = mixed_blocks.reshape(row_count, local_width)
    attn_out = (
        lax.psum(
            jnp.dot(mixed_flat, w_proj, preferred_element_type=jnp.float32).astype(jnp.bfloat16),
            "mp",
        )
        .astype(jnp.float32)
        .reshape(seq_count, length, model_width)
    )
    x_mid = x_in + gate_one * attn_out
    normed_two, inv_two = norm_rows(x_mid)
    h_mlp = (
        (normed_two * gain_two * (1.0 + scale_two) + shift_two)
        .astype(jnp.bfloat16)
        .reshape(row_count, model_width)
    )
    up_pre = jnp.dot(h_mlp, w_up, preferred_element_type=jnp.float32) + up_bias
    act_b = jax.nn.gelu(up_pre, approximate=True).astype(jnp.bfloat16)
    mlp_out = (
        lax.psum(
            jnp.dot(act_b, w_down, preferred_element_type=jnp.float32).astype(jnp.bfloat16), "mp"
        )
        .astype(jnp.float32)
        .reshape(seq_count, length, model_width)
        + down_bias
    )
    block_out = (x_mid + gate_two * mlp_out).astype(jnp.bfloat16)
    grad_y = cotangent.astype(jnp.float32)
    grad_mlp = grad_y * gate_two
    grad_gate_two = jnp.sum(grad_y * mlp_out, axis=1)
    grad_down_bias = jnp.sum(grad_mlp, axis=(0, 1))
    grad_mlp_b = grad_mlp.reshape(row_count, model_width).astype(jnp.bfloat16)
    grad_w_down = jnp.dot(act_b.T, grad_mlp_b, preferred_element_type=jnp.float32)
    grad_act = jnp.dot(grad_mlp_b, w_down.T, preferred_element_type=jnp.float32)
    unused, gelu_pull = jax.vjp(partial(jax.nn.gelu, approximate=True), up_pre)
    grad_up_b = gelu_pull(grad_act)[0].astype(jnp.bfloat16)
    grad_up_bias = jnp.sum(grad_up_b, axis=0, dtype=jnp.float32)
    grad_w_up = jnp.dot(h_mlp.T, grad_up_b, preferred_element_type=jnp.float32)
    grad_h_mlp = (
        lax.psum(
            jnp.dot(grad_up_b, w_up.T, preferred_element_type=jnp.float32).astype(jnp.bfloat16),
            "mp",
        )
        .astype(jnp.float32)
        .reshape(seq_count, length, model_width)
    )
    grad_shift_two = jnp.sum(grad_h_mlp, axis=1)
    grad_scale_two = jnp.sum(grad_h_mlp * normed_two * gain_two, axis=1)
    grad_gain_two = jnp.sum(grad_h_mlp * normed_two * (1.0 + scale_two), axis=(0, 1))
    grad_mid = grad_y + norm_back(grad_h_mlp * gain_two * (1.0 + scale_two), normed_two, inv_two)
    grad_gate_one = jnp.sum(grad_mid * attn_out, axis=1)
    grad_attn_b = (grad_mid * gate_one).reshape(row_count, model_width).astype(jnp.bfloat16)
    grad_w_proj = jnp.dot(mixed_flat.T, grad_attn_b, preferred_element_type=jnp.float32)
    grad_mixed = (
        jnp.dot(grad_attn_b, w_proj.T, preferred_element_type=jnp.float32)
        .astype(jnp.bfloat16)
        .reshape(seq_count, length, local_heads, HEAD)
    )

    def attend_back(seq_no):
        seq_keys = keys_all[seq_no]
        seq_values = values_all[seq_no]
        seq_docs = doc_ids[seq_no]

        def block_step(carry, block_no):
            key_acc, value_acc = carry
            offset = block_no * block_rows
            query_blk = lax.dynamic_slice_in_dim(queries[seq_no], offset, block_rows, 0)
            grad_blk = lax.dynamic_slice_in_dim(grad_mixed[seq_no], offset, block_rows, 0)
            doc_query = lax.dynamic_slice_in_dim(seq_docs, offset, block_rows, 0)
            same_doc = doc_query[:, None] == seq_docs[None, :]
            scores = (
                jnp.einsum("qhd,khd->hqk", query_blk, seq_keys, preferred_element_type=jnp.float32)
                * factor
            )
            kept_total = log_totals[seq_no * blocks + block_no][..., None]
            soft_probs = jnp.where(same_doc[None], jnp.exp(scores - kept_total), 0.0)
            probs_b = soft_probs.astype(jnp.bfloat16)
            grad_prob = jnp.einsum(
                "qhd,khd->hqk", grad_blk, seq_values, preferred_element_type=jnp.float32
            )
            delta_row = jnp.sum(soft_probs * grad_prob, axis=-1, keepdims=True)
            grad_score = (soft_probs * (grad_prob - delta_row)).astype(jnp.bfloat16)
            grad_query = (
                jnp.einsum("hqk,khd->qhd", grad_score, seq_keys, preferred_element_type=jnp.float32)
                * factor
            )
            key_acc = (
                key_acc
                + jnp.einsum(
                    "hqk,qhd->khd", grad_score, query_blk, preferred_element_type=jnp.float32
                )
                * factor
            )
            value_acc = value_acc + jnp.einsum(
                "hqk,qhd->khd", probs_b, grad_blk, preferred_element_type=jnp.float32
            )
            return ((key_acc, value_acc), grad_query)

        zeros_kv = jnp.zeros(seq_keys.shape, jnp.float32)
        (grad_key, grad_value), grad_query = lax.scan(
            block_step, (zeros_kv, zeros_kv), jnp.arange(blocks)
        )
        return (grad_query.reshape(length, local_heads, HEAD), grad_key, grad_value)

    grad_query, grad_key, grad_value = lax.map(attend_back, jnp.arange(seq_count))
    grad_proj = (
        jnp.stack(
            [
                rotate_back(grad_query, cosine, sine),
                rotate_back(grad_key, cosine, sine),
                grad_value,
            ],
            axis=2,
        )
        .astype(jnp.bfloat16)
        .reshape(row_count, 3 * local_width)
    )
    grad_w_qkv = jnp.dot(h_attn.T, grad_proj, preferred_element_type=jnp.float32).reshape(
        model_width, 3, local_width
    )
    grad_h_attn = (
        lax.psum(
            jnp.dot(grad_proj, w_qkv_flat.T, preferred_element_type=jnp.float32).astype(
                jnp.bfloat16
            ),
            "mp",
        )
        .astype(jnp.float32)
        .reshape(seq_count, length, model_width)
    )
    grad_shift_one = jnp.sum(grad_h_attn, axis=1)
    grad_scale_one = jnp.sum(grad_h_attn * normed_one * gain_one, axis=1)
    grad_gain_one = jnp.sum(grad_h_attn * normed_one * (1.0 + scale_one), axis=(0, 1))
    grad_tokens = grad_mid + norm_back(
        grad_h_attn * gain_one * (1.0 + scale_one), normed_one, inv_one
    )
    grad_mod = jnp.stack(
        [
            grad_shift_one,
            grad_scale_one,
            grad_gate_one,
            grad_shift_two,
            grad_scale_two,
            grad_gate_two,
        ],
        axis=1,
    )
    grad_mod_b = grad_mod.reshape(seq_count, 6 * model_width).astype(jnp.bfloat16)
    share_cols = model_width // lax.axis_size("mp")
    owned = (jnp.arange(model_width, dtype=jnp.int32) // share_cols == mp_index)[None, :]
    head_rows = jnp.concatenate(
        [grad_gain_one[None], grad_gain_two[None], grad_down_bias[None], jnp.sum(grad_mod, axis=0)],
        axis=0,
    )
    per_device = hidden_local // model_width
    bias_rows = lax.dynamic_update_slice_in_dim(
        jnp.zeros((vec_master.shape[0] - 9, model_width), jnp.float32),
        grad_up_bias.reshape(per_device, model_width),
        mp_index * per_device,
        0,
    )
    grad_vec = lax.psum(
        jnp.concatenate([jnp.where(owned, head_rows, 0.0), bias_rows], axis=0), ("dp", "mp")
    )
    grad_w_ada = jnp.dot(cond_b.T, grad_mod_b, preferred_element_type=jnp.float32)
    sum_qkv, sum_proj, sum_up, sum_down, sum_ada = (
        lax.psum_scatter(grad_w_qkv, "dp", scatter_dimension=0, tiled=True),
        lax.psum_scatter(grad_w_proj, "dp", scatter_dimension=1, tiled=True),
        lax.psum_scatter(grad_w_up, "dp", scatter_dimension=0, tiled=True),
        lax.psum_scatter(grad_w_down, "dp", scatter_dimension=1, tiled=True),
        lax.psum_scatter(grad_w_ada, "dp", scatter_dimension=0, tiled=True),
    )
    qkv_up = adamw(qkv_master, qkv_first, qkv_second, sum_qkv, DECAY, RATE)
    proj_up = adamw(proj_master, proj_first, proj_second, sum_proj, DECAY, RATE)
    up_up = adamw(up_master, up_first, up_second, sum_up, DECAY, RATE)
    down_up = adamw(down_master, down_first, down_second, sum_down, DECAY, RATE)
    ada_up = adamw(ada_master, ada_first, ada_second, sum_ada, DECAY, RATE)
    vec_up = adamw(vec_master, vec_first, vec_second, grad_vec, 0.0, RATE_VEC)
    return (
        block_out,
        grad_tokens,
        qkv_up[0],
        qkv_up[1],
        qkv_up[2],
        proj_up[0],
        proj_up[1],
        proj_up[2],
        up_up[0],
        up_up[1],
        up_up[2],
        down_up[0],
        down_up[1],
        down_up[2],
        ada_up[0],
        ada_up[1],
        ada_up[2],
        vec_up[0],
        vec_up[1],
        vec_up[2],
    )


LEN_FAST = 1024
WIDTH = 768
COPIES = 400
VMEM_BYTES = 66 * 2**20
NT = (((1,), (1,)), ((), ()))
NN = (((1,), (0,)), ((), ()))
TN = (((0,), (0,)), ((), ()))
F32 = jnp.float32
BF16 = jnp.bfloat16
MESH = pl.DeviceIdType.MESH
SHARD = 96
QUARTER = 1152
STACK = (2, 4, 2, SHARD, WIDTH)
CHUNKS = (
    (0, 0, 256), (0, 256, 256), (0, 512, 256), (1, 0, 384), (1, 384, 384), (2, 0, 384), (2, 384, 384),
)
GATHER = (
    ((0, 16, "zxy"), (16, 32, "zyx"), (48, 16, "xyz"), (64, 32, "zxy")),
    ((0, 16, "zyx"), (16, 32, "zyx"), (48, 32, "zxy"), (80, 16, "zyx")),
    ((0, 32, "zxy"), (32, 16, "yxz"), (48, 32, "zyx"), (80, 16, "xyz")),
    ((0, 32, "zyx"), (32, 16, "yxz"), (48, 32, "zxy"), (80, 16, "zyx")),
    ((0, 16, "yxz"), (16, 16, "xzy"), (32, 16, "zyx"), (48, 48, "zxy")),
    ((0, 16, "zyx"), (16, 16, "zxy"), (32, 32, "zyx"), (64, 32, "xyz")),
    ((0, 32, "zxy"), (32, 32, "xyz"), (64, 16, "zyx"), (80, 16, "zyx")),
)
REDUCE = (
    ((0, 16, "zxy"), (16, 16, "xyz"), (32, 32, "zxy"), (64, 32, "yzx")),
    ((0, 16, "yxz"), (16, 16, "zyx"), (32, 48, "xyz"), (80, 16, "zyx")),
    ((0, 16, "zyx"), (16, 32, "yzx"), (48, 16, "yzx"), (64, 32, "xyz")),
    ((0, 32, "yzx"), (32, 32, "xyz"), (64, 16, "xyz"), (80, 16, "zyx")),
    ((0, 16, "xzy"), (16, 32, "yxz"), (48, 16, "yzx"), (64, 32, "zyx")),
    ((0, 16, "yxz"), (16, 48, "yzx"), (64, 16, "zyx"), (80, 16, "yzx")),
    ((0, 32, "zxy"), (32, 16, "yzx"), (48, 16, "xyz"), (64, 32, "yxz")),
)
PLAN = (
    (("I", "g", 0, 0, 0), ("I", "g", 0, 1, 0), ("I", "g", 0, 3, 0), ("I", "g", 0, 2, 0), ("I", "g", 1, 0, 0), ("I", "g", 2, 1, 0), ("I", "g", 2, 3, 0), ("I", "g", 3, 1, 0), ("I", "g", 4, 0, 0), ("I", "g", 4, 1, 0), ("I", "g", 5, 3, 0), ("I", "g", 6, 1, 0)),
    (),
    (("W", "g", 0, 2, 0), ("W", "g", 2, 1, 0), ("I", "g", 0, 2, 1), ("I", "g", 2, 1, 1)),
    (("W", "g", 2, 3, 0), ("I", "g", 2, 3, 1), ("W", "g", 3, 1, 0), ("I", "g", 3, 1, 1), ("W", "g", 4, 1, 0), ("W", "g", 4, 0, 0), ("I", "g", 4, 0, 1), ("W", "g", 5, 3, 0), ("I", "g", 5, 3, 1), ("W", "g", 6, 1, 0), ("I", "g", 6, 1, 1), ("W", "g", 0, 2, 1), ("W", "g", 2, 1, 1), ("W", "g", 2, 3, 1), ("I", "g", 1, 1, 0)),
    (),
    (("W", "g", 3, 1, 1), ("W", "g", 0, 0, 0), ("I", "g", 0, 0, 3), ("I", "g", 1, 2, 0), ("W", "g", 4, 0, 1), ("W", "g", 5, 3, 1), ("W", "g", 0, 1, 0), ("I", "g", 0, 1, 3), ("I", "g", 1, 3, 0), ("W", "g", 6, 1, 1), ("W", "g", 0, 3, 0), ("I", "g", 0, 3, 3), ("I", "g", 2, 0, 0), ("W", "g", 0, 0, 3), ("I", "g", 0, 0, 1), ("W", "g", 1, 0, 0), ("I", "g", 1, 0, 3), ("I", "g", 2, 2, 0), ("W", "g", 1, 1, 0), ("I", "g", 1, 1, 3), ("I", "g", 0, 2, 2), ("W", "g", 0, 1, 3), ("I", "g", 0, 1, 1), ("W", "g", 1, 2, 0), ("I", "g", 1, 2, 3), ("I", "g", 3, 0, 0), ("W", "g", 0, 3, 3), ("I", "g", 0, 3, 1), ("W", "g", 1, 0, 3), ("W", "g", 1, 3, 0), ("I", "g", 1, 0, 1), ("I", "g", 1, 3, 3), ("I", "g", 3, 2, 0)),
    (),
    (("W", "g", 0, 0, 1), ("I", "g", 0, 0, 2), ("W", "g", 2, 0, 0), ("I", "g", 2, 0, 3), ("I", "g", 3, 3, 0), ("W", "g", 1, 1, 3), ("I", "g", 1, 1, 1), ("W", "g", 2, 2, 0), ("I", "g", 2, 2, 3), ("I", "g", 4, 2, 0), ("W", "g", 1, 2, 3), ("W", "g", 0, 1, 1), ("I", "g", 0, 1, 2), ("I", "g", 1, 2, 1), ("W", "g", 1, 3, 3), ("I", "g", 1, 3, 1), ("W", "g", 1, 0, 1), ("I", "g", 1, 0, 2), ("W", "g", 0, 3, 1), ("I", "g", 0, 3, 2), ("W", "g", 2, 0, 3), ("I", "g", 2, 0, 1), ("W", "g", 0, 2, 2), ("I", "g", 0, 2, 5), ("I", "g", 4, 3, 0)),
    (("W", "g", 0, 0, 2), ("W", "g", 2, 2, 3), ("I", "g", 2, 2, 1)),
    (("W", "g", 3, 0, 0), ("W", "g", 1, 1, 1), ("I", "g", 1, 1, 2), ("I", "g", 3, 0, 3), ("I", "g", 4, 1, 1)),
    (("W", "g", 1, 3, 1), ("W", "g", 3, 2, 0), ("I", "g", 3, 2, 3), ("I", "g", 2, 1, 2), ("W", "g", 0, 1, 2), ("I", "g", 1, 3, 2), ("W", "g", 0, 2, 5), ("W", "g", 3, 3, 0), ("I", "g", 3, 3, 3), ("I", "g", 2, 3, 2), ("W", "g", 4, 2, 0), ("W", "g", 1, 2, 1), ("I", "g", 1, 2, 2), ("I", "g", 4, 2, 3), ("I", "g", 5, 0, 0), ("W", "g", 0, 3, 2)),
    (("W", "g", 3, 0, 3), ("W", "g", 1, 0, 2), ("W", "g", 3, 2, 3), ("W", "g", 3, 3, 3), ("W", "g", 2, 2, 1), ("W", "g", 4, 3, 0), ("I", "g", 2, 2, 2), ("I", "g", 4, 3, 3), ("I", "g", 3, 0, 1), ("I", "g", 3, 2, 1), ("I", "g", 3, 3, 1), ("I", "g", 5, 1, 0)),
    (("W", "g", 4, 2, 3), ("W", "g", 2, 0, 1), ("W", "g", 4, 1, 1), ("I", "g", 2, 0, 2), ("I", "g", 4, 1, 4), ("I", "g", 5, 2, 0)),
    (("W", "g", 1, 2, 2), ("W", "g", 1, 1, 2), ("W", "g", 2, 1, 2), ("W", "g", 4, 3, 3), ("I", "g", 2, 1, 5), ("I", "g", 4, 2, 1), ("I", "g", 4, 3, 1), ("I", "g", 3, 1, 2)),
    (("W", "g", 1, 3, 2),),
    (("W", "g", 3, 0, 1), ("W", "g", 4, 1, 4), ("W", "g", 2, 3, 2), ("W", "g", 3, 3, 1), ("W", "g", 5, 0, 0), ("I", "g", 5, 0, 3), ("I", "g", 2, 3, 5), ("I", "g", 3, 0, 2), ("I", "g", 3, 3, 2), ("I", "g", 6, 0, 0), ("I", "g", 6, 2, 0), ("I", "g", 4, 1, 2)),
    (("W", "g", 5, 1, 0), ("W", "g", 2, 1, 5), ("W", "g", 2, 2, 2), ("W", "g", 5, 2, 0), ("W", "g", 2, 0, 2), ("I", "g", 5, 1, 3), ("I", "g", 5, 2, 3), ("I", "g", 6, 3, 0), ("I", "g", 4, 0, 2)),
    (("W", "g", 5, 0, 3), ("W", "g", 3, 2, 1), ("W", "g", 4, 2, 1), ("W", "g", 2, 3, 5), ("I", "g", 3, 2, 2), ("I", "g", 4, 2, 2), ("I", "g", 5, 0, 1)),
    (),
    (("W", "g", 5, 1, 3), ("W", "g", 3, 1, 2), ("W", "g", 4, 1, 2), ("W", "g", 5, 2, 3), ("I", "g", 3, 1, 5), ("I", "g", 5, 1, 1), ("I", "g", 5, 2, 1), ("I", "g", 5, 3, 2)),
    (("W", "g", 4, 3, 1), ("W", "g", 6, 0, 0), ("W", "g", 6, 2, 0), ("W", "g", 6, 3, 0), ("I", "g", 6, 0, 3), ("I", "g", 6, 2, 3), ("I", "g", 6, 3, 3), ("I", "g", 4, 3, 2), ("I", "g", 6, 1, 2)),
    (("W", "g", 3, 1, 5),),
    (("W", "g", 3, 0, 2), ("W", "g", 3, 2, 2)),
    (("W", "g", 6, 0, 3), ("I", "g", 6, 0, 1), ("W", "g", 4, 0, 2), ("I", "g", 4, 0, 5), ("W", "g", 6, 2, 3), ("I", "g", 6, 2, 1), ("W", "g", 5, 0, 1), ("I", "g", 5, 0, 2), ("W", "g", 6, 3, 3), ("I", "g", 6, 3, 1)),
    (),
    (),
    (("W", "g", 3, 3, 2),),
    (),
    (),
    (),
    (("W", "g", 5, 2, 1), ("I", "g", 5, 2, 2)),
    (),
    (("W", "g", 4, 2, 2), ("W", "g", 4, 0, 5), ("W", "g", 5, 1, 1), ("I", "g", 5, 1, 2)),
    (("W", "g", 5, 3, 2), ("W", "g", 6, 0, 1), ("I", "g", 5, 3, 5)),
    (),
    (("I", "r", 5, 2, 0),),
    (("W", "g", 5, 0, 2), ("W", "g", 4, 3, 2), ("I", "g", 6, 0, 2)),
    (("W", "g", 6, 2, 1), ("I", "g", 6, 2, 2), ("I", "r", 5, 0, 0)),
    (("W", "g", 6, 3, 1), ("W", "g", 5, 3, 5), ("W", "g", 6, 1, 2), ("I", "g", 6, 1, 5), ("I", "g", 6, 3, 2), ("I", "r", 5, 1, 0)),
    (("W", "g", 5, 2, 2), ("W", "g", 5, 1, 2), ("I", "r", 5, 3, 0)),
    (("I", "r", 6, 0, 0), ("I", "r", 6, 2, 0)),
    (),
    (("W", "g", 6, 2, 2), ("W", "r", 5, 2, 0), ("I", "r", 5, 2, 3)),
    (("W", "g", 6, 3, 2), ("W", "g", 6, 0, 2), ("I", "r", 6, 1, 0)),
    (("I", "r", 3, 1, 0), ("I", "r", 3, 2, 0), ("I", "r", 3, 3, 0)),
    (("W", "g", 6, 1, 5),),
    (("W", "r", 6, 2, 0), ("W", "r", 5, 0, 0), ("W", "r", 5, 2, 3), ("I", "r", 5, 0, 1), ("I", "r", 5, 2, 1)),
    (),
    (("I", "r", 4, 0, 0), ("I", "r", 4, 3, 0)),
    (("W", "r", 6, 0, 0), ("I", "r", 6, 0, 3), ("I", "r", 4, 1, 0), ("I", "r", 4, 2, 0)),
    (("W", "r", 3, 1, 0), ("W", "r", 3, 3, 0), ("W", "r", 5, 1, 0), ("I", "r", 3, 3, 3), ("I", "r", 5, 1, 1), ("I", "r", 6, 3, 0)),
    (("W", "r", 3, 2, 0),),
    (),
    (),
    (("W", "r", 5, 0, 1), ("W", "r", 5, 3, 0), ("I", "r", 5, 3, 1), ("I", "r", 5, 0, 2), ("I", "r", 6, 2, 1)),
    (("I", "b", 0, 0, 0),),
    (),
    (),
    (),
    (("I", "b", 1, 0, 0),),
    (),
    (),
    (("W", "r", 6, 0, 3), ("W", "r", 4, 0, 0), ("W", "r", 6, 1, 0), ("I", "r", 6, 0, 1), ("I", "r", 3, 0, 0), ("I", "r", 3, 1, 1)),
    (("W", "r", 5, 2, 1), ("I", "r", 5, 2, 2), ("I", "b", 2, 0, 0)),
    (),
    (),
    (("W", "r", 3, 3, 3), ("W", "r", 4, 3, 0), ("I", "r", 4, 3, 3), ("I", "r", 4, 0, 1)),
    (("I", "b", 3, 0, 0),),
    (),
    (("W", "b", 0, 0, 0), ("W", "r", 4, 1, 0), ("I", "r", 4, 1, 1), ("I", "r", 3, 2, 1)),
    (("W", "r", 5, 1, 1), ("W", "r", 4, 2, 0), ("W", "r", 4, 3, 3), ("I", "r", 5, 1, 4), ("I", "r", 4, 2, 1), ("I", "r", 4, 3, 1), ("I", "r", 6, 1, 1)),
    (("W", "r", 5, 3, 1), ("W", "r", 5, 0, 2), ("W", "b", 1, 0, 0), ("I", "r", 5, 0, 5), ("I", "r", 5, 3, 4)),
    (("W", "r", 6, 0, 1), ("W", "r", 4, 0, 1), ("W", "r", 5, 2, 2), ("I", "r", 4, 0, 4)),
    (("W", "r", 6, 3, 0), ("W", "r", 4, 2, 1), ("W", "r", 6, 2, 1), ("W", "r", 5, 1, 4), ("I", "r", 4, 2, 4), ("I", "r", 5, 1, 2), ("I", "r", 6, 3, 1), ("I", "r", 6, 0, 2), ("I", "r", 6, 2, 2), ("I", "r", 3, 3, 1)),
    (("I", "r", 0, 0, 0), ("I", "r", 0, 1, 0), ("I", "r", 0, 2, 0)),
    (("W", "r", 5, 0, 5), ("W", "r", 6, 1, 1), ("W", "r", 5, 3, 4), ("W", "r", 4, 0, 4), ("W", "b", 2, 0, 0), ("I", "r", 6, 1, 4), ("I", "r", 5, 3, 2)),
    (("W", "r", 4, 2, 4), ("W", "r", 6, 2, 2), ("I", "r", 6, 2, 5), ("I", "r", 4, 2, 2)),
    (("W", "r", 3, 0, 0), ("W", "r", 6, 1, 4), ("I", "r", 0, 3, 0), ("I", "r", 6, 1, 2), ("I", "r", 3, 0, 1)),
    (("W", "r", 0, 0, 0), ("W", "b", 3, 0, 0), ("W", "r", 3, 1, 1), ("W", "r", 6, 2, 5), ("I", "r", 0, 0, 3), ("I", "r", 4, 0, 2), ("I", "r", 3, 1, 2)),
    (("W", "r", 3, 2, 1), ("W", "r", 4, 1, 1), ("W", "r", 4, 3, 1), ("I", "r", 4, 1, 2), ("I", "r", 4, 3, 2)),
    (("I", "r", 1, 0, 0), ("I", "r", 1, 2, 0)),
    (("W", "r", 6, 0, 2), ("W", "r", 5, 1, 2), ("W", "r", 3, 3, 1), ("W", "r", 0, 2, 0), ("W", "r", 0, 0, 3), ("I", "r", 0, 2, 3), ("I", "r", 1, 1, 0), ("I", "r", 0, 0, 1), ("I", "r", 3, 3, 2)),
    (("W", "r", 6, 3, 1), ("W", "r", 0, 3, 0)),
    (("W", "r", 4, 0, 2), ("W", "r", 0, 1, 0), ("W", "r", 3, 0, 1), ("W", "r", 5, 3, 2), ("W", "r", 4, 2, 2), ("W", "r", 6, 1, 2), ("W", "r", 4, 3, 2), ("W", "r", 1, 0, 0), ("I", "r", 3, 0, 4), ("I", "r", 1, 3, 0), ("I", "r", 1, 0, 1), ("I", "r", 0, 1, 1), ("I", "r", 0, 3, 1)),
    (("W", "r", 3, 1, 2), ("W", "r", 0, 2, 3), ("W", "r", 4, 1, 2), ("I", "r", 3, 1, 5), ("I", "r", 4, 1, 5), ("I", "r", 0, 2, 1), ("I", "r", 6, 3, 2)),
    (("W", "r", 0, 1, 1),),
    (("I", "r", 2, 1, 0), ("I", "r", 2, 2, 0), ("I", "r", 2, 3, 0)),
    (("W", "r", 1, 1, 0), ("W", "r", 1, 2, 0), ("W", "r", 3, 0, 4), ("W", "r", 0, 0, 1), ("W", "r", 3, 3, 2), ("W", "r", 3, 1, 5), ("W", "r", 1, 0, 1), ("I", "r", 1, 1, 3), ("I", "r", 1, 2, 1), ("I", "r", 1, 0, 2), ("I", "r", 0, 0, 2), ("I", "r", 0, 1, 2), ("I", "r", 3, 0, 2)),
    (),
    (("W", "r", 1, 3, 0), ("W", "r", 4, 1, 5), ("W", "r", 0, 2, 1), ("I", "r", 1, 3, 3), ("I", "r", 0, 2, 2)),
    (("I", "t", 0, 0, 0),),
    (),
    (("W", "r", 0, 3, 1), ("I", "r", 0, 3, 4), ("I", "r", 2, 0, 0)),
    (("I", "t", 1, 0, 0),),
    (),
    (("W", "r", 2, 1, 0), ("W", "r", 2, 3, 0), ("W", "r", 1, 1, 3), ("W", "r", 6, 3, 2), ("W", "r", 3, 0, 2), ("I", "r", 6, 3, 5), ("I", "r", 1, 1, 1), ("I", "r", 2, 1, 1), ("I", "r", 2, 3, 1), ("I", "r", 3, 2, 2)),
    (("W", "r", 1, 0, 2), ("W", "r", 2, 2, 0), ("I", "r", 1, 0, 5), ("I", "t", 2, 0, 0)),
    (),
    (("W", "r", 0, 1, 2), ("W", "r", 1, 3, 3), ("I", "r", 0, 1, 5), ("I", "r", 1, 3, 1), ("I", "r", 2, 2, 1)),
    (("I", "t", 3, 0, 0),),
    (("W", "r", 0, 3, 4), ("I", "r", 0, 3, 2)),
    (("W", "r", 1, 2, 1), ("W", "r", 0, 0, 2), ("W", "r", 0, 2, 2), ("W", "r", 2, 0, 0), ("I", "r", 2, 0, 3), ("W", "r", 1, 1, 1), ("I", "r", 1, 1, 2), ("W", "r", 6, 3, 5), ("W", "r", 1, 0, 5), ("W", "t", 0, 0, 0), ("W", "r", 0, 1, 5), ("W", "r", 2, 3, 1), ("W", "r", 2, 1, 1), ("W", "r", 1, 3, 1), ("I", "r", 2, 1, 4), ("I", "r", 1, 2, 2), ("I", "r", 1, 3, 2), ("W", "r", 3, 2, 2), ("I", "r", 3, 2, 5), ("I", "r", 2, 3, 2), ("W", "r", 2, 0, 3), ("I", "r", 2, 0, 1), ("W", "r", 2, 2, 1), ("I", "r", 2, 2, 4)),
    (("W", "t", 1, 0, 0), ("W", "r", 2, 1, 4), ("I", "r", 2, 1, 2), ("W", "r", 3, 2, 5), ("W", "r", 2, 0, 1), ("I", "r", 2, 0, 2), ("W", "r", 1, 2, 2), ("I", "r", 1, 2, 5), ("W", "r", 2, 2, 4), ("I", "r", 2, 2, 2), ("W", "r", 2, 3, 2), ("I", "r", 2, 3, 5)),
    (("W", "r", 1, 2, 5), ("W", "t", 2, 0, 0), ("W", "r", 2, 3, 5), ("W", "t", 3, 0, 0), ("W", "r", 0, 3, 2), ("W", "r", 1, 1, 2), ("W", "r", 1, 3, 2), ("W", "r", 2, 1, 2), ("W", "r", 2, 0, 2), ("W", "r", 2, 2, 2)),
    (),
)


def inbox_shapes():
    shapes = {}
    for chunk, (_, _, width) in enumerate(CHUNKS):
        for piece, (_, height, order) in enumerate(REDUCE[chunk]):
            for phase, axis in enumerate(order):
                extent = [
                    {"x": 2, "z": 4, "y": 2}[other] for other in "xzy" if other in order[phase + 1:]
                ]
                slots = (4,) if axis == "z" else (1,)
                shapes[chunk, piece, phase] = slots + tuple(extent) + (height, width)
    return shapes


INBOX = inbox_shapes()


def mm(left, right, dims):
    return lax.dot_general(left, right, dims, preferred_element_type=F32)


def norm_tile(values):
    centred = values - jnp.mean(values, axis=1, keepdims=True)
    inv = lax.rsqrt(jnp.mean(centred * centred, axis=1, keepdims=True) + EPS_NORM)
    return centred * inv, inv


def rows(index, size):
    return pl.ds(pl.multiple_of(index * size, size), size)


def lower_lanes(shape):
    return lax.broadcasted_iota(jnp.int32, shape, 1) < 64


def interleave(first, second):
    lower = lower_lanes(first.shape)
    left = jnp.where(lower, first, pltpu.roll(second, 64, 1))
    right = jnp.where(lower, pltpu.roll(first, 64, 1), second)
    return left, right


def step_kernel(
    time_ref, doc_ref, tokens, cotangent, qkv_h, proj_h, up_h, down_h, ada_h, vec_h, freq, theta,
    grads_out, stats_out, block_out, grad_out,
    wt, ada, modq, mod, wqk, wv, wp, tok, cot, h1, q, k, v, o, lse, cosine, sine, same, other, kt, vt,
    attn_own, attn_in, dh2_in, mlp_in,
    x1, h2, act, slope, dm, do, dzv, bo, bo_in, gt_in, g1, g2, st, dup, dup_acc, grads, acc, ka, va,
    qkv_m, proj_m, up_m, down_m, ada_m, vec, local_sem, send_sem, recv_sem, *inbox_refs,
):
    inbox = dict(zip(INBOX, inbox_refs))
    dp = lax.axis_index("dp")
    mp = lax.axis_index("mp")
    z, y, x, core = dp // 2, dp % 2, mp // 2, mp % 2
    own = {"x": x, "y": y, "z": z}

    def device(zz, yy, xx, cc):
        return (zz * 2 + yy, xx * 2 + cc)

    to_core = device(z, y, x, 1 - core)
    to_x = device(z, y, 1 - x, core)
    to_diag = device(z, y, 1 - x, 1 - core)
    to_y = device(z, 1 - y, x, core)
    z_next = [lax.rem(z + hop, 4) for hop in (1, 2, 3)]
    outer, inner = (z == 0) | (z == 3), (z == 1) | (z == 2)
    z_beside, z_other, z_across = z + 1 - 2 * (z % 2), lax.rem(z + 2, 4), 3 - z
    to_beside, to_other, to_across = [device(at, y, x, core) for at in (z_beside, z_other, z_across)]
    to_z = [device(place, y, x, core) for place in z_next]
    peers = {"x": (1 - x, to_x), "y": (1 - y, to_y)}
    counter = {"send": 0, "receive": 0}
    sent = []
    sent_inner = []
    sent_outer = []
    done = []

    def slots(side, count=1):
        counter[side] += count
        assert counter[side] <= COPIES
        return counter[side] - count

    def copy_of(src, dst, target, landing, starts=True):
        number = slots("send") if starts else 0
        return pltpu.make_async_remote_copy(
            src_ref=src, dst_ref=dst, send_sem=send_sem.at[number], recv_sem=recv_sem.at[landing],
            device_id=target, device_id_type=MESH,
        )

    def send(src, dst, target, landing=None):
        copy = copy_of(src, dst, target, slots("receive") if landing is None else landing)
        copy.start()
        sent.append(copy)
        return copy

    def arrive(copies):
        for copy in copies:
            copy.wait_recv()

    def flush(copies):
        for copy in copies:
            copy.wait_send()
            done.append(id(copy))

    barrier = pltpu.get_barrier_semaphore()
    partners = [to_core, to_x, to_diag, to_y] + to_z
    for partner in partners:
        pl.semaphore_signal(barrier, inc=1, device_id=partner, device_id_type=MESH)

    loads = [
        pltpu.make_async_copy(src, dst, local_sem.at[number])
        for number, (src, dst) in enumerate((
            (ada_h.at[:, pl.ds(pl.multiple_of(mp * QUARTER, 128), QUARTER)], ada_m), (qkv_h, qkv_m),
            (proj_h, proj_m), (up_h, up_m), (down_h, down_m), (vec_h, vec), (tokens.at[x], tok),
            (cotangent.at[x], cot),
        ))
    ]
    for load in loads:
        load.start()

    loads[0].wait()
    ada[z, y] = ada_m[...].astype(BF16)
    loads[1].wait()
    loads[2].wait()
    proj_t = jnp.transpose(proj_m[...])
    wt[0, x, z, y] = jnp.concatenate(
        [
            part[:, 64 * head:64 * head + 64]
            for head in range(3) for part in (qkv_m[0], qkv_m[1], qkv_m[2], proj_t)
        ],
        axis=1,
    ).astype(BF16)
    loads[3].wait()
    wt[1, x, z, y] = up_m[...].astype(BF16)
    loads[4].wait()
    wt[2, x, z, y] = down_m[...].astype(BF16)
    loads[5].wait()
    pl.semaphore_wait(barrier, len(partners))

    def view(ref, fixed, height, columns):
        index = [fixed.get(axis, slice(None)) for axis in "xzy"]
        return ref.at[(*index, height, columns)]

    flying = {}
    sources = [wt.at[1], g1, g2]

    def gather(chunk, piece, phase):
        tensor, start, width = CHUNKS[chunk]
        first_row, height, order = GATHER[chunk][piece]
        axis = order[phase]
        fixed = {name: own[name] for name in order[phase:]}

        def block(at):
            return view(
                wt.at[tensor], {**fixed, axis: at}, pl.ds(first_row, height), pl.ds(start, width)
            )

        mine = block(own[axis])
        if axis != "z":
            return [send(mine, mine, peers[axis][1])]
        beside, other = send(mine, mine, to_beside), send(mine, mine, to_other)
        landing = slots("receive")
        across = copy_of(mine, mine, to_across, landing)
        passed = block(z_other)
        onward = copy_of(passed, passed, to_beside, landing)
        pl.when(inner)(across.start)
        sent_inner.extend((across, onward))
        return [beside, other, across, onward]

    def reduce(chunk, piece, phase):
        tensor, start, width = CHUNKS[chunk]
        first_row, height, order = REDUCE[chunk][piece]
        axis = order[phase]
        fixed = {name: own[name] for name in order[:phase]}
        landing = inbox[chunk, piece, phase]

        def block(at):
            return view(
                sources[tensor], {**fixed, axis: at}, pl.ds(first_row, height), pl.ds(start, width)
            )

        if axis != "z":
            at, target = peers[axis]
            return [send(block(at), landing.at[0], target)]
        beside = send(block(z_beside), landing.at[0], to_beside)
        number = slots("receive", 3)
        at = jnp.where(outer, z_other, z_across)
        kind = jnp.where(outer, 0, 1)
        direct = send(block(at), landing.at[1 + kind], device(at, y, x, core), number + kind)
        given = copy_of(block(z_across), landing.at[3], to_beside, number + 2)
        pl.when(outer)(given.start)
        sent_outer.append(given)
        total = copy_of(block(z_other), landing.at[1], to_other, number)
        sent_inner.append(total)
        waits = [
            copy_of(block(z_other), landing.at[1 + slot], to_other, number + slot, False) for slot in (0, 1)
        ]
        return [beside, waits[0], waits[1], given, total]

    def take(kind, chunk, piece, phase):
        tensor, start, width = CHUNKS[chunk]
        first_row, height, order = (GATHER if kind == "g" else REDUCE)[chunk][piece]
        axis = order[phase % 3]
        copies = flying[kind, chunk, piece, phase % 3]
        if kind == "g":
            if axis != "z":
                arrive(copies)
            elif phase < 3:
                arrive(copies[:2])
                pl.when(inner)(copies[3].start)
            else:
                arrive(copies[2:3])
            return
        landing = inbox[chunk, piece, phase % 3]
        source = sources[tensor]

        def place(at):
            fixed = {**{name: own[name] for name in order[:phase % 3]}, axis: at}
            index = [fixed.get(name, slice(None)) for name in "xzy"]
            return (*index, pl.ds(first_row, height), pl.ds(start, width))

        target = place(own[axis])
        if axis != "z":
            arrive(copies)
            total = source[target].astype(F32) + landing[0].astype(F32)
        elif phase < 3:
            arrive(copies[:1])

            @pl.when(inner)
            def _():
                arrive(copies[1:4])
                target = place(z_other)
                source[target] = (source[target].astype(F32) + landing[3].astype(F32)).astype(BF16)
                copies[4].start()

            return
        else:

            @pl.when(outer)
            def _():
                arrive(copies[1:2])

            total = source[target].astype(F32) + landing[0].astype(F32) + landing[1].astype(F32)
            across = landing[jnp.where(inner, 2, 0)].astype(F32)
            total = total + across * jnp.where(inner, 1.0, 0.0)
        if phase % 3 == 2:
            grads[tensor, pl.ds(first_row, height), pl.ds(start, width)] = total
        else:
            source[target] = total.astype(BF16)

    def cross(ref, landing, part):
        piece = pl.ds(pl.multiple_of(part * 256 + core * 128, 128), 128)
        return [send(ref.at[piece, :], landing.at[piece, :], to_x)]

    def share(landing, part):
        piece = landing.at[pl.ds(pl.multiple_of(part * 256 + core * 128, 128), 128), :]
        shared.append(send(piece, piece, to_core))

    shared = []
    outputs = {"b": (bo, bo_in), "t": (slope.at[0], gt_in)}
    position = [0]

    def serve():
        for action, kind, chunk, piece, phase in PLAN[position[0]]:
            if action == "I":
                if phase < 3:
                    begin = {"g": gather, "r": reduce}.get(kind)
                    flying[kind, chunk, piece, phase] = (
                        begin(chunk, piece, phase) if begin else cross(*outputs[kind], chunk)
                    )
            elif kind in "gr":
                take(kind, chunk, piece, phase)
            else:
                arrive(flying[kind, chunk, piece, phase])
                share(outputs[kind][1], chunk)
        position[0] += 1

    own_ada = ada.at[z, y]
    ada_one = [send(own_ada, own_ada, target) for target in to_z]
    serve()

    row_id = lax.broadcasted_iota(jnp.int32, (16, 128), 0)
    lane_id = lax.broadcasted_iota(jnp.int32, (16, 128), 1)
    steps = jnp.where(row_id == 0, time_ref[0], time_ref[1]).astype(F32)
    angles = steps * freq[0:1, :]
    cond = jnp.where(lane_id < 64, jnp.cos(angles), jnp.sin(angles)).astype(BF16)

    ends = []
    total = 0
    for number in range(4):
        total = total + doc_ref[x, number]
        ends.append(total)
    serve()

    def tables(index):
        block = rows(index, 128)
        token_id = lax.broadcasted_iota(jnp.int32, (128, 128), 0) + index * 128
        lanes = lax.broadcasted_iota(jnp.int32, (128, 128), 1)
        document = sum((token_id >= end).astype(jnp.int32) for end in ends)
        place = lax.rem(lanes, 64)
        same[block, :] = jnp.where(place == document, 1.0, 0.0).astype(BF16)
        apart = jnp.where((place < 4) & (place != document), NEG_BIG, 0.0)
        other[block, :] = jnp.where((place >= 4) & (place < 7), 1.0, apart).astype(BF16)
        begin = jnp.zeros((128, 128), jnp.int32)
        for end in ends[:3]:
            begin = jnp.where(token_id >= end, end, begin)
        turned = (token_id - begin).astype(F32) * theta[0:1, :]
        cosine[block, :] = jnp.cos(turned)
        turned_sine = jnp.sin(turned)
        sine[block, :] = jnp.where(lax.rem(lanes, 64) < 32, -turned_sine, turned_sine)

    pl.loop(0, 8)(tables)
    serve()
    serve()
    arrive(ada_one)
    own_ada = ada.at[:, y]
    ada_two = [send(own_ada, own_ada, to_y)]
    serve()
    serve()
    arrive(ada_two)
    modq[mp] = mm(cond, ada[...].reshape(COND, QUARTER), NN)[0:8]
    own_mod = modq.at[mp]
    mod_copies = [send(own_mod, own_mod, target) for target in (to_core, to_x, to_diag)]
    serve()
    serve()
    arrive(mod_copies)
    own_row = pl.ds(x, 1)
    half_width = WIDTH // 2
    mod[0:1, :] = modq[0, own_row, 0:WIDTH] + vec[3:4, :]
    mod[1:2, :] = (
        jnp.concatenate([modq[0, own_row, WIDTH:QUARTER], modq[1, own_row, 0:half_width]], axis=1)
        + vec[4:5, :]
    )
    mod[2:3, :] = modq[1, own_row, half_width:QUARTER] + vec[5:6, :]
    mod[3:4, :] = modq[2, own_row, 0:WIDTH] + vec[6:7, :]
    mod[4:5, :] = (
        jnp.concatenate([modq[2, own_row, WIDTH:QUARTER], modq[3, own_row, 0:half_width]], axis=1)
        + vec[7:8, :]
    )
    mod[5:6, :] = modq[3, own_row, half_width:QUARTER] + vec[8:9, :]

    loads[6].wait()
    loads[7].wait()

    for part in range(2):

        @pl.loop(part * 2, part * 2 + 2)
        def _(index):
            block = rows(index, 256)
            normed, _ = norm_tile(tok[block, :].astype(F32))
            h1[block, :] = (normed * (vec[0:1, :] * (1.0 + mod[1:2, :])) + mod[0:1, :]).astype(BF16)
            dm[block, :] = (cot[block, :].astype(F32) * mod[5:6, :]).astype(BF16)

        serve()

    def rotate(tile, block):
        lanes = lax.broadcasted_iota(jnp.int32, tile.shape, 1)
        swapped = jnp.where(
            lax.rem(lanes, 64) < 32, pltpu.roll(tile, 96, 1), pltpu.roll(tile, 32, 1)
        )
        return tile * cosine[block, :] + swapped * sine[block, :]

    def rotate_transposed(tile, block):
        lanes = lax.broadcasted_iota(jnp.int32, tile.shape, 1)
        turned = tile * sine[block, :]
        swapped = jnp.where(
            lax.rem(lanes, 64) < 32, pltpu.roll(turned, 96, 1), pltpu.roll(turned, 32, 1)
        )
        return tile * cosine[block, :] + swapped

    def project(pair):
        start = 256 * pair
        tiles = [
            [
                wt[0, side, :, :, :, start + 128 * part:start + 128 * part + 128].reshape(WIDTH, 128)
                for part in (0, 1)
            ]
            for side in (0, 1)
        ]
        cols = slice(pair * 128, pair * 128 + 128)
        both = slice(pair * 256, pair * 256 + 256)
        left, right = interleave(tiles[0][0], tiles[1][0])
        wqk[:, both] = jnp.concatenate([left, right], axis=1)
        wv[:, cols], wp[:, cols] = interleave(tiles[0][1], tiles[1][1])

        @pl.loop(0, LEN_FAST // 256)
        def _(index):
            block = rows(index, 256)
            full = mm(h1[block, :], wqk[:, both], NN)
            turned = rotate(full[:, 0:128], block).astype(BF16)
            q[block, cols] = (turned.astype(F32) * 0.125).astype(BF16)
            k[block, cols] = rotate(full[:, 128:256], block).astype(BF16)
            v[block, cols] = mm(h1[block, :], wv[:, cols], NN).astype(BF16)

    def own_half(shape, head):
        lower = lower_lanes(shape)
        return lower if head == 0 else ~lower

    def keep_head(tile, head):
        return jnp.where(own_half(tile.shape, head), tile, jnp.zeros_like(tile))

    def head_tiles(pair):
        cols = slice(pair * 128, pair * 128 + 128)
        for head in range(2):
            mine = own_half((LEN_FAST, 128), head)
            kt[head] = jnp.where(mine, k[:, cols], other[...])
            vt[head] = jnp.where(mine, v[:, cols], jnp.ones((LEN_FAST, 128), BF16))

    def beside(tile, values):
        place = lax.rem(lax.broadcasted_iota(jnp.int32, tile.shape, 1), 64)
        for number in range(3):
            term = values.astype(BF16)
            values = values - term.astype(F32)
            tile = jnp.where(place == 4 + number, term, tile)
        return tile

    def attend(pair, part):
        cols = slice(pair * 128, pair * 128 + 128)
        block = slice(512 * part, 512 * part + 512)
        if part == 0:
            head_tiles(pair)
        mixed = []
        for head in range(2):
            mine = own_half((512, 128), head)
            scores = mm(jnp.where(mine, q[block, cols], same[block, :]), kt[head], NT)
            top = jnp.max(scores, axis=1, keepdims=True)
            total = mm(jnp.exp(scores - top).astype(BF16), vt[head], NN)
            mixed.append(total * (1.0 / pltpu.roll(total, 64, 1)))
            number = 2 * pair + head
            beyond = 64 - 64 * head
            lse[block, number:number + 1] = top + jnp.log(total[:, beyond:beyond + 1])
        o[block, cols] = jnp.where(lower_lanes((512, 128)), mixed[0], mixed[1]).astype(BF16)

    for pair in range(3):
        serve()
        project(pair)
        serve()
        attend(pair, 0)
        serve()
        attend(pair, 1)
        serve()

    def swap(own_ref, incoming, make):
        copies = []
        for index in range(4):
            block = slice(index * 256, index * 256 + 256)
            own_ref[block, :] = make(block).astype(BF16)
            piece = pl.ds(index * 256, 256)
            copies.append(send(own_ref.at[piece, :], incoming.at[piece, :], to_core))
        return copies

    attn_copies = swap(attn_own, attn_in, lambda block: mm(o[block, :], wp[...], NT))
    serve()

    for part in range(4):
        serve()
        attn_copies[part].wait_recv()

        @pl.loop(part, part + 1)
        def _(index):
            block = rows(index, 256)
            attn = attn_own[block, :].astype(F32) + attn_in[block, :].astype(F32)
            middle = tok[block, :].astype(F32) + mod[2:3, :] * attn
            x1[block, :] = middle
            normed, _ = norm_tile(middle)
            h2[block, :] = (normed * (vec[1:2, :] * (1.0 + mod[4:5, :])) + mod[3:4, :]).astype(BF16)

        serve()

    def raise_hidden(half):
        cols = slice(384 * half, 384 * half + 384)
        for side in range(2):

            @pl.loop(0, LEN_FAST // 512)
            def _(index):
                block = rows(index, 512)
                bias = vec[pl.ds(9 + 2 * side + core, 1), cols]
                u = mm(h2[block, :], wt[1, side, :, :, :, cols].reshape(WIDTH, 384), NN) + bias
                square = u * u
                bent = jnp.tanh(u * (0.7978845608028654 + 0.03567740813636141 * square))
                half_u = 0.5 * u
                act[side, block, cols] = (half_u + half_u * bent).astype(BF16)
                rising = half_u * (0.7978845608028654 + 0.10703222440908423 * square)
                slope[side, block, cols] = (
                    0.5 + 0.5 * bent + (1.0 - bent * bent) * rising
                ).astype(BF16)

            serve()

        for side in range(2):
            grad = mm(dm[...], act[side, :, cols], TN).astype(BF16)
            g2[side, :, :, :, cols] = grad.reshape(4, 2, SHARD, 384)

    for half in range(2):
        serve()
        raise_hidden(half)
        serve()
        serve()

    def lower_hidden(half):
        cols = slice(384 * half, 384 * half + 384)
        for side in range(2):

            @pl.loop(0, LEN_FAST // 512)
            def _(index):
                block = rows(index, 512)
                back = mm(dm[block, :], wt[2, side, :, :, :, cols].reshape(WIDTH, 384), NN)
                grad = (back * slope[side, block, cols].astype(F32)).astype(BF16)
                slope[side, block, cols] = grad
                dup_acc[side, :, cols] = dup_acc[side, :, cols] + jnp.sum(
                    grad.astype(F32).reshape(64, 8, 384), axis=0
                )

        serve()
        for side in range(2):
            grad = mm(h2[...], slope[side, :, cols], TN).astype(BF16)
            g1[side, :, :, :, cols] = grad.reshape(4, 2, SHARD, 384)

    dup_acc[...] = jnp.zeros_like(dup_acc)
    for half in range(2):
        serve()
        lower_hidden(half)
        serve()
        serve()

    def back_two(block):
        return mm(slope[0, block, :], wt[1, 0].reshape(WIDTH, WIDTH), NT) + mm(
            slope[1, block, :], wt[1, 1].reshape(WIDTH, WIDTH), NT
        )

    dh2_own, mlp_own = slope.at[0], act.at[0]
    dh2_copies = swap(dh2_own, dh2_in, back_two)
    serve()

    def forward_two(block):
        return mm(act[0, block, :], wt[2, 0].reshape(WIDTH, WIDTH), NT) + mm(
            act[1, block, :], wt[2, 1].reshape(WIDTH, WIDTH), NT
        )

    mlp_copies = swap(mlp_own, mlp_in, forward_two)
    serve()

    dup[0] = jnp.zeros((8, WIDTH), F32)
    for side in range(2):
        dup[0, side:side + 1, :] = jnp.sum(dup_acc[side], axis=0, keepdims=True)
    dup_copy = send(dup.at[0], dup.at[1], to_core)
    serve()

    acc[...] = jnp.zeros_like(acc)

    def add_row(row, values):
        count = values.shape[0]
        acc[row] = acc[row] + jnp.sum(values.reshape(count // 8, 8, WIDTH), axis=0)

    for part in range(4):
        serve()
        dh2_copies[part].wait_recv()
        serve()
        mlp_copies[part].wait_recv()

        @pl.loop(part * 2, part * 2 + 2)
        def _(index):
            block = rows(index, 128)
            middle = x1[block, :]
            seen = cot[block, :].astype(F32)
            mlp = mlp_own[block, :].astype(F32) + mlp_in[block, :].astype(F32) + vec[2:3, :]
            bo[block, :] = (middle + mod[5:6, :] * mlp).astype(BF16)
            add_row(3, seen * mlp)
            add_row(4, seen)
            back = dh2_own[block, :].astype(F32) + dh2_in[block, :].astype(F32)
            normed, inv = norm_tile(middle)
            add_row(0, back)
            add_row(1, back * normed)
            scaled = back * (vec[1:2, :] * (1.0 + mod[4:5, :]))
            grad = seen + inv * (
                scaled - jnp.mean(scaled, axis=1, keepdims=True)
                - normed * jnp.mean(scaled * normed, axis=1, keepdims=True)
            )
            x1[block, :] = grad
            attn = attn_own[block, :].astype(F32) + attn_in[block, :].astype(F32)
            add_row(2, grad * attn)
            dm[block, :] = (grad * mod[2:3, :]).astype(BF16)

        serve()
        serve()

    bo_store = pltpu.make_async_copy(bo, block_out.at[x], local_sem.at[8])
    bo_store.start()

    @pl.loop(0, LEN_FAST // 256)
    def _(index):
        block = rows(index, 256)
        do[block, :] = mm(dm[block, :], wp[...], NN).astype(BF16)

    for key, copies in flying.items():
        if key[:2] in (("g", 3), ("g", 4)):
            flush([copy for copy in copies if any(copy is other for other in sent)])
            inner_copies = [copy for copy in copies if any(copy is other for other in sent_inner)]
            done.extend(id(copy) for copy in inner_copies)

            @pl.when(inner)
            def _():
                for copy in inner_copies:
                    copy.wait_send()

    g0 = sources[0]
    dzqk = h2

    def attend_back(pair, index):
        cols = slice(pair * 128, pair * 128 + 128)
        both = 256 * pair
        if index == 0:
            head_tiles(pair)
        begin, end = max(0, index - 2) * 256, min(4, index + 3) * 256
        keys = slice(begin, end)
        block = slice(256 * index, 256 * index + 256)
        query = q[block, cols]
        back = do[block, cols]
        product = back.astype(F32) * o[block, cols].astype(F32)
        grad_q = []
        for head in range(2):
            number = 2 * pair + head
            mine = own_half(query.shape, head)
            queries = jnp.where(mine, query, beside(same[block, :], -lse[block, number:number + 1]))
            probs = jnp.exp(mm(queries, kt[head, keys, :], NT))
            delta = jnp.sum(keep_head(product, head), axis=1, keepdims=True)
            backs = jnp.where(mine, back, beside(jnp.zeros_like(back), -delta))
            grad_s = (probs * mm(backs, vt[head, keys, :], NT)).astype(BF16)
            grad_q.append(mm(grad_s, k[keys, cols], NN))
            ka[keys, :] += mm(grad_s, keep_head(query, head), TN)
            va[keys, :] += mm(probs.astype(BF16), keep_head(back, head), TN)
        full = jnp.where(lower_lanes(grad_q[0].shape), grad_q[0], grad_q[1]) * 0.125
        dzqk[block, both:both + 128] = rotate_transposed(full, block).astype(BF16)

    grad_p = mm(dm[...], o[...], TN).astype(BF16)
    for pair in range(3):
        g0[0, :, :, :, 256 * pair + 128:256 * pair + 256] = grad_p[
            :, 128 * pair:128 * pair + 128
        ].reshape(4, 2, SHARD, 128)

    def finish(pair):
        cols = slice(pair * 128, pair * 128 + 128)
        start = 256 * pair
        dzqk[:, start + 128:start + 256] = rotate_transposed(ka[...], pl.ds(0, LEN_FAST)).astype(BF16)
        dzv[:, cols] = va[...].astype(BF16)

    def head_grads(pair):
        cols = slice(pair * 128, pair * 128 + 128)
        start = 256 * pair
        grad_qk = mm(h1[...], dzqk[:, start:start + 256], TN).astype(BF16)
        grad_v = mm(h1[...], dzv[:, cols], TN).astype(BF16)
        held = g0[0, :, :, :, start + 128:start + 256].reshape(WIDTH, 128)
        for number, (first, second) in enumerate(
            ((grad_qk[:, 0:128], grad_qk[:, 128:256]), (grad_v, held))
        ):
            sides = interleave(first, second)
            place = start + 128 * number
            for side in range(2):
                g0[side, :, :, :, place:place + 128] = sides[side].reshape(4, 2, SHARD, 128)

    def clear():
        ka[...] = jnp.zeros_like(ka)
        va[...] = jnp.zeros_like(va)

    serve()
    for pair in range(3):
        clear()
        for index in range(4):
            attend_back(pair, index)
            serve()
        finish(pair)
        head_grads(pair)
        serve()
        serve()

    def back_one(block):
        return mm(dzqk[block, :], wqk[...], NT) + mm(dzv[block, :], wv[...], NT)

    flush(dh2_copies)
    flush(mlp_copies)
    gt = slope.at[0]
    dh1_copies = swap(act.at[0], act.at[1], back_one)
    serve()
    for part in range(4):
        serve()
        dh1_copies[part].wait_recv()

        @pl.loop(part * 2, part * 2 + 2)
        def _(index):
            block = rows(index, 128)
            back = act[0, block, :].astype(F32) + act[1, block, :].astype(F32)
            normed, inv = norm_tile(tok[block, :].astype(F32))
            add_row(5, back)
            add_row(6, back * normed)
            scaled = back * (vec[0:1, :] * (1.0 + mod[1:2, :]))
            gt[block, :] = (
                x1[block, :] + inv * (
                    scaled - jnp.mean(scaled, axis=1, keepdims=True)
                    - normed * jnp.mean(scaled * normed, axis=1, keepdims=True)
                )
            ).astype(BF16)

        serve()
        serve()

    gt_store = pltpu.make_async_copy(gt, grad_out.at[x], local_sem.at[9])
    gt_store.start()

    sums = [jnp.sum(acc[row], axis=0, keepdims=True) for row in range(7)]
    shift2, prod2, gate1, gate2, seen, shift1, prod1 = sums
    dup_copy.wait_recv()
    first_rows = jnp.where(core == 0, dup[0], dup[1])
    second_rows = jnp.where(core == 0, dup[1], dup[0])
    cond_row = jnp.where(x == 0, cond[0:1, :].astype(F32), cond[1:2, :].astype(F32))
    st[x, z, y] = jnp.concatenate(
        [
            shift1, prod1 * vec[0:1, :], gate1, shift2, prod2 * vec[1:2, :], gate2,
            prod1 * (1.0 + mod[1:2, :]), prod2 * (1.0 + mod[4:5, :]), seen * mod[5:6, :],
            jnp.concatenate([cond_row, jnp.zeros((1, WIDTH - 128), F32)], axis=1),
            first_rows[0:1, :], second_rows[0:1, :], first_rows[1:2, :], second_rows[1:2, :],
            jnp.zeros((2, WIDTH), F32),
        ],
        axis=0,
    ).astype(BF16)
    half_cols = pl.ds(pl.multiple_of(core * 384, 128), 384)
    own_stats = st.at[x, z, y, :, half_cols]
    stats_one = [send(own_stats, own_stats, target) for target in to_z]
    serve()
    serve()
    arrive(stats_one)
    own_stats = st.at[x, :, y, :, half_cols]
    stats_two = [send(own_stats, own_stats, to_y)]
    serve()
    arrive(stats_two)
    own_stats = st.at[x, :, :, :, half_cols]
    stats_three = [send(own_stats, own_stats, to_x)]
    serve()
    grads_store = pltpu.make_async_copy(grads, grads_out, local_sem.at[10])
    grads_store.start()
    arrive(shared)
    bo_rest = pltpu.make_async_copy(bo_in, block_out.at[1 - x], local_sem.at[12])
    gt_rest = pltpu.make_async_copy(gt_in, grad_out.at[1 - x], local_sem.at[13])
    bo_rest.start()
    gt_rest.start()
    serve()
    arrive(stats_three)
    own_stats = st.at[:, :, :, :, half_cols]
    arrive([send(own_stats, own_stats, to_core)])
    stats_store = pltpu.make_async_copy(st, stats_out, local_sem.at[11])
    stats_store.start()
    assert position[0] == len(PLAN)
    for copy in sent:
        if id(copy) not in done:
            copy.wait_send()

    @pl.when(inner)
    def _():
        for copy in sent_inner:
            if id(copy) not in done:
                copy.wait_send()

    @pl.when(outer)
    def _():
        for copy in sent_outer:
            copy.wait_send()

    for store in (bo_store, gt_store, grads_store, stats_store, bo_rest, gt_rest):
        store.wait()


def update_kernel(
    grads, stats, blocks_in, gt,
    qkv_m, qkv_f, qkv_s, proj_m, proj_f, proj_s, up_m, up_f, up_s, down_m, down_f, down_s,
    ada_m, ada_f, ada_s, vec_m, vec_f, vec_s,
    blocks_out, gt_out,
    qkv_mo, qkv_fo, qkv_so, proj_mo, proj_fo, proj_so, up_mo, up_fo, up_so, down_mo, down_fo, down_so,
    ada_mo, ada_fo, ada_so, vec_mo, vec_fo, vec_so,
    proj_grad, ada_grad,
):
    step = pl.program_id(0)
    blocks_out[...] = blocks_in[...]
    gt_out[...] = gt[...].astype(F32)

    def put(refs, outs, gradient, decay, rate, index=...):
        new = adamw(refs[0][index], refs[1][index], refs[2][index], gradient, decay, rate)
        for out, value in zip(outs, new):
            out[index] = value

    def columns(part):
        return jnp.concatenate(
            [grads[0, :, 256 * head + 64 * part:256 * head + 64 * part + 64] for head in range(3)], axis=1
        )

    for part in range(3):
        put((qkv_m, qkv_f, qkv_s), (qkv_mo, qkv_fo, qkv_so), columns(part), DECAY, RATE, part)
    put((up_m, up_f, up_s), (up_mo, up_fo, up_so), grads[1], DECAY, RATE)
    put((down_m, down_f, down_s), (down_mo, down_fo, down_so), grads[2], DECAY, RATE)
    proj_grad[rows(step, SHARD // 2), :] = columns(3)

    every = stats[...].reshape(16, 16, WIDTH)
    cond = every[:, 9, 0:COND]
    for number in range(2):

        @pl.when(step == number)
        def _():
            moved = jnp.concatenate([every[:, 3 * number + part, :] for part in range(3)], axis=1)
            ada_grad[...] = mm(cond, moved, TN)

    own_rows = pl.ds(pl.multiple_of(lax.axis_index("dp") * 16, 16), 16)
    put((ada_m, ada_f, ada_s), (ada_mo, ada_fo, ada_so), ada_grad[own_rows, :], DECAY, RATE)

    @pl.when(step == 1)
    def _():
        put(
            (proj_m, proj_f, proj_s), (proj_mo, proj_fo, proj_so), jnp.transpose(proj_grad[...]),
            DECAY, RATE,
        )
        total = jnp.sum(every.astype(F32), axis=0)
        gradient = jnp.concatenate([total[6:9], total[0:6], total[10:14]], axis=0)
        put((vec_m, vec_f, vec_s), (vec_mo, vec_fo, vec_so), gradient, 0.0, RATE_VEC)


def fast_shards(
    tokens, cotangent, doc_lengths, time_steps,
    qkv_master, qkv_first, qkv_second, proj_master, proj_first, proj_second,
    up_master, up_first, up_second, down_master, down_first, down_second,
    ada_master, ada_first, ada_second, vec_master, vec_first, vec_second,
):
    freq = np.tile(np.exp(-np.log(10000.0) * np.arange(64) / 64).astype(np.float32), (8, 2))
    theta = np.tile(np.exp(-np.log(ROPE_BASE) * np.arange(32) * 2.0 / HEAD).astype(np.float32), (8, 4))
    vmem = pl.BlockSpec(memory_space=pltpu.VMEM)
    smem = pl.BlockSpec(memory_space=pltpu.SMEM)
    anywhere = pl.BlockSpec(memory_space=pl.ANY)
    tall = (LEN_FAST, WIDTH)
    third = (LEN_FAST, 384)
    buffers = [
        ((3,) + STACK, BF16),
        ((4, 2, 16, QUARTER), BF16),
        ((4, 8, QUARTER), F32),
        ((8, WIDTH), F32),
        ((WIDTH, WIDTH), BF16), ((WIDTH, 384), BF16), ((WIDTH, 384), BF16),
        (tall, BF16), (tall, BF16), (tall, BF16),
        (third, BF16), (third, BF16), (third, BF16), (third, BF16),
        ((LEN_FAST, 128), F32),
        ((LEN_FAST, 128), F32), ((LEN_FAST, 128), F32),
        ((LEN_FAST, 128), BF16), ((LEN_FAST, 128), BF16),
        ((2, LEN_FAST, 128), BF16), ((2, LEN_FAST, 128), BF16),
        (tall, BF16), (tall, BF16),
        (tall, BF16), (tall, BF16),
        (tall, F32),
        (tall, BF16),
        ((2,) + tall, BF16), ((2,) + tall, BF16),
        (tall, BF16),
        (third, BF16), (third, BF16),
        (tall, BF16), (tall, BF16), (tall, BF16),
        (STACK, BF16), (STACK, BF16),
        ((2, 4, 2, 16, WIDTH), BF16),
        ((2, 8, WIDTH), F32), ((2, 8, WIDTH), F32),
        ((3, SHARD, WIDTH), F32),
        ((8, 8, WIDTH), F32),
        ((LEN_FAST, 128), F32), ((LEN_FAST, 128), F32),
    ]
    turned_qkv = [jnp.transpose(a, (1, 0, 2)) for a in (qkv_master, qkv_first, qkv_second)]
    turned_down = [a.T for a in (down_master, down_first, down_second)]
    grads, stats, blocks, grad_tokens = pl.pallas_call(
        step_kernel,
        out_shape=[
            jax.ShapeDtypeStruct((3, SHARD, WIDTH), F32),
            jax.ShapeDtypeStruct((2, 4, 2, 16, WIDTH), BF16),
            jax.ShapeDtypeStruct((2,) + tall, BF16),
            jax.ShapeDtypeStruct((2,) + tall, BF16),
        ],
        in_specs=[smem, smem] + [anywhere] * 8 + [vmem] * 2,
        out_specs=[anywhere] * 4,
        scratch_shapes=[pltpu.VMEM(shape, kind) for shape, kind in buffers]
        + [
            pltpu.VMEM((3, SHARD, 192), F32), pltpu.VMEM((192, SHARD), F32), pltpu.VMEM((SHARD, WIDTH), F32),
            pltpu.VMEM((SHARD, WIDTH), F32), pltpu.VMEM((16, QUARTER), F32), pltpu.VMEM(vec_master.shape, F32),
        ]
        + [pltpu.SemaphoreType.DMA((14,))] + [pltpu.SemaphoreType.DMA((COPIES,))] * 2
        + [pltpu.VMEM(shape, BF16) for shape in INBOX.values()],
        compiler_params=pltpu.CompilerParams(
            collective_id=0, has_side_effects=True, vmem_limit_bytes=VMEM_BYTES
        ),
    )(time_steps, doc_lengths, tokens, cotangent, turned_qkv[0], proj_master, up_master,
      turned_down[0], ada_master, vec_master, freq, theta)
    states = [
        *turned_qkv, proj_master, proj_first, proj_second, up_master, up_first, up_second,
        *turned_down, ada_master, ada_first, ada_second, vec_master, vec_first, vec_second,
    ]

    def whole(a):
        return pl.BlockSpec(a.shape, lambda i: (0,) * a.ndim)

    strip = pl.BlockSpec((2, LEN_FAST // 2, WIDTH), lambda i: (0, i, 0))
    part_rows = SHARD // 2
    shared = {
        "qkv": pl.BlockSpec((3, part_rows, 192), lambda i: (0, i, 0)),
        "row": pl.BlockSpec((part_rows, WIDTH), lambda i: (i, 0)),
        "ada": pl.BlockSpec((16, 2 * QUARTER), lambda i: (0, i)),
    }
    state_specs = [
        spec
        for spec in (shared["qkv"], whole(proj_master), shared["row"], shared["row"], shared["ada"], whole(vec_master))
        for _ in range(3)
    ]
    new = pl.pallas_call(
        update_kernel,
        grid=(2,),
        out_shape=[jax.ShapeDtypeStruct((2,) + tall, BF16), jax.ShapeDtypeStruct((2,) + tall, F32)]
        + [jax.ShapeDtypeStruct(a.shape, F32) for a in states],
        in_specs=[pl.BlockSpec((3, part_rows, WIDTH), lambda i: (0, i, 0)), whole(stats), strip, strip]
        + state_specs,
        out_specs=[strip, strip] + state_specs,
        scratch_shapes=[pltpu.VMEM((SHARD, 192), F32), pltpu.VMEM((COND, 2 * QUARTER), F32)],
        compiler_params=pltpu.CompilerParams(vmem_limit_bytes=VMEM_BYTES),
    )(grads, stats, blocks, grad_tokens, *states)
    blocks, grad_tokens, *new = new
    new[0:3] = [jnp.transpose(a, (1, 0, 2)) for a in new[0:3]]
    new[9:12] = [a.T for a in new[9:12]]
    return (blocks, grad_tokens, *new)


def solution(mesh):
    placed = (
        P("dp", None, None),
        P("dp", None, None),
        P("dp", None),
        P("dp"),
        P("dp", None, "mp"),
        P("dp", None, "mp"),
        P("dp", None, "mp"),
        P("mp", "dp"),
        P("mp", "dp"),
        P("mp", "dp"),
        P("dp", "mp"),
        P("dp", "mp"),
        P("dp", "mp"),
        P("mp", "dp"),
        P("mp", "dp"),
        P("mp", "dp"),
        P("dp", None),
        P("dp", None),
        P("dp", None),
        P(),
        P(),
        P(),
    )
    fast = mesh.shape["dp"] == 8 and mesh.shape["mp"] == 4
    return jax.shard_map(
        fast_shards if fast else shards,
        mesh=mesh,
        in_specs=placed,
        out_specs=(
            P("dp", None, None),
            P("dp", None, None),
            P("dp", None, "mp"),
            P("dp", None, "mp"),
            P("dp", None, "mp"),
            P("mp", "dp"),
            P("mp", "dp"),
            P("mp", "dp"),
            P("dp", "mp"),
            P("dp", "mp"),
            P("dp", "mp"),
            P("mp", "dp"),
            P("mp", "dp"),
            P("mp", "dp"),
            P("dp", None),
            P("dp", None),
            P("dp", None),
            P(),
            P(),
            P(),
        ),
        check_vma=False,
    )
```
